32 devices in a mesh: level: 4 (over z), img: 8 (over y, x, core).
Axes of the slice: x: 2, y: 2, z: 4, core: 2. Of those that a mesh axis runs over, the one named last changes fastest.
Arguments:
- pyramid: bfloat16 [4, 16, 64, 16, 256], P('level', 'img'), may hold values from -6 to 6
- levels: int32 [16, 512, 1], P('img', 'level'), may hold values from 0 to 3; in each aligned block of 128 rows (0 to 127, 128 to 255, ..., all dimensions but the last counted through in order) at most 64 rows name the same one
- region_boxes: int32 [16, 512, 4], P('img', 'level'), may hold values from 0 to 63, as said below
- labels: int32 [16, 512], P('img', 'level'), may hold values from 0 to 80, as said below
- crowd_ignore: int32 [16, 512], P('img', 'level'), may hold values 0 or 1
- targets: float32 [16, 512, 4], P('img', 'level'), may hold values from -6 to 6
- hidden_weight: bfloat16 [12544, 1024], P(('level', 'img')), may hold values from -0.109375 to 0.109375
- hidden_bias: float32 [1024], replicated, may hold values from -3 to 3
- inner_weight: bfloat16 [1024, 1024], P(('level', 'img')), may hold values from -0.25 to 0.25
- inner_bias: float32 [1024], replicated, may hold values from -3 to 3
- class_weight: bfloat16 [1024, 81], P(('level', 'img')), may hold values from -0.75 to 0.75
- class_bias: float32 [81], replicated, may hold values from -3 to 3
- delta_weight: bfloat16 [1024, 320], P(('level', 'img')), may hold values from -0.375 to 0.375
- delta_bias: float32 [320], replicated, may hold values from -3 to 3
Outputs:
- logits: float32 [16, 512, 81], P('img', 'level')
- deltas: float32 [16, 512, 320], P('img', 'level')
- pyramid_grad: float32 [4, 16, 64, 16, 256], P('level', 'img')
- hidden_grad: float32 [12544, 1024], P(('level', 'img'))
- bias_hidden: float32 [1024], replicated
- inner_grad: float32 [1024, 1024], P(('level', 'img'))
- bias_inner: float32 [1024], replicated
- class_grad: float32 [1024, 81], P(('level', 'img'))
- bias_class: float32 [81], replicated
- delta_grad: float32 [1024, 320], P(('level', 'img'))
- bias_delta: float32 [320], replicated
The draws below stay inside these ranges and needn't reach their ends.
Inputs may be any that keep to these rules, and one draw needn't show every extreme that they name: `levels`: among the 128 regions of one image that one device holds, at most 64 lie on any one level, and some image and level reach 64. `region_boxes`: each row is x0, y0, x1, y1 with 0 <= x0 < x1 <= 15 and 0 <= y0 < y1 <= 63. `labels`: 80 marks background; smaller values are foreground classes.
All inputs are finite; a program needn't handle non-finite values. No bound on the sum of `crowd_ignore` on one device may be relied on, other than what follows from the above.
Results may differ from the reference program's by a relative error of at most 0.011.
Values may be sent and summed in bfloat16 or wider, within the bound.
No kernel may reach another device: no remote copies, remote signals or barrier semaphores. Data moves between devices by JAX's collectives and lax.ppermute only.
A program may use at most 256 MiB of HBM per device.

```python
import math
import jax
import jax.numpy as jnp
import numpy as np
from jax import lax

C = 256
POOL = 7
SAMPLES = 2
FEAT = 12544
HID = 1024
CLS = 81
BOX = 320
HF = 64
WF = 16
RPI = 512
RPD = 128
CAPI = 64
IMAGES = 16
N_LEVEL = 4


def draw_region_boxes(key, part):
    key = jax.random.fold_in(key, 11)
    subkeys = jax.random.split(key, 4)
    grid_shape = (IMAGES, RPI)
    left_edge = jax.random.randint(subkeys[0], grid_shape, 0, WF - 1)
    top_edge = jax.random.randint(subkeys[1], grid_shape, 0, HF - 1)
    right_edge = left_edge + 1 + jax.random.randint(subkeys[2], grid_shape, 0, WF - 1 - left_edge)
    bottom_edge = top_edge + 1 + jax.random.randint(subkeys[3], grid_shape, 0, HF - 1 - top_edge)
    return jnp.stack([left_edge, top_edge, right_edge, bottom_edge], axis=-1).astype(jnp.int32)


def draw_labels(key, part):
    key = jax.random.fold_in(key, 12)
    subkeys = jax.random.split(key, 2)
    grid_shape = (IMAGES, RPI)
    chosen = jax.random.randint(subkeys[0], grid_shape, 0, 4) == 0
    classes = jax.random.randint(subkeys[1], grid_shape, 0, CLS - 1)
    return jnp.where(chosen, classes, CLS - 1).astype(jnp.int32)


def plant(array, own_key, least, largest):
    longest = array.shape.index(max(array.shape))
    spots = []
    for shift in (0, 1):
        where = [jax.random.randint(jax.random.fold_in(own_key, axis), (), 0, length) for axis, length in enumerate(array.shape)]
        where[longest] = (where[longest] + shift) % array.shape[longest]
        spots.append(tuple(where))
    return array.at[spots[0]].set(least).at[spots[1]].set(largest)


def shard_levels(key, dims, cuts, low, top_value):
    gain = 1.0
    for axis_at, blocks in cuts:
        steps = jax.random.uniform(jax.random.fold_in(jax.random.fold_in(key, 6), axis_at), (blocks,), jnp.float32, low / len(cuts), top_value / len(cuts))
        gain = gain * jnp.repeat(jnp.exp(steps), dims[axis_at] // blocks).reshape((-1,) + (1,) * (len(dims) - 1 - axis_at))
    return gain


def assign_block(stream_key, own, number, rows, amount, top, bound, skew):
    sequence = jax.random.permutation(stream_key, amount)
    heavy_load, common = portions_of(amount, rows * top, bound, skew, True), portions_of(amount, rows * top, bound, skew, False)
    places = jnp.arange(amount)

    def named(lengths, turn):
        used = int((lengths > 0).sum())
        fixed = max(1, used // 4)
        passed = fixed + (places - fixed + turn * (used - fixed)) % max(1, amount - fixed)
        return jnp.zeros((amount,), jnp.int32).at[sequence[jnp.where(places < fixed, places, passed)]].set(jnp.asarray(lengths, jnp.int32))

    lengths = jnp.where(number % 4 == 0, named(heavy_load, number // 4), named(common, number - number // 4 - 1))
    mixed = jax.random.permutation(jax.random.fold_in(own, 3), amount)
    giver, receiver = mixed[0:amount // 2 * 2:2], mixed[1:amount // 2 * 2:2]
    margin = jnp.minimum(lengths[giver] - 1, bound - lengths[receiver]) // 2
    margin = jnp.where((giver == sequence[0]) | (receiver == sequence[0]) | (lengths[receiver] == 0), 0, jnp.maximum(margin, 0))
    passed = jax.random.randint(jax.random.fold_in(own, 4), (amount // 2,), 0, 1 << 20) % (margin + 1)
    lengths = lengths.at[giver].add(-passed).at[receiver].add(passed)
    items = jnp.searchsorted(jnp.cumsum(lengths), jnp.arange(rows * top), side="right").astype(jnp.int32)
    table = items.reshape(top, rows).T
    table = table[jax.random.permutation(jax.random.fold_in(own, 1), rows)]
    turn = jax.random.randint(jax.random.fold_in(own, 2), (rows, 1), 0, top)
    return jnp.take_along_axis(table, (jnp.arange(top)[None, :] + turn) % top, axis=1)


def portions_of(number_of, total, reach, skew, full):
    weights = [(1 << 20) // math.isqrt(rank ** skew) + 1 for rank in range(1, number_of + 1)]
    largest = reach if full else min(reach, max(-(-total // number_of), total * weights[0] // sum(weights)))
    least = 1 if total - largest >= number_of - 1 else 0
    given, spare = [largest] + [least] * (number_of - 1), total - largest - least * (number_of - 1)
    while spare > 0:
        free = [i for i in range(1, number_of) if given[i] < largest] or [i for i in range(1, number_of) if given[i] < reach]
        mass, budget = sum([weights[i] for i in free]), spare
        for i in free:
            more = min(reach - given[i], max(1, budget * weights[i] // mass), spare)
            given[i] = given[i] + more
            spare = spare - more
    return np.array(given)


def scatter_about(stream_key, shape, deviation, bound, cuts=(), held_as=jnp.bfloat16):
    level = shard_levels(stream_key, shape, cuts, -0.22, 0.18) if cuts else 1.0
    drawn = jax.random.normal(stream_key, shape, jnp.float32) * deviation * level
    return jnp.minimum(jnp.maximum(drawn, -bound), bound).astype(held_as)


def setup_inputs(seed: int = 0) -> dict:
    key_list = jax.random.split(jax.random.key(seed), 15)
    pyramid = scatter_about(key_list[0], (N_LEVEL, IMAGES, HF, WF, C), 1.0, 6.0, ((0, 4), (1, 8)))
    levels_keys = jax.random.split(jax.random.fold_in(key_list[1], 1), IMAGES * RPI // RPD)
    levels_turns = jax.random.permutation(jax.random.fold_in(key_list[1], 3), IMAGES * RPI // RPD)
    levels = jax.vmap(lambda own, number: assign_block(jax.random.fold_in(key_list[1], 2), own, number, RPD, N_LEVEL, 1, CAPI, 2))(levels_keys, levels_turns).reshape((IMAGES, RPI, 1))
    region_boxes = draw_region_boxes(jax.random.fold_in(key_list[14], 71), 0)
    labels = draw_labels(jax.random.fold_in(key_list[14], 71), 0)
    crowd_ignore = plant((jax.random.randint(key_list[4], (IMAGES, RPI), 0, 8) < 1).astype(jnp.int32), jax.random.fold_in(key_list[4], 1), 0, 1)
    targets = scatter_about(key_list[5], (IMAGES, RPI, 4), 1.0, 6.0, ((0, 8), (1, 4)), jnp.float32)
    hidden_weight = scatter_about(key_list[6], (FEAT, HID), (FEAT // 4) ** -0.5, 0.109375, ((0, 32),))
    hidden_bias = scatter_about(key_list[7], (HID,), 0.5, 3.0, (), jnp.float32)
    inner_weight = scatter_about(key_list[8], (HID, HID), (HID // 2) ** -0.5, 0.25, ((0, 32),))
    inner_bias = scatter_about(key_list[9], (HID,), 0.5, 3.0, (), jnp.float32)
    class_weight = scatter_about(key_list[10], (HID, CLS), (HID // 16) ** -0.5, 0.75, ((0, 32),))
    class_bias = scatter_about(key_list[11], (CLS,), 0.5, 3.0, (), jnp.float32)
    delta_weight = scatter_about(key_list[12], (HID, BOX), (HID // 4) ** -0.5, 0.375, ((0, 32),))
    delta_bias = scatter_about(key_list[13], (BOX,), 0.5, 3.0, (), jnp.float32)
    return {"pyramid": pyramid, "levels": levels, "region_boxes": region_boxes, "labels": labels, "crowd_ignore": crowd_ignore, "targets": targets, "hidden_weight": hidden_weight, "hidden_bias": hidden_bias, "inner_weight": inner_weight, "inner_bias": inner_bias, "class_weight": class_weight, "class_bias": class_bias, "delta_weight": delta_weight, "delta_bias": delta_bias}


@jax.custom_vjp
def low(v):
    return lax.optimization_barrier(v.astype(jnp.bfloat16)).astype(jnp.float32)

@jax.custom_vjp
def low_back(v):
    return v

def low_keep(v):
    return (low(v), None)

def low_pass(kept, grad):
    return (grad,)

def back_keep(v):
    return (v, None)

def back_low(kept, grad):
    return (low(grad),)
low.defvjp(low_keep, low_pass)
low_back.defvjp(back_keep, back_low)
highest = lax.Precision.HIGHEST

def sample_weights(low_edge, high_edge, extent):
    offsets = (jnp.arange(SAMPLES * POOL, dtype=jnp.float32) + 0.5) / (SAMPLES * POOL)
    box_spans = (high_edge - low_edge).astype(jnp.float32)
    points = low_edge.astype(jnp.float32)[:, None] + offsets[None, :] * box_spans[:, None]
    centres = jnp.arange(extent, dtype=jnp.float32)
    tent_values = jnp.maximum(1.0 - jnp.abs(points[:, :, None] - centres[None, None, :]), 0.0)
    tent_values = tent_values.reshape(points.shape[0], POOL, SAMPLES, extent)
    return lax.optimization_barrier(jnp.sum(tent_values, axis=2)) / SAMPLES

def image_loss(maps, level_rows, box_rows, label_rows, ignore_rows, target_rows, weights):
    hidden_weight, hidden_bias, inner_weight, inner_bias, class_weight, class_bias, delta_weight, delta_bias = weights
    weights_down = low(sample_weights(box_rows[:, 1], box_rows[:, 3], HF))
    weights_across = low(sample_weights(box_rows[:, 0], box_rows[:, 2], WF))
    crop = jnp.zeros((RPI, POOL, POOL, C), jnp.float32)
    for level_index in range(N_LEVEL):
        chosen_level = (level_rows == level_index).astype(jnp.float32)
        partial_sum = jnp.einsum('rpy,yxc->rpxc', weights_down * chosen_level[:, None, None], maps[level_index], precision=highest)
        crop = crop + jnp.einsum('rqx,rpxc->rpqc', weights_across, partial_sum, precision=highest)
    crop = low_back(low(crop.reshape(RPI, FEAT)))
    first_pre = low_back(jnp.dot(crop, hidden_weight, precision=highest) + hidden_bias)
    first_act = low(jax.nn.gelu(first_pre, approximate=False))
    second_pre = low_back(jnp.dot(first_act, inner_weight, precision=highest) + inner_bias)
    second_act = low(jax.nn.gelu(second_pre, approximate=False))
    logits = low_back(jnp.dot(second_act, class_weight, precision=highest) + class_bias)
    deltas = low_back(jnp.dot(second_act, delta_weight, precision=highest) + delta_bias)
    kept_rows = 1.0 - ignore_rows.astype(jnp.float32)
    class_hot = (label_rows[:, None] == jnp.arange(CLS, dtype=jnp.int32)[None, :]).astype(jnp.float32)
    row_max = lax.optimization_barrier(jnp.max(logits, axis=1, keepdims=True))
    log_total = row_max[:, 0] + jnp.log(lax.optimization_barrier(jnp.sum(jnp.exp(logits - row_max), axis=1)))
    cross_entropy = log_total - lax.optimization_barrier(jnp.sum(logits * class_hot, axis=1))
    foreground = kept_rows * (label_rows < CLS - 1).astype(jnp.float32)
    box_hot = (label_rows[:, None] == jnp.arange(BOX // 4, dtype=jnp.int32)[None, :]).astype(jnp.float32)
    chosen_box = lax.optimization_barrier(jnp.sum(deltas.reshape(RPI, BOX // 4, 4) * box_hot[:, :, None], axis=1))
    difference = chosen_box - target_rows
    huber_terms = jnp.where(jnp.abs(difference) < 1.0, 0.5 * difference * difference, jnp.abs(difference) - 0.5)
    loss_value = jnp.sum(kept_rows * cross_entropy + foreground * lax.optimization_barrier(jnp.sum(huber_terms, axis=1))) / RPI
    return (loss_value, (logits, deltas))

def reference(pyramid, levels, region_boxes, labels, crowd_ignore, targets, hidden_weight, hidden_bias, inner_weight, inner_bias, class_weight, class_bias, delta_weight, delta_bias):
    maps_all = jnp.transpose(pyramid.astype(jnp.float32), (1, 0, 2, 3, 4))
    weights = (hidden_weight.astype(jnp.float32), hidden_bias.astype(jnp.float32), inner_weight.astype(jnp.float32), inner_bias.astype(jnp.float32), class_weight.astype(jnp.float32), class_bias.astype(jnp.float32), delta_weight.astype(jnp.float32), delta_bias.astype(jnp.float32))

    def total(maps_all, weights):

        def per_image(pieces):
            return image_loss(pieces[0], pieces[1], pieces[2], pieces[3], pieces[4], pieces[5], weights)
        losses, outputs = lax.map(jax.checkpoint(per_image), (maps_all, levels[:, :, 0], region_boxes, labels, crowd_ignore, targets))
        return (jnp.sum(losses), outputs)
    loss_value, pullback, outputs = jax.vjp(total, maps_all, weights, has_aux=True)
    maps_grad, weight_grads = pullback(jnp.ones_like(loss_value))
    pyramid_grad = jnp.transpose(maps_grad, (1, 0, 2, 3, 4))
    return (outputs[0], outputs[1], pyramid_grad, weight_grads[0], weight_grads[1], weight_grads[2], weight_grads[3], weight_grads[4], weight_grads[5], weight_grads[6], weight_grads[7])
```

```python
import functools

import jax
import jax.numpy as jnp
import numpy as np
from jax import lax
from jax.experimental import pallas as pl
from jax.experimental.pallas import tpu as pltpu
from jax.sharding import PartitionSpec as P

POOL = 7
SAMPLES = 2
CLS = 81
BOX = 320
RPI = 512
BINS = POOL * POOL
LANES = 128
AXES = ("level", "img")
OFFSETS = (np.arange(SAMPLES * POOL, dtype=np.float32) + np.float32(0.5)) / np.float32(
    SAMPLES * POOL
)
SMALL_COST = pl.CostEstimate(flops=10**9, bytes_accessed=1, transcendentals=0)
LARGE_COST = pl.CostEstimate(flops=4 * 10**10, bytes_accessed=1, transcendentals=0)
f32 = jnp.float32
bf16 = jnp.bfloat16
ANY = pl.BlockSpec(memory_space=pl.ANY)
WHOLE = pl.BlockSpec(memory_space=pltpu.VMEM)
SCALAR = pl.BlockSpec(memory_space=pltpu.SMEM)
like = jax.ShapeDtypeStruct


def bin_weights(low, span, centres, at):
    first = jnp.maximum(1.0 - jnp.abs((low + OFFSETS[2 * at] * span) - centres), 0.0)
    second = jnp.maximum(1.0 - jnp.abs((low + OFFSETS[2 * at + 1] * span) - centres), 0.0)
    return ((first + second) * 0.5).astype(bf16)


def fill_weights(box_ref, down_ref, across_ref, height, width, level_count):
    x0, y0, x1, y1, level = [box_ref[k : k + 1, :] for k in range(5)]
    centres = lax.broadcasted_iota(jnp.int32, (width, LANES), 0).astype(f32)
    for q in range(POOL):
        across_ref[q] = bin_weights(x0, x1 - x0, centres, q).astype(f32)
    centres = lax.broadcasted_iota(jnp.int32, (height, LANES), 0).astype(f32)
    for p in range(POOL):
        weights = bin_weights(y0, y1 - y0, centres, p).astype(f32)
        for k in range(level_count):
            down_ref[k * height : (k + 1) * height, p * LANES : (p + 1) * LANES] = jnp.where(
                level == float(k), weights, 0.0
            ).astype(bf16)


def runs_of(order, length, part, group, room):
    place = {chunk: at // group * room + at % group * length for at, chunk in enumerate(order)}
    table = []
    for at in range(BINS):
        row, end, runs = at * part, (at + 1) * part, []
        while row < end:
            chunk = row // length
            stop = min(end, (chunk + 1) * length)
            runs.append((row - at * part, place[chunk] + row - chunk * length, stop - row))
            row = stop
        table.append(runs)
    return table


def gaps_of(table, features):
    held = sorted((kept, kept + count) for runs in table for row, kept, count in runs)
    gaps, last = [], 0
    for first, end in held + [(features, features)]:
        if first > last:
            gaps.append((last, first))
        last = end
    return gaps


def fetch_pieces(seat_ref, piece_refs, kept_ref, sems):
    rows = piece_refs[0].shape[0]
    return [
        pltpu.make_async_copy(
            ref, kept_ref.at[pl.ds(pl.multiple_of((seat_ref[0] ^ k) * rows, 16), rows)], sems.at[k]
        )
        for k, ref in enumerate(piece_refs)
    ]


def crop_kernel(table, sizes, number, at_ref, seat_ref, box_ref, maps_ref, *refs):
    piece_refs, refs = refs[:number], refs[number:]
    if number:
        crop_ref, out_ref, down_ref, across_ref, sums_ref, rows_ref, turned_ref, kept_ref, sems = refs[-9:]
        copies = fetch_pieces(seat_ref, piece_refs, kept_ref, sems)

        @pl.when(pl.program_id(0) == 0)
        def start():
            for copy in copies:
                copy.start()
    else:
        crop_ref, out_ref, down_ref, across_ref, sums_ref, rows_ref = refs[-6:]
    height, width, part, level_count = sizes
    for first, end in gaps_of(table, rows_ref.shape[0]):
        rows_ref[first:end, :] = jnp.zeros((end - first, LANES), f32)
    fill_weights(box_ref, down_ref, across_ref, height, width, level_count)
    sums_ref[...] = jnp.dot(maps_ref[...], down_ref[...], preferred_element_type=f32)
    for p in range(POOL):
        lanes = slice(p * LANES, (p + 1) * LANES)
        for start in range(0, POOL, 2):
            bins = range(start, min(POOL, start + 2))
            totals = [None for q in bins]
            for x in range(width):
                piece = sums_ref[x * part : (x + 1) * part, lanes]
                for at, q in enumerate(bins):
                    term = across_ref[q, x : x + 1, :] * piece
                    totals[at] = term if x == 0 else totals[at] + term
            for at, q in enumerate(bins):
                for row, kept, count in table[p * POOL + q]:
                    rows_ref[kept : kept + count, :] = totals[at][row : row + count]
    crop = rows_ref[...].astype(bf16)
    crop_ref[...] = crop
    if not number:
        out_ref[...] = crop.T
        return
    turned_ref[pl.ds(pl.multiple_of(pl.program_id(0) * LANES, LANES), LANES), :] = crop.T

    @pl.when(pl.program_id(0) == pl.num_programs(0) - 1)
    def multiply():
        for copy in copies:
            copy.wait()
        out_ref[...] = jnp.dot(
            turned_ref[...], kept_ref[...], preferred_element_type=f32
        ).astype(out_ref.dtype)


def spread_kernel(table, sizes, number, seat_ref, box_ref, grad_ref, held_ref, *refs):
    piece_refs = refs[:number]
    total_ref, down_ref, across_ref, sums_ref, rows_ref, crop_ref, kept_ref, sems = refs[-8:]
    height, width, part, level_count = sizes
    images = box_ref.shape[0]
    copies = fetch_pieces(seat_ref, piece_refs, kept_ref, sems)
    for copy in copies:
        copy.start()
    for n in range(images):
        fill_weights(
            box_ref.at[n], down_ref.at[n], across_ref.at[n], height, width, level_count
        )
    for copy in copies:
        copy.wait()
    crop_ref[...] = lax.dot_general(
        kept_ref[...], grad_ref[...], (((1,), (1,)), ((), ())), preferred_element_type=f32
    ).astype(bf16)
    for n in range(images):
        rows_ref[...] = crop_ref[:, n * LANES : (n + 1) * LANES].astype(f32)
        for p in range(POOL):
            lanes = slice(p * LANES, (p + 1) * LANES)
            pieces = []
            for q in range(POOL):
                runs = [rows_ref[kept : kept + count, :] for row, kept, count in table[p * POOL + q]]
                pieces.append(runs[0] if len(runs) == 1 else jnp.concatenate(runs, axis=0))
            for x in range(width):
                total = across_ref[n, 0, x : x + 1, :] * pieces[0]
                for q in range(1, POOL):
                    total = total + across_ref[n, q, x : x + 1, :] * pieces[q]
                sums_ref[x * part : (x + 1) * part, lanes] = total.astype(bf16)
        total_ref[n] = held_ref[n] + lax.dot_general(
            sums_ref[...], down_ref[n], (((1,), (1,)), ((), ())), preferred_element_type=f32
        )


def crop_block(table, sizes, features, boxes, maps, at, count, held, seat, weight=(), out_type=bf16, earlier=()):
    height, width, part, level_count = sizes
    images = boxes.shape[0]
    number = len(weight)
    operands = [boxes, maps, *weight] + ([] if held is None else [held])
    place = len(operands) + 1
    operands += earlier
    rows = images * LANES
    if number:
        units = weight[0].shape[1]
        out_spec = pl.BlockSpec((rows, units), lambda n, *at: (0, 0))
        out_shape = like((rows, units), out_type)
        more = [
            pltpu.VMEM((rows, features), bf16),
            pltpu.VMEM((features, units), bf16),
            pltpu.SemaphoreType.DMA((number,)),
        ]
    else:
        out_spec = pl.BlockSpec((LANES, features), lambda n, *at: (n, 0))
        out_shape = like((rows, features), bf16)
        more = []
    return pl.pallas_call(
        functools.partial(crop_kernel, table, sizes, number),
        grid_spec=pltpu.PrefetchScalarGridSpec(
            num_scalar_prefetch=2,
            grid=(images,),
            in_specs=[
                pl.BlockSpec((None, 8, LANES), lambda n, *at: (n, 0, 0)),
                pl.BlockSpec((None, width * part, level_count * height), lambda n, *at: (n, 0, 0)),
            ]
            + [ANY for one in operands[2:]],
            out_specs=[
                pl.BlockSpec((features, LANES), lambda n, at, seat: (0, at[0] * images + n)),
                out_spec,
            ],
            scratch_shapes=[
                pltpu.VMEM((level_count * height, POOL * LANES), bf16),
                pltpu.VMEM((POOL, width, LANES), f32),
                pltpu.VMEM((width * part, POOL * LANES), f32),
                pltpu.VMEM((features, LANES), f32),
            ]
            + more,
        ),
        out_shape=[like((features, count * images * LANES), bf16), out_shape],
        input_output_aliases={} if held is None else {place: 0},
        compiler_params=pltpu.CompilerParams(vmem_limit_bytes=48 * 2**20),
        cost_estimate=LARGE_COST,
        name="crop_block",
    )(jnp.full((1,), at, jnp.int32), seat, *operands)


def multiply_kernel(number, seat_ref, rows_ref, *refs):
    out_ref, kept_ref, sems = refs[-3:]
    copies = fetch_pieces(seat_ref, refs[:number], kept_ref, sems)
    for copy in copies:
        copy.start()
    for copy in copies:
        copy.wait()
    out_ref[...] = jnp.dot(rows_ref[...], kept_ref[...], preferred_element_type=f32).astype(
        out_ref.dtype
    )


def multiply_block(rows, seat, weight):
    units = weight[0].shape[1]
    return pl.pallas_call(
        functools.partial(multiply_kernel, len(weight)),
        in_specs=[SCALAR, WHOLE] + [ANY for one in weight],
        out_specs=WHOLE,
        out_shape=like((rows.shape[0], units), bf16),
        scratch_shapes=[
            pltpu.VMEM((rows.shape[1], units), bf16),
            pltpu.SemaphoreType.DMA((len(weight),)),
        ],
        compiler_params=pltpu.CompilerParams(vmem_limit_bytes=48 * 2**20),
        cost_estimate=LARGE_COST,
        name="multiply_block",
    )(seat, rows, *weight)


def spread_block(table, sizes, features, boxes, grads, seat, weight, held, earlier=()):
    height, width, part, level_count = sizes
    images = boxes.shape[0]
    units = grads.shape[1]
    return pl.pallas_call(
        functools.partial(spread_kernel, table, sizes, len(weight)),
        in_specs=[SCALAR, WHOLE, WHOLE, WHOLE] + [ANY for one in (*weight, *earlier)],
        out_specs=WHOLE,
        out_shape=like((images, width * part, level_count * height), f32),
        scratch_shapes=[
            pltpu.VMEM((images, level_count * height, POOL * LANES), bf16),
            pltpu.VMEM((images, POOL, width, LANES), f32),
            pltpu.VMEM((width * part, POOL * LANES), bf16),
            pltpu.VMEM((features, LANES), f32),
            pltpu.VMEM((features, images * LANES), bf16),
            pltpu.VMEM((features, units), bf16),
            pltpu.SemaphoreType.DMA((len(weight),)),
        ],
        compiler_params=pltpu.CompilerParams(vmem_limit_bytes=48 * 2**20),
        cost_estimate=LARGE_COST,
        name="spread_block",
    )(seat, boxes, grads, held, *weight, *earlier)


def call(kernel, outs, scalars, arrays, earlier=(), alias=None, name=None):
    arrays = list(arrays)

    def body(*refs):
        at, end = len(scalars), len(scalars) + len(arrays)
        kernel(refs[:at], refs[at:end], refs[end + len(earlier) :])

    result = pl.pallas_call(
        body,
        in_specs=[SCALAR for one in scalars] + [WHOLE for one in arrays] + [ANY for one in earlier],
        out_specs=[WHOLE for one in outs],
        out_shape=outs,
        compiler_params=pltpu.CompilerParams(vmem_limit_bytes=48 * 2**20),
        cost_estimate=SMALL_COST,
        name=name,
    )(*[jnp.full((1,), one, jnp.int32) for one in scalars], *arrays, *earlier)
    return result


def tie_kernel(*refs):
    pass


def tie(array, *earlier):
    return pl.pallas_call(
        tie_kernel,
        in_specs=[ANY for one in (array, *earlier)],
        out_specs=ANY,
        out_shape=like(array.shape, array.dtype),
        input_output_aliases={0: 0},
        cost_estimate=SMALL_COST,
        name="tie",
    )(array, *earlier)


def order_kernel(scalars, arrays, outs):
    for k, ref in enumerate(arrays):
        outs[0][scalars[0][0] ^ k] = ref[...]


def in_order(at, arrays, earlier):
    shape = (len(arrays),) + arrays[0].shape
    return call(order_kernel, [like(shape, arrays[0].dtype)], [at], arrays, earlier, name="in_order")[0]


def full_small_kernel(rows, scalars, arrays, outs):
    units = outs[0].shape[1]
    for k, ref in enumerate(arrays):
        core = scalars[0][0] ^ k
        for y in range(2):
            for x in range(2):
                for level in range(ref.shape[2]):
                    at = pl.multiple_of((((level * 2 + y) * 2 + x) * 2 + core) * rows, rows)
                    outs[0][pl.ds(at, rows), :] = ref[y, x, level, :rows, :]
                    for part in range(2):
                        outs[1][pl.ds(at + part * (rows // 2), rows // 2), :] = ref[
                            y, x, level, rows:, part * (units // 2) : (part + 1) * (units // 2)
                        ]


def split_rows(core, array, rows, sent, kept):
    for at in range(kept.shape[0] // rows):
        mine = pl.multiple_of((2 * at + core) * rows, rows)
        other = pl.multiple_of((2 * at + 1 - core) * rows, rows)
        kept[at * rows : (at + 1) * rows, :] = array[pl.ds(mine, rows), :].astype(bf16)
        sent[at * rows : (at + 1) * rows, :] = array[pl.ds(other, rows), :].astype(bf16)


def small_product_kernel(rows, core_ref, first_ref, second_grad_ref, second_ref, slopes_ref, sent_ref, kept_ref, total_ref):
    turned = (((0,), (0,)), ((), ()))
    units = first_ref.shape[1]
    total_ref[:, :units] = lax.dot_general(
        first_ref[...], second_grad_ref[...], turned, preferred_element_type=f32
    )
    total_ref[:, units:] = lax.dot_general(
        second_ref[...], slopes_ref[...], turned, preferred_element_type=f32
    )
    split_rows(core_ref[0], total_ref, rows, sent_ref, kept_ref)


def small_product(core, rows, first_act, second_grad, second_act, slopes):
    units = first_act.shape[1]
    wide = units + slopes.shape[1]
    half = like((units // 2, wide), bf16)
    return pl.pallas_call(
        functools.partial(small_product_kernel, rows),
        in_specs=[SCALAR] + [WHOLE] * 4,
        out_specs=[WHOLE] * 2,
        out_shape=[half, half],
        scratch_shapes=[pltpu.VMEM((units, wide), f32)],
        compiler_params=pltpu.CompilerParams(vmem_limit_bytes=48 * 2**20),
        cost_estimate=SMALL_COST,
        name="small_product",
    )(jnp.full((1,), core, jnp.int32), first_act, second_grad, second_act, slopes)


def fold_kernel(rows, bit_ref, kept_ref, come_ref, *refs):
    sent_out, kept_out, total_ref = refs[-3:]
    total_ref[...] = kept_ref[...].astype(f32) + come_ref[...].astype(f32)
    split_rows(bit_ref[0], total_ref, rows, sent_out, kept_out)


def fold_rows(bit, rows, kept, come, earlier):
    half = like((kept.shape[0] // 2, kept.shape[1]), bf16)
    return pl.pallas_call(
        functools.partial(fold_kernel, rows),
        in_specs=[SCALAR, WHOLE, WHOLE] + [ANY for one in earlier],
        out_specs=[WHOLE] * 2,
        out_shape=[half, half],
        scratch_shapes=[pltpu.VMEM(kept.shape, f32)],
        compiler_params=pltpu.CompilerParams(vmem_limit_bytes=48 * 2**20),
        cost_estimate=SMALL_COST,
        name="fold_rows",
    )(jnp.full((1,), bit, jnp.int32), kept, come, *earlier)


def last_fold_kernel(rows, scalars, arrays, outs):
    units = outs[0].shape[1]
    for way, out in enumerate(outs):
        at = pl.multiple_of((scalars[0][0] ^ way) * rows, rows)
        total = sum(ref[pl.ds(at, rows), :].astype(f32) for ref in arrays).astype(bf16)
        out[:rows, :] = total[:, :units]
        for part in range(2):
            out[rows:, part * (units // 2) : (part + 1) * (units // 2)] = total[
                part * (rows // 2) : (part + 1) * (rows // 2), units:
            ]


def small_sum_kernel(scalars, arrays, outs):
    total = sum(ref[...].astype(f32) for ref in arrays)
    rows, units = outs[0].shape
    outs[0][...] = total[:rows]
    for part in range(2):
        at = slice(part * (rows // 2), (part + 1) * (rows // 2))
        beside = total[rows:, part * (units // 2) : (part + 1) * (units // 2)]
        outs[1][at, :] = beside[:, :CLS]
        outs[2][at, :] = beside[:, LANES : LANES + BOX]


def gelu_and_slope(values):
    normal = 0.5 * (1.0 + lax.erf(values * np.float32(np.sqrt(0.5))))
    density = jnp.exp(-0.5 * values * values) * np.float32(1.0 / np.sqrt(2.0 * np.pi))
    return values * normal, normal + values * density


def head_kernel(
    own_ref, one_ref, two_ref, three_ref, rows_ref, hidden_bias_ref, inner_ref, inner_bias_ref, heads_ref, heads_bias_ref,
    logits_ref, deltas_ref, first_act_ref, second_act_ref, slopes_ref, second_grad_ref, first_grad_ref, again_ref, bias_ref, first_slope_ref, second_slope_ref,
):
    first_pre = own_ref[...] + hidden_bias_ref[...]
    for come_ref in (one_ref, two_ref, three_ref):
        first_pre = first_pre + come_ref[...].astype(f32)
    act, slope = gelu_and_slope(first_pre)
    first_slope_ref[...] = slope
    act = act.astype(bf16)
    first_act_ref[...] = act
    second_pre = jnp.dot(act, inner_ref[...], preferred_element_type=f32) + inner_bias_ref[...]
    act, slope = gelu_and_slope(second_pre)
    second_slope_ref[...] = slope
    act = act.astype(bf16)
    second_act_ref[...] = act
    heads = jnp.dot(act, heads_ref[...], preferred_element_type=f32) + heads_bias_ref[...]
    logits, deltas = heads[:, :LANES], heads[:, LANES:]
    logits_ref[...] = logits[:, :CLS]
    deltas_ref[...] = deltas[:, :BOX]
    label = rows_ref[:, 0:1]
    kept = 1.0 - rows_ref[:, 1:2]
    column = lax.broadcasted_iota(jnp.int32, logits.shape, 1)
    valid = column < CLS
    row_max = jnp.max(jnp.where(valid, logits, -jnp.inf), axis=1, keepdims=True)
    exponent = jnp.where(valid, jnp.exp(jnp.where(valid, logits - row_max, 0.0)), 0.0)
    softmax_rows = exponent / jnp.sum(exponent, axis=1, keepdims=True)
    hot = (column.astype(f32) == label).astype(f32)
    logit_slope = (softmax_rows - hot) * (kept * np.float32(1.0 / RPI))
    column = lax.broadcasted_iota(jnp.int32, deltas.shape, 1)
    target = rows_ref[:, 2:3]
    for j in range(1, 4):
        target = jnp.where((column & 3) == j, rows_ref[:, 2 + j : 3 + j], target)
    foreground = jnp.where(label < CLS - 1, kept, 0.0)
    hot = ((column >> 2).astype(f32) == label) & (column < BOX)
    delta_slope = jnp.where(
        hot,
        jnp.clip(deltas - target, -1.0, 1.0) * (foreground * np.float32(1.0 / RPI)),
        0.0,
    )
    slopes = jnp.concatenate([logit_slope, delta_slope], axis=1).astype(bf16)
    slopes_ref[...] = slopes
    turned = (((1,), (1,)), ((), ()))
    act_grad = lax.dot_general(slopes, heads_ref[...], turned, preferred_element_type=f32)
    second_grad = (act_grad * second_slope_ref[...]).astype(bf16)
    second_grad_ref[...] = second_grad
    act_grad = lax.dot_general(second_grad, inner_ref[...], turned, preferred_element_type=f32)
    first_grad = (act_grad * first_slope_ref[...]).astype(bf16)
    first_grad_ref[...] = first_grad
    again_ref[...] = first_grad
    units = first_grad.shape[1]
    bias_ref[...] = jnp.zeros_like(bias_ref)
    bias_ref[0:1, :] = jnp.sum(first_grad.astype(f32), axis=0, keepdims=True)
    bias_ref[1:2, :] = jnp.sum(second_grad.astype(f32), axis=0, keepdims=True)
    bias_ref[2:3, : slopes.shape[1]] = jnp.sum(slopes.astype(f32), axis=0, keepdims=True)


def head_block(own, come, rows, hidden_bias, inner, inner_bias, heads, heads_bias):
    count, units = own.shape
    wide = heads.shape[1]
    return pl.pallas_call(
        head_kernel,
        in_specs=[pl.BlockSpec(memory_space=pltpu.VMEM)] * 10,
        out_specs=[pl.BlockSpec(memory_space=pltpu.VMEM)] * 9,
        out_shape=[
            like((count, CLS), f32),
            like((count, BOX), f32),
            like((count, units), bf16),
            like((count, units), bf16),
            like((count, wide), bf16),
            like((count, units), bf16),
            like((count, units), bf16),
            like((count, units), bf16),
            like((8, units), f32),
        ],
        scratch_shapes=[pltpu.VMEM((count, units), f32)] * 2,
        compiler_params=pltpu.CompilerParams(vmem_limit_bytes=48 * 2**20),
        cost_estimate=LARGE_COST,
        name="head_block",
    )(own, *come, rows, hidden_bias, inner, inner_bias, heads, heads_bias)


def arrange_kernel(sizes, came_ref, maps_ref):
    height, width, part, level_count = sizes
    for x in range(width):
        for k in range(level_count):
            maps_ref[x * part : (x + 1) * part, k * height : (k + 1) * height] = came_ref[
                k, :, x * height : (x + 1) * height
            ]


def arrange(sizes, came):
    height, width, part, level_count = sizes
    images = came.shape[1]
    return pl.pallas_call(
        functools.partial(arrange_kernel, sizes),
        grid=(images,),
        in_specs=[
            pl.BlockSpec((level_count, None, part, width * height), lambda n: (0, n, 0, 0))
        ],
        out_specs=pl.BlockSpec((None, width * part, level_count * height), lambda n: (n, 0, 0)),
        out_shape=jax.ShapeDtypeStruct((images, width * part, level_count * height), bf16),
        name="arrange",
    )(came)


def return_kernel(sizes, total_ref, sent_ref):
    height, width, part, level_count = sizes
    for x in range(width):
        for k in range(level_count):
            sent_ref[k, :, x * height : (x + 1) * height] = total_ref[
                x * part : (x + 1) * part, k * height : (k + 1) * height
            ].astype(bf16)


def arrange_back(sizes, total):
    height, width, part, level_count = sizes
    images = total.shape[0]
    return pl.pallas_call(
        functools.partial(return_kernel, sizes),
        grid=(images,),
        in_specs=[pl.BlockSpec((None, width * part, level_count * height), lambda n: (n, 0, 0))],
        out_specs=pl.BlockSpec((level_count, None, part, width * height), lambda n: (0, n, 0, 0)),
        out_shape=jax.ShapeDtypeStruct((level_count, images, part, width * height), bf16),
        name="arrange_back",
    )(total)


def picking(rows, columns, pairs):
    matrix = np.zeros((rows, columns), np.float32)
    for a, b in pairs:
        matrix[a, b] = 1.0
    return jnp.asarray(matrix, bf16)


def reorder(matrix, array, out_type=bf16):
    return jnp.dot(matrix, array, preferred_element_type=f32).astype(out_type)


def swap(array, axis, bit):
    size = lax.axis_size(axis)
    return lax.ppermute(array, axis, [(at, at ^ bit) for at in range(size)])


def exchange(array, axis):
    return lax.all_to_all(array, axis, split_axis=0, concat_axis=0, tiled=True)


def gather_pieces(piece):
    near = [piece] + [swap(piece, "img", bit) for bit in (2, 4, 6)]
    pieces = []
    for one in near:
        pieces += [one, swap(one, "img", 1)]
    return pieces


def product_kernel(number, with_sum, at_ref, grad_ref, *refs):
    crop_refs, refs = refs[:number], refs[number:]
    outs = refs[-number:] if with_sum else [refs[-1].at[n] for n in range(number)]
    for n in range(number):
        total = jnp.dot(crop_refs[n][...], grad_ref[...], preferred_element_type=f32)
        if with_sum:
            total = total + refs[0][n].astype(f32)
        outs[n][...] = total.astype(bf16)


def piece_product(crops, grads, pieces, come, earlier):
    features, count = crops.shape
    units = grads.shape[1]
    rows = features // 8
    number = pieces.shape[0]
    with_sum = come is not None
    crops = crops.reshape(8, rows, count)
    single = pl.BlockSpec((rows, units), lambda n, at: (0, 0))
    stacked = pl.BlockSpec((number, rows, units), lambda n, at: (0, 0, 0))
    return pl.pallas_call(
        functools.partial(product_kernel, number, with_sum),
        grid_spec=pltpu.PrefetchScalarGridSpec(
            num_scalar_prefetch=1,
            grid=(1,),
            in_specs=[pl.BlockSpec((count, units), lambda n, at: (0, 0))]
            + [
                pl.BlockSpec((None, rows, count), lambda n, at, k=k: (at[k], 0, 0))
                for k in range(number)
            ]
            + ([stacked] if with_sum else [])
            + [ANY for one in earlier],
            out_specs=[single] * number if with_sum else stacked,
        ),
        out_shape=[like((rows, units), bf16)] * number
        if with_sum
        else like((number, rows, units), bf16),
        compiler_params=pltpu.CompilerParams(vmem_limit_bytes=48 * 2**20),
        cost_estimate=LARGE_COST,
        name="piece_product",
    )(pieces, grads, *[crops] * number, *([come] if with_sum else []), *earlier)


def scatter_product(crops, grads, place, earlier):
    pairs = ((6, 2), (4, 0))
    others = []
    for bits in pairs:
        pieces = jnp.stack([place ^ bit ^ 1 for bit in bits])
        products = piece_product(crops, grads, pieces, None, earlier)
        earlier = [products]
        others.append(swap(products, "img", 1))
    parts = []
    for bits, other in zip(pairs, others):
        pieces = jnp.stack([place ^ bit for bit in bits])
        sums = piece_product(crops, grads, pieces, other, earlier)
        earlier = sums
        parts += [swap(one, "img", bit) if bit else one for one, bit in zip(sums, bits)]
    return parts, earlier


def butterfly(array):
    for axis in ("img", "level"):
        bit = 1
        while bit < lax.axis_size(axis):
            array = array + swap(array, axis, bit)
            bit *= 2
    return array


def contract_rows(left_side, right_side):
    return lax.dot_general(
        left_side, right_side, (((0,), (0,)), ((), ())), preferred_element_type=f32
    )


def contract_cols(left_side, right_side):
    return lax.dot_general(
        left_side, right_side, (((1,), (1,)), ((), ())), preferred_element_type=f32
    )


def pack_rows(array):
    rows, units = array.shape[-2], array.shape[-1] // 3 * 2
    beside = array[..., units:]
    below = jnp.concatenate([beside[..., : rows // 2, :], beside[..., rows // 2 :, :]], axis=-1)
    return jnp.concatenate([array[..., :units], below], axis=-2)


def per_device(
    pyramid,
    levels,
    region_boxes,
    labels,
    crowd_ignore,
    targets,
    hidden_weight,
    hidden_bias,
    inner_weight,
    inner_bias,
    class_weight,
    class_bias,
    delta_weight,
    delta_bias,
):
    size = lax.axis_size("level")
    planes = lax.axis_size("img")
    z = lax.axis_index("level")
    place = lax.axis_index("img")
    core, x, y = place % 2, place // 2 % 2, place // 4
    images, height, width, channels = pyramid.shape[1:]
    regions = levels.shape[1]
    part = channels // size
    sizes = (height, width, part, size)
    rows, units = hidden_weight.shape
    block_rows = images * regions
    direct = planes == 8 and rows % size == 0

    packed = jnp.concatenate(
        [
            jnp.transpose(region_boxes, (0, 2, 1)),
            jnp.transpose(levels, (0, 2, 1)),
            jnp.zeros((images, 3, regions), jnp.int32),
        ],
        axis=1,
    )
    class_room, delta_room = LANES, units // 2 - LANES
    small = jnp.concatenate(
        [
            inner_weight,
            jnp.pad(class_weight, ((0, 0), (0, class_room - CLS))),
            jnp.pad(delta_weight, ((0, 0), (0, delta_room - BOX))),
        ],
        axis=1,
    )
    heads_bias = jnp.concatenate(
        [
            jnp.pad(class_bias, (0, class_room - CLS)),
            jnp.pad(delta_bias, (0, delta_room - BOX)),
        ]
    )[None]

    if direct:
        length = rows // size
        pad = -(-(length + images) // 8) * 8
        small_rows = small.shape[0] // 2 * 3
        span = pad
        extra = jnp.concatenate(
            [packed.astype(bf16).reshape(images, units), jnp.zeros((16 - images, units), bf16)]
        )
        to_span = picking(
            size * span,
            rows,
            [(k * span + j, j * size + k) for k in range(size) for j in range(length)],
        )
        extra_span = picking(
            size * span,
            16,
            [(k * span + length + n, n) for k in range(size) for n in range(images)],
        )
        room = -(-rows // 16) * 16
        features = planes * room
        from_span = picking(
            room,
            size * span,
            [(k * length + j, k * span + j) for k in range(size) for j in range(length)],
        )
        sent = (
            jnp.dot(to_span, hidden_weight, preferred_element_type=f32)
            + jnp.dot(extra_span, extra, preferred_element_type=f32)
        ).astype(bf16)
        came = exchange(sent.reshape(size, span, units), "level")
        boxes = came[:, length : length + images].reshape(size, images, 8, regions).astype(f32)
        piece = reorder(from_span, came.reshape(size * span, units))
        weight = gather_pieces(piece)
        seat = jnp.full((1,), place, jnp.int32)
        order = [k * planes + at for at in range(planes) for k in range(size)]
        table = runs_of(order, length, part, size, room)
    else:
        boxes = exchange(jnp.broadcast_to(packed[None], (size,) + packed.shape), "level").astype(f32)
        features = BINS * part
        whole = lax.all_gather(hidden_weight, AXES, axis=0, tiled=True)
        weight = [lax.dynamic_index_in_dim(whole.reshape(features, size, units), z, 1, False)]
        seat = jnp.zeros((1,), jnp.int32)
        table = runs_of([0], features, part, 1, features)

    spots = height * width
    by_class = picking(
        channels, channels, [(c % size * part + c // size, c) for c in range(channels)]
    )
    across_first = picking(
        spots, spots, [(y * width + x, x * height + y) for y in range(height) for x in range(width)]
    )
    maps = []
    for n in range(images):
        flat = pyramid[0, n].reshape(spots, channels)
        flat = contract_cols(by_class, flat).astype(bf16)
        maps.append(reorder(flat, across_first).reshape(size, part, spots))
    maps = jnp.stack(maps, axis=1)
    if direct:
        maps = tie(maps, piece)
    maps_came = exchange(maps, "level")
    maps = arrange(sizes, maps_came)

    ways = (2, 3, 1, 0)
    crops, owns, came_sums = None, [], []
    for turn, way in enumerate(ways):
        at = lax.dynamic_index_in_dim(boxes, z ^ way, 0, False)
        if turn == 0:
            crops, crop = crop_block(
                table, sizes, features, at, maps, turn, size, crops, seat
            )
            owns.append(multiply_block(crop, seat, weight))
        else:
            crops, own = crop_block(
                table,
                sizes,
                features,
                at,
                maps,
                turn,
                size,
                crops,
                seat,
                weight,
                bf16 if way else f32,
                owns[-1:],
            )
            owns.append(own)
        if way:
            came_sums.append(swap(owns[-1], "level", way))

    if direct:
        smalls = tie(pack_rows(small), maps_came)
        smalls = [smalls] + [swap(smalls, "level", way) for way in (1, 2, 3)]
        smalls = in_order(z, smalls, owns[:1])
        smalls = in_order(x, [smalls, swap(smalls, "img", 2)], owns[1:2])
        smalls = in_order(y, [smalls, swap(smalls, "img", 4)], owns[2:3])
        full_inner, full_heads = call(
            functools.partial(full_small_kernel, small.shape[0]),
            [like((units, units), bf16), like((units, units // 2), bf16)],
            [core],
            [smalls, swap(smalls, "img", 1)],
            name="full_small",
        )
    else:
        smalls = lax.all_gather(small, AXES, axis=0, tiled=True)
        full_inner, full_heads = smalls[:, :units], smalls[:, units:]

    row_facts = jnp.concatenate(
        [
            labels.reshape(-1, 1).astype(f32),
            crowd_ignore.reshape(-1, 1).astype(f32),
            targets.reshape(-1, 4),
            jnp.zeros((block_rows, 2), f32),
        ],
        axis=1,
    )
    logits, deltas, first_act, second_act, slopes, second_grad, first_grad, first_again, bias_sums = head_block(
        owns[-1],
        came_sums,
        row_facts,
        hidden_bias[None],
        full_inner,
        inner_bias[None],
        full_heads,
        heads_bias,
    )

    near = swap(first_grad, "level", 1)
    far = swap(first_grad, "level", 2)
    farthest = swap(tie(first_again, far), "level", 3)
    grad_of = {0: first_grad, 1: near, 2: far, 3: farthest}
    whole_grads = jnp.concatenate([grad_of[way] for way in ways])

    def take_up(way, held, earlier=()):
        at = lax.dynamic_index_in_dim(boxes, z ^ way, 0, False)
        return spread_block(table, sizes, features, at, grad_of[way], seat, weight, held, earlier)

    held = jnp.zeros((images, width * part, size * height), f32)
    if direct:
        count = small.shape[0]
        sent, kept = small_product(core, count, first_act, second_grad, second_act, slopes)
        held = take_up(0, held, [kept])
        sent, kept = fold_rows(x, count, kept, swap(sent, "img", 1), [held])
        held = take_up(1, held, [kept])
        sent, kept = fold_rows(y, count, kept, swap(sent, "img", 2), [held])
        held = take_up(2, held, [kept])
        smalls = call(
            functools.partial(last_fold_kernel, count),
            [like((small_rows, units), bf16)] * size,
            [z],
            [kept, swap(sent, "img", 4)],
            [held],
            name="last_fold",
        )
        parts, earlier = scatter_product(crops, whole_grads, place, smalls[:1])
        held = take_up(3, held, earlier)
    else:
        for way in range(size):
            held = take_up(way, held)
        small_sum = jnp.concatenate(
            [contract_rows(first_act, second_grad), contract_rows(second_act, slopes)], axis=1
        )
        small_sum = lax.psum_scatter(small_sum, AXES, scatter_dimension=0, tiled=True)
        product = jnp.dot(crops, whole_grads, preferred_element_type=f32)
        own = (jnp.arange(size, dtype=jnp.int32) == z)[None, :, None]
        hidden_sum = lax.psum_scatter(
            jnp.where(own, product[:, None, :], 0.0).reshape(features * size, units),
            AXES,
            scatter_dimension=0,
            tiled=True,
        )

    back = arrange_back(sizes, held)
    if direct:
        smalls = [smalls[0]] + [swap(smalls[way], "level", way) for way in (1, 2, 3)]
        inner_sum, class_sum, delta_sum = call(
            small_sum_kernel,
            [like((count, units), f32), like((count, CLS), f32), like((count, BOX), f32)],
            [],
            smalls,
            [back],
            name="small_sum",
        )
    else:
        inner_sum = small_sum[:, :units]
        class_sum = small_sum[:, units : units + CLS]
        delta_sum = small_sum[:, units + class_room : units + class_room + BOX]
    back = exchange(back, "level").reshape(size, images, part, spots)
    map_grads = []
    for n in range(images):
        flat = contract_cols(across_first, back[:, n].reshape(channels, spots)).astype(bf16)
        map_grads.append(jnp.dot(flat, by_class, preferred_element_type=f32))
    map_grads = jnp.stack(map_grads).reshape(1, images, height, width, channels)

    if direct:
        piece = sum(part.astype(f32) for part in parts).astype(bf16)
        sent = contract_rows(from_span, piece).astype(bf16).reshape(size, span, units)
        bias_sums = tie(bias_sums, sent)
        came = exchange(sent, "level").reshape(size * span, units)
        hidden_sum = contract_rows(to_span, came)

    bias_total = butterfly(bias_sums)
    head_bias = bias_total[2, : class_room + delta_room]
    return (
        logits.reshape(images, regions, -1),
        deltas.reshape(images, regions, -1),
        map_grads,
        hidden_sum,
        bias_total[0],
        inner_sum,
        bias_total[1],
        class_sum,
        head_bias[:CLS],
        delta_sum,
        head_bias[class_room : class_room + BOX],
    )


def solution(mesh):
    return jax.shard_map(
        per_device,
        mesh=mesh,
        in_specs=(
            P("level", "img", None, None, None),
            P("img", "level", None),
            P("img", "level", None),
            P("img", "level"),
            P("img", "level"),
            P("img", "level", None),
            P(AXES, None),
            P(),
            P(AXES, None),
            P(),
            P(AXES, None),
            P(),
            P(AXES, None),
            P(),
        ),
        out_specs=(
            P("img", "level", None),
            P("img", "level", None),
            P("level", "img", None, None, None),
            P(AXES, None),
            P(),
            P(AXES, None),
            P(),
            P(AXES, None),
            P(),
            P(AXES, None),
            P(),
        ),
        check_vma=False,
    )
```

```python
import functools

import jax
import jax.numpy as jnp
import numpy as np
from jax import lax
from jax.experimental import pallas as pl
from jax.experimental.pallas import tpu as pltpu
from jax.sharding import PartitionSpec as P

POOL = 7
SAMPLES = 2
CLS = 81
BOX = 320
RPI = 512
BINS = POOL * POOL
LANES = 128
AXES = ("level", "img")
OFFSETS = (np.arange(SAMPLES * POOL, dtype=np.float32) + np.float32(0.5)) / np.float32(
    SAMPLES * POOL
)
SMALL_COST = pl.CostEstimate(flops=10**9, bytes_accessed=1, transcendentals=0)
LARGE_COST = pl.CostEstimate(flops=4 * 10**10, bytes_accessed=1, transcendentals=0)
f32 = jnp.float32
bf16 = jnp.bfloat16
ANY = pl.BlockSpec(memory_space=pl.ANY)
WHOLE = pl.BlockSpec(memory_space=pltpu.VMEM)
SCALAR = pl.BlockSpec(memory_space=pltpu.SMEM)
like = jax.ShapeDtypeStruct


def bin_weights(low, span, centres, at):
    first = jnp.maximum(1.0 - jnp.abs((low + OFFSETS[2 * at] * span) - centres), 0.0)
    second = jnp.maximum(1.0 - jnp.abs((low + OFFSETS[2 * at + 1] * span) - centres), 0.0)
    return ((first + second) * 0.5).astype(bf16)


def fill_weights(box_ref, down_ref, across_ref, height, width, level_count):
    x0, y0, x1, y1, level = [box_ref[k : k + 1, :] for k in range(5)]
    centres = lax.broadcasted_iota(jnp.int32, (width, LANES), 0).astype(f32)
    for q in range(POOL):
        across_ref[q] = bin_weights(x0, x1 - x0, centres, q).astype(f32)
    centres = lax.broadcasted_iota(jnp.int32, (height, LANES), 0).astype(f32)
    for p in range(POOL):
        weights = bin_weights(y0, y1 - y0, centres, p).astype(f32)
        for k in range(level_count):
            down_ref[k * height : (k + 1) * height, p * LANES : (p + 1) * LANES] = jnp.where(
                level == float(k), weights, 0.0
            ).astype(bf16)


def runs_of(order, length, part, group, room):
    place = {chunk: at // group * room + at % group * length for at, chunk in enumerate(order)}
    table = []
    for at in range(BINS):
        row, end, runs = at * part, (at + 1) * part, []
        while row < end:
            chunk = row // length
            stop = min(end, (chunk + 1) * length)
            runs.append((row - at * part, place[chunk] + row - chunk * length, stop - row))
            row = stop
        table.append(runs)
    return table


def gaps_of(table, features):
    held = sorted((kept, kept + count) for runs in table for row, kept, count in runs)
    gaps, last = [], 0
    for first, end in held + [(features, features)]:
        if first > last:
            gaps.append((last, first))
        last = end
    return gaps


def gather_kernel(number, seat_ref, *refs):
    kept_ref, sems = refs[-2:]
    rows = refs[0].shape[0]
    copies = []
    for k, ref in enumerate(refs[:number]):
        at = pl.multiple_of((seat_ref[0] ^ k) * rows, 16)
        copies.append(pltpu.make_async_copy(ref, kept_ref.at[pl.ds(at, rows)], sems.at[k]))
    for copy in copies:
        copy.start()
    for copy in copies:
        copy.wait()


def gather_pieces(seat, pieces):
    rows, units = pieces[0].shape
    number = len(pieces)
    return pl.pallas_call(
        functools.partial(gather_kernel, number),
        in_specs=[SCALAR] + [ANY for one in pieces],
        out_specs=WHOLE,
        out_shape=like((number * rows, units), bf16),
        scratch_shapes=[pltpu.SemaphoreType.DMA((number,))],
        compiler_params=pltpu.CompilerParams(vmem_limit_bytes=24 * 2**20),
        cost_estimate=LARGE_COST,
        name="gather_pieces",
    )(seat, *pieces)


def crop_kernel(table, sizes, product, box_ref, maps_ref, *refs):
    if product:
        weight_ref = refs[0]
        crop_ref, out_ref, down_ref, across_ref, sums_ref, rows_ref, turned_ref = refs[-7:]
    else:
        crop_ref, out_ref, down_ref, across_ref, sums_ref, rows_ref = refs[-6:]
    height, width, part, level_count = sizes
    for first, end in gaps_of(table, rows_ref.shape[0]):
        rows_ref[first:end, :] = jnp.zeros((end - first, LANES), f32)
    fill_weights(box_ref, down_ref, across_ref, height, width, level_count)
    sums_ref[...] = jnp.dot(maps_ref[...], down_ref[...], preferred_element_type=f32)
    for p in range(POOL):
        lanes = slice(p * LANES, (p + 1) * LANES)
        for start in range(0, POOL, 2):
            bins = range(start, min(POOL, start + 2))
            totals = [None for q in bins]
            for x in range(width):
                piece = sums_ref[x * part : (x + 1) * part, lanes]
                for at, q in enumerate(bins):
                    term = across_ref[q, x : x + 1, :] * piece
                    totals[at] = term if x == 0 else totals[at] + term
            for at, q in enumerate(bins):
                for row, kept, count in table[p * POOL + q]:
                    rows_ref[kept : kept + count, :] = totals[at][row : row + count]
    crop = rows_ref[...].astype(bf16)
    crop_ref[...] = crop
    if not product:
        out_ref[...] = crop.T
        return
    turned_ref[pl.ds(pl.multiple_of(pl.program_id(0) * LANES, LANES), LANES), :] = crop.T

    @pl.when(pl.program_id(0) == pl.num_programs(0) - 1)
    def multiply():
        out_ref[...] = jnp.dot(
            turned_ref[...], weight_ref[...], preferred_element_type=f32
        ).astype(out_ref.dtype)


def spread_kernel(table, sizes, more, box_ref, grad_ref, weight_ref, *refs):
    held_ref = refs[0]
    total_ref, down_ref, across_ref, sums_ref, rows_ref, crop_ref = refs[-6:]
    height, width, part, level_count = sizes
    images = box_ref.shape[0]
    for n in range(images):
        fill_weights(
            box_ref.at[n], down_ref.at[n], across_ref.at[n], height, width, level_count
        )
    crop_ref[...] = lax.dot_general(
        weight_ref[...], grad_ref[...], (((1,), (1,)), ((), ())), preferred_element_type=f32
    ).astype(bf16)
    for n in range(images):
        rows_ref[...] = crop_ref[:, n * LANES : (n + 1) * LANES].astype(f32)
        for p in range(POOL):
            lanes = slice(p * LANES, (p + 1) * LANES)
            pieces = []
            for q in range(POOL):
                runs = [rows_ref[kept : kept + count, :] for row, kept, count in table[p * POOL + q]]
                pieces.append(runs[0] if len(runs) == 1 else jnp.concatenate(runs, axis=0))
            for x in range(width):
                total = across_ref[n, 0, x : x + 1, :] * pieces[0]
                for q in range(1, POOL):
                    total = total + across_ref[n, q, x : x + 1, :] * pieces[q]
                sums_ref[x * part : (x + 1) * part, lanes] = total.astype(bf16)
        total = lax.dot_general(
            sums_ref[...], down_ref[n], (((1,), (1,)), ((), ())), preferred_element_type=f32
        )
        total_ref[n] = held_ref[n] + total if more else total


def crop_block(table, sizes, features, boxes, maps, weight=None, out_type=bf16, earlier=()):
    height, width, part, level_count = sizes
    images = boxes.shape[0]
    product = weight is not None
    first = [boxes, maps] + ([weight] if product else [])
    rows = images * LANES
    if product:
        units = weight.shape[1]
        out_spec = pl.BlockSpec((rows, units), lambda n: (0, 0))
        out_shape = like((rows, units), out_type)
        more = [pltpu.VMEM((rows, features), bf16)]
    else:
        out_spec = pl.BlockSpec((LANES, features), lambda n: (n, 0))
        out_shape = like((rows, features), bf16)
        more = []
    return pl.pallas_call(
        functools.partial(crop_kernel, table, sizes, product),
        grid=(images,),
        in_specs=[
            pl.BlockSpec((None, 8, LANES), lambda n: (n, 0, 0)),
            pl.BlockSpec((None, width * part, level_count * height), lambda n: (n, 0, 0)),
        ]
        + [WHOLE for one in first[2:]]
        + [ANY for one in earlier],
        out_specs=[pl.BlockSpec((features, LANES), lambda n: (0, n)), out_spec],
        out_shape=[like((features, rows), bf16), out_shape],
        scratch_shapes=[
            pltpu.VMEM((level_count * height, POOL * LANES), bf16),
            pltpu.VMEM((POOL, width, LANES), f32),
            pltpu.VMEM((width * part, POOL * LANES), f32),
            pltpu.VMEM((features, LANES), f32),
        ]
        + more,
        compiler_params=pltpu.CompilerParams(vmem_limit_bytes=24 * 2**20),
        cost_estimate=LARGE_COST,
        name="crop_block",
    )(*first, *earlier)


def multiply_kernel(scalars, arrays, outs):
    outs[0][...] = jnp.dot(
        arrays[0][...], arrays[1][...], preferred_element_type=f32
    ).astype(outs[0].dtype)


def spread_block(table, sizes, boxes, grads, weight, held, earlier=()):
    height, width, part, level_count = sizes
    images = boxes.shape[0]
    features = weight.shape[0]
    held = [] if held is None else [held]
    return pl.pallas_call(
        functools.partial(spread_kernel, table, sizes, bool(held)),
        in_specs=[WHOLE, WHOLE, WHOLE] + [WHOLE for one in held] + [ANY for one in earlier],
        out_specs=WHOLE,
        out_shape=like((images, width * part, level_count * height), f32),
        scratch_shapes=[
            pltpu.VMEM((images, level_count * height, POOL * LANES), bf16),
            pltpu.VMEM((images, POOL, width, LANES), f32),
            pltpu.VMEM((width * part, POOL * LANES), bf16),
            pltpu.VMEM((features, LANES), f32),
            pltpu.VMEM((features, images * LANES), bf16),
        ],
        compiler_params=pltpu.CompilerParams(vmem_limit_bytes=24 * 2**20),
        cost_estimate=LARGE_COST,
        name="spread_block",
    )(boxes, grads, weight, *held, *earlier)


def call(kernel, outs, scalars, arrays, earlier=(), scratch=(), name=None):
    arrays = list(arrays)

    def body(*refs):
        at, end = len(scalars), len(scalars) + len(arrays)
        kernel(refs[:at], refs[at:end], refs[end + len(earlier) :])

    result = pl.pallas_call(
        body,
        in_specs=[SCALAR for one in scalars] + [WHOLE for one in arrays] + [ANY for one in earlier],
        out_specs=[WHOLE for one in outs],
        out_shape=outs,
        scratch_shapes=scratch,
        compiler_params=pltpu.CompilerParams(vmem_limit_bytes=24 * 2**20),
        cost_estimate=LARGE_COST,
        name=name,
    )(*[jnp.full((1,), one, jnp.int32) for one in scalars], *arrays, *earlier)
    return result


def tie_kernel(*refs):
    pass


def tie(arrays, *earlier):
    return pl.pallas_call(
        tie_kernel,
        in_specs=[ANY for one in (*arrays, *earlier)],
        out_specs=[ANY for one in arrays],
        out_shape=[like(one.shape, one.dtype) for one in arrays],
        input_output_aliases={k: k for k in range(len(arrays))},
        cost_estimate=SMALL_COST,
        name="tie",
    )(*arrays, *earlier)


def order_kernel(first, scalars, arrays, outs):
    for k, ref in enumerate(arrays):
        outs[0][scalars[0][0] ^ k] = ref[first:]


def in_order(at, arrays, first, earlier):
    shape = (len(arrays), arrays[0].shape[0] - first) + arrays[0].shape[1:]
    return call(
        functools.partial(order_kernel, first),
        [like(shape, arrays[0].dtype)],
        [at],
        arrays,
        earlier,
        name="in_order",
    )[0]


def full_small_kernel(rows, scalars, arrays, outs):
    units = outs[0].shape[1]
    for k, ref in enumerate(arrays):
        core = scalars[0][0] ^ k
        for chip in range(ref.shape[0]):
            for level in range(ref.shape[1]):
                at = pl.multiple_of(((level * ref.shape[0] + chip) * 2 + core) * rows, rows)
                outs[0][pl.ds(at, rows), :] = ref[chip, level, :rows, :]
                for part in range(2):
                    outs[1][pl.ds(at + part * (rows // 2), rows // 2), :] = ref[
                        chip, level, rows:, part * (units // 2) : (part + 1) * (units // 2)
                    ]


def split_rows(core, array, rows, sent, kept):
    for at in range(array.shape[0] // rows // 2):
        mine = pl.multiple_of((2 * at + core) * rows, rows)
        other = pl.multiple_of((2 * at + 1 - core) * rows, rows)
        kept[at * rows : (at + 1) * rows, :] = array[pl.ds(mine, rows), :].astype(bf16)
        sent[at * rows : (at + 1) * rows, :] = array[pl.ds(other, rows), :].astype(bf16)


def put_biases(biases, refs):
    high = biases.astype(bf16)
    low = (biases - high.astype(f32)).astype(bf16)
    for ref in refs:
        end = ref.shape[0]
        ref[end - 16 : end - 8, : high.shape[1]] = high
        ref[end - 8 : end, : high.shape[1]] = low


def get_biases(ref, units):
    end = ref.shape[0]
    last = ref[end - 16 :, :units].astype(f32)
    return last[:8] + last[8:]


def small_product_kernel(rows, core_ref, first_ref, second_grad_ref, second_ref, slopes_ref, bias_ref, sent_ref, kept_ref, total_ref):
    turned = (((0,), (0,)), ((), ()))
    units = first_ref.shape[1]
    total_ref[:, :units] = lax.dot_general(
        first_ref[...], second_grad_ref[...], turned, preferred_element_type=f32
    )
    total_ref[:, units:] = lax.dot_general(
        second_ref[...], slopes_ref[...], turned, preferred_element_type=f32
    )
    split_rows(core_ref[0], total_ref, rows, sent_ref, kept_ref)
    put_biases(bias_ref[...], [sent_ref, kept_ref])


def small_product(core, rows, first_act, second_grad, second_act, slopes, biases):
    units = first_act.shape[1]
    wide = units + slopes.shape[1]
    half = like((units // 2 + 16, wide), bf16)
    return pl.pallas_call(
        functools.partial(small_product_kernel, rows),
        in_specs=[SCALAR] + [WHOLE] * 5,
        out_specs=[WHOLE] * 2,
        out_shape=[half, half],
        scratch_shapes=[pltpu.VMEM((units, wide), f32)],
        compiler_params=pltpu.CompilerParams(vmem_limit_bytes=24 * 2**20),
        cost_estimate=LARGE_COST,
        name="small_product",
    )(jnp.full((1,), core, jnp.int32), first_act, second_grad, second_act, slopes, biases)


def fold_kernel(rows, bit_ref, kept_ref, come_ref, *refs):
    sent_out, kept_out, total_ref = refs[-3:]
    count, units = total_ref.shape[0], total_ref.shape[1] // 3 * 2
    total_ref[...] = kept_ref[:count, :].astype(f32) + come_ref[:count, :].astype(f32)
    split_rows(bit_ref[0], total_ref, rows, sent_out, kept_out)
    put_biases(get_biases(kept_ref, units) + get_biases(come_ref, units), [sent_out, kept_out])


def fold_rows(bit, rows, kept, come, earlier):
    count = kept.shape[0] - 16
    half = like((count // 2 + 16, kept.shape[1]), bf16)
    return pl.pallas_call(
        functools.partial(fold_kernel, rows),
        in_specs=[SCALAR, WHOLE, WHOLE] + [ANY for one in earlier],
        out_specs=[WHOLE] * 2,
        out_shape=[half, half],
        scratch_shapes=[pltpu.VMEM((count, kept.shape[1]), f32)],
        compiler_params=pltpu.CompilerParams(vmem_limit_bytes=24 * 2**20),
        cost_estimate=LARGE_COST,
        name="fold_rows",
    )(jnp.full((1,), bit, jnp.int32), kept, come, *earlier)


def last_fold_kernel(rows, scalars, arrays, outs):
    units = outs[0].shape[1]
    biases = get_biases(arrays[0], units) + get_biases(arrays[1], units)
    put_biases(biases, outs)
    for way, out in enumerate(outs):
        at = pl.multiple_of((scalars[0][0] ^ way) * rows, rows)
        total = sum(ref[pl.ds(at, rows), :].astype(f32) for ref in arrays).astype(bf16)
        out[:rows, :] = total[:, :units]
        for part in range(2):
            out[rows : rows // 2 * 3, part * (units // 2) : (part + 1) * (units // 2)] = total[
                part * (rows // 2) : (part + 1) * (rows // 2), units:
            ]


def small_sum_kernel(scalars, arrays, outs):
    total = sum(ref[...].astype(f32) for ref in arrays)
    rows, units = outs[0].shape
    biases = [get_biases(ref, units) for ref in arrays]
    outs[3][...] = (biases[0] + biases[1]) + (biases[2] + biases[3])
    outs[0][...] = total[:rows]
    for part in range(2):
        at = slice(part * (rows // 2), (part + 1) * (rows // 2))
        beside = total[rows : rows // 2 * 3, part * (units // 2) : (part + 1) * (units // 2)]
        outs[1][at, :] = beside[:, :CLS]
        outs[2][at, :] = beside[:, LANES : LANES + BOX]


def gelu_and_slope(values):
    normal = 0.5 * (1.0 + lax.erf(values * np.float32(np.sqrt(0.5))))
    density = jnp.exp(-0.5 * values * values) * np.float32(1.0 / np.sqrt(2.0 * np.pi))
    return values * normal, normal + values * density


def head_kernel(
    own_ref, one_ref, two_ref, three_ref, rows_ref, hidden_bias_ref, inner_ref, inner_bias_ref, heads_ref, heads_bias_ref,
    logits_ref, deltas_ref, first_act_ref, second_act_ref, slopes_ref, second_grad_ref, first_grad_ref, again_ref, bias_ref, first_slope_ref, second_slope_ref,
):
    first_pre = own_ref[...] + hidden_bias_ref[...]
    for come_ref in (one_ref, two_ref, three_ref):
        first_pre = first_pre + come_ref[...].astype(f32)
    act, slope = gelu_and_slope(first_pre)
    first_slope_ref[...] = slope
    act = act.astype(bf16)
    first_act_ref[...] = act
    second_pre = jnp.dot(act, inner_ref[...], preferred_element_type=f32) + inner_bias_ref[...]
    act, slope = gelu_and_slope(second_pre)
    second_slope_ref[...] = slope
    act = act.astype(bf16)
    second_act_ref[...] = act
    heads = jnp.dot(act, heads_ref[...], preferred_element_type=f32) + heads_bias_ref[...]
    logits, deltas = heads[:, :LANES], heads[:, LANES:]
    logits_ref[...] = logits[:, :CLS]
    deltas_ref[...] = deltas[:, :BOX]
    label = rows_ref[:, 0:1]
    kept = 1.0 - rows_ref[:, 1:2]
    column = lax.broadcasted_iota(jnp.int32, logits.shape, 1)
    valid = column < CLS
    row_max = jnp.max(jnp.where(valid, logits, -jnp.inf), axis=1, keepdims=True)
    exponent = jnp.where(valid, jnp.exp(jnp.where(valid, logits - row_max, 0.0)), 0.0)
    softmax_rows = exponent / jnp.sum(exponent, axis=1, keepdims=True)
    hot = (column.astype(f32) == label).astype(f32)
    logit_slope = (softmax_rows - hot) * (kept * np.float32(1.0 / RPI))
    column = lax.broadcasted_iota(jnp.int32, deltas.shape, 1)
    target = rows_ref[:, 2:3]
    for j in range(1, 4):
        target = jnp.where((column & 3) == j, rows_ref[:, 2 + j : 3 + j], target)
    foreground = jnp.where(label < CLS - 1, kept, 0.0)
    hot = ((column >> 2).astype(f32) == label) & (column < BOX)
    delta_slope = jnp.where(
        hot,
        jnp.clip(deltas - target, -1.0, 1.0) * (foreground * np.float32(1.0 / RPI)),
        0.0,
    )
    slopes = jnp.concatenate([logit_slope, delta_slope], axis=1).astype(bf16)
    slopes_ref[...] = slopes
    turned = (((1,), (1,)), ((), ()))
    act_grad = lax.dot_general(slopes, heads_ref[...], turned, preferred_element_type=f32)
    second_grad = (act_grad * second_slope_ref[...]).astype(bf16)
    second_grad_ref[...] = second_grad
    act_grad = lax.dot_general(second_grad, inner_ref[...], turned, preferred_element_type=f32)
    first_grad = (act_grad * first_slope_ref[...]).astype(bf16)
    first_grad_ref[...] = first_grad
    again_ref[...] = first_grad
    units = first_grad.shape[1]
    bias_ref[...] = jnp.zeros_like(bias_ref)
    bias_ref[0:1, :] = jnp.sum(first_grad.astype(f32), axis=0, keepdims=True)
    bias_ref[1:2, :] = jnp.sum(second_grad.astype(f32), axis=0, keepdims=True)
    bias_ref[2:3, : slopes.shape[1]] = jnp.sum(slopes.astype(f32), axis=0, keepdims=True)


def head_block(own, come, rows, hidden_bias, inner, inner_bias, heads, heads_bias):
    count, units = own.shape
    wide = heads.shape[1]
    return pl.pallas_call(
        head_kernel,
        in_specs=[pl.BlockSpec(memory_space=pltpu.VMEM)] * 10,
        out_specs=[pl.BlockSpec(memory_space=pltpu.VMEM)] * 9,
        out_shape=[
            like((count, CLS), f32),
            like((count, BOX), f32),
            like((count, units), bf16),
            like((count, units), bf16),
            like((count, wide), bf16),
            like((count, units), bf16),
            like((count, units), bf16),
            like((count, units), bf16),
            like((8, units), f32),
        ],
        scratch_shapes=[pltpu.VMEM((count, units), f32)] * 2,
        compiler_params=pltpu.CompilerParams(vmem_limit_bytes=24 * 2**20),
        cost_estimate=LARGE_COST,
        name="head_block",
    )(own, *come, rows, hidden_bias, inner, inner_bias, heads, heads_bias)


def maps_kernel(scalars, arrays, outs):
    maps_ref, by_class_ref, across_first_ref = arrays[:3]
    pick_ref = outs[-1]
    size, part = by_class_ref.shape[:2]
    images = maps_ref.shape[0]
    for way in range(size):
        pick_ref[way * part : (way + 1) * part, :] = by_class_ref[scalars[0][0] ^ way]
    for n in range(images):
        flat = lax.dot_general(
            pick_ref[...], maps_ref[n], (((1,), (1,)), ((), ())), preferred_element_type=f32
        ).astype(bf16)
        flat = jnp.dot(flat, across_first_ref[...], preferred_element_type=f32).astype(bf16)
        for way in range(size):
            outs[way][n * part : (n + 1) * part, :] = flat[way * part : (way + 1) * part]
    for out in outs[:size]:
        for below in arrays[3:]:
            out[images * part :, :] = below[...]


def maps_back_kernel(scalars, arrays, outs):
    came_refs, (by_class_ref, across_first_ref) = arrays[:-2], arrays[-2:]
    out_ref, pick_ref, flat_ref = outs
    size, part = by_class_ref.shape[:2]
    for way in range(size):
        pick_ref[way * part : (way + 1) * part, :] = by_class_ref[scalars[0][0] ^ way]
    for n in range(out_ref.shape[0]):
        for way in range(size):
            flat_ref[way * part : (way + 1) * part, :] = came_refs[way][n]
        cells = lax.dot_general(
            across_first_ref[...], flat_ref[...], (((1,), (1,)), ((), ())), preferred_element_type=f32
        ).astype(bf16)
        out_ref[n] = jnp.dot(cells, pick_ref[...], preferred_element_type=f32)


def arrange_kernel(sizes, scalars, arrays, outs):
    height, width, part, level_count = sizes
    for n in range(outs[0].shape[0]):
        for x in range(width):
            for k, ref in enumerate(arrays):
                outs[0][n, x * part : (x + 1) * part, k * height : (k + 1) * height] = ref[
                    n * part : (n + 1) * part, x * height : (x + 1) * height
                ]


def arrange_back_kernel(sizes, scalars, arrays, outs):
    height, width, part, level_count = sizes
    for n in range(arrays[0].shape[0]):
        for x in range(width):
            for k, ref in enumerate(outs):
                ref[n, :, x * height : (x + 1) * height] = arrays[0][
                    n, x * part : (x + 1) * part, k * height : (k + 1) * height
                ].astype(bf16)


def split_span_kernel(scalars, arrays, outs):
    total_ref = outs[-1]
    span = outs[0].shape[0]
    total_ref[...] = sum(
        jnp.dot(arrays[k][...], arrays[k + 1][...], preferred_element_type=f32)
        for k in range(0, len(arrays), 2)
    )
    for way, out in enumerate(outs[:-1]):
        at = pl.multiple_of((scalars[0][0] ^ way) * span, 8)
        out[...] = total_ref[pl.ds(at, span), :].astype(bf16)


def join_span_kernel(scalars, arrays, outs):
    total_ref = outs[-1]
    span = arrays[1].shape[0]
    for way, ref in enumerate(arrays[1:]):
        at = pl.multiple_of((scalars[0][0] ^ way) * span, 8)
        total_ref[pl.ds(at, span), :] = ref[...].astype(f32)
    product = jnp.dot(arrays[0][...], total_ref[...].astype(bf16), preferred_element_type=f32)
    for out in outs[:-1]:
        out[...] = product.astype(out.dtype)


def return_span_kernel(scalars, arrays, outs):
    total_ref = outs[-1]
    span = outs[0].shape[0]
    piece = sum(ref[...].astype(f32) for ref in arrays[1:]).astype(bf16)
    total_ref[...] = jnp.dot(arrays[0][...], piece, preferred_element_type=f32)
    for way, out in enumerate(outs[:-1]):
        at = pl.multiple_of((scalars[0][0] ^ way) * span, 8)
        out[...] = total_ref[pl.ds(at, span), :].astype(bf16)


def picking(rows, columns, pairs):
    matrix = np.zeros((rows, columns), np.float32)
    for a, b in pairs:
        matrix[a, b] = 1.0
    return jnp.asarray(matrix, bf16)


def swap(array, axis, bit):
    size = lax.axis_size(axis)
    return lax.ppermute(array, axis, [(at, at ^ bit) for at in range(size)])


def exchange(array, axis):
    return lax.all_to_all(array, axis, split_axis=0, concat_axis=0, tiled=True)


def exchange_ways(arrays, axis):
    return [arrays[0]] + [swap(one, axis, way) for way, one in enumerate(arrays) if way]


def product_kernel(number, parts, with_sum, at_ref, *refs):
    grad_refs, crop_refs, refs = refs[:parts], refs[parts : parts * (number + 1)], refs[parts * (number + 1) :]
    outs = refs[-number:] if with_sum else [refs[-1].at[n] for n in range(number)]
    for n in range(number):
        total = refs[0][n].astype(f32) if with_sum else 0.0
        for k, grad_ref in enumerate(grad_refs):
            total = total + jnp.dot(
                crop_refs[n * parts + k][...], grad_ref[...], preferred_element_type=f32
            )
        outs[n][...] = total.astype(bf16)


def piece_product(crops, grads, pieces, come, earlier):
    features, count = crops[0].shape
    units = grads[0].shape[1]
    rows = features // 8
    number = len(pieces)
    with_sum = come is not None
    crops = [one.reshape(8, rows, count) for one in crops]
    single = pl.BlockSpec((rows, units), lambda n, at: (0, 0))
    stacked = pl.BlockSpec((number, rows, units), lambda n, at: (0, 0, 0))
    return pl.pallas_call(
        functools.partial(product_kernel, number, len(grads), with_sum),
        grid_spec=pltpu.PrefetchScalarGridSpec(
            num_scalar_prefetch=1,
            grid=(1,),
            in_specs=[pl.BlockSpec(one.shape, lambda n, at: (0, 0)) for one in grads]
            + [
                pl.BlockSpec((None, rows, count), lambda n, at, k=k: (at[k], 0, 0))
                for k in range(number)
                for one in crops
            ]
            + ([stacked] if with_sum else [])
            + [ANY for one in earlier],
            out_specs=[single] * number if with_sum else stacked,
        ),
        out_shape=[like((rows, units), bf16)] * number
        if with_sum
        else like((number, rows, units), bf16),
        compiler_params=pltpu.CompilerParams(vmem_limit_bytes=24 * 2**20),
        cost_estimate=LARGE_COST,
        name="piece_product",
    )(jnp.stack(pieces), *grads, *crops * number, *([come] if with_sum else []), *earlier)


def butterfly(array):
    for axis in ("img", "level"):
        bit = 1
        while bit < lax.axis_size(axis):
            array = array + swap(array, axis, bit)
            bit *= 2
    return array


def contract_rows(left_side, right_side):
    return lax.dot_general(
        left_side, right_side, (((0,), (0,)), ((), ())), preferred_element_type=f32
    )


def pack_rows(array):
    rows, units = array.shape[-2], array.shape[-1] // 3 * 2
    beside = array[..., units:]
    below = jnp.concatenate([beside[..., : rows // 2, :], beside[..., rows // 2 :, :]], axis=-1)
    return jnp.concatenate([array[..., :units], below], axis=-2)


def per_device(
    pyramid,
    levels,
    region_boxes,
    labels,
    crowd_ignore,
    targets,
    hidden_weight,
    hidden_bias,
    inner_weight,
    inner_bias,
    class_weight,
    class_bias,
    delta_weight,
    delta_bias,
):
    size = lax.axis_size("level")
    planes = lax.axis_size("img")
    z = lax.axis_index("level")
    place = lax.axis_index("img")
    core, x, y = place % 2, place // 2 % 2, place // 4
    images, height, width, channels = pyramid.shape[1:]
    regions = levels.shape[1]
    part = channels // size
    sizes = (height, width, part, size)
    rows, units = hidden_weight.shape
    block_rows = images * regions
    direct = planes == 8 and rows % size == 0

    packed = jnp.concatenate(
        [
            jnp.transpose(region_boxes, (0, 2, 1)),
            jnp.transpose(levels, (0, 2, 1)),
            jnp.zeros((images, 3, regions), jnp.int32),
        ],
        axis=1,
    )
    class_room, delta_room = LANES, units // 2 - LANES
    small = jnp.concatenate(
        [
            inner_weight,
            jnp.pad(class_weight, ((0, 0), (0, class_room - CLS))),
            jnp.pad(delta_weight, ((0, 0), (0, delta_room - BOX))),
        ],
        axis=1,
    )
    heads_bias = jnp.concatenate(
        [
            jnp.pad(class_bias, (0, class_room - CLS)),
            jnp.pad(delta_bias, (0, delta_room - BOX)),
        ]
    )[None]

    if direct:
        length = rows // size
        span = -(-(length + images) // 8) * 8
        extra = jnp.concatenate(
            [packed.astype(bf16).reshape(images, units), jnp.zeros((16 - images, units), bf16)]
        )
        to_span = picking(
            size * span,
            rows,
            [(k * span + j, j * size + k) for k in range(size) for j in range(length)],
        )
        extra_span = picking(
            size * span,
            16,
            [(k * span + length + n, n) for k in range(size) for n in range(images)],
        )
        room = -(-rows // 16) * 16
        features = planes * room
        from_span = picking(
            room,
            size * span,
            [(k * length + j, k * span + j) for k in range(size) for j in range(length)],
        )
        total = [pltpu.VMEM((size * span, units), f32)]
        sent = call(
            split_span_kernel,
            [like((span, units), bf16)] * size,
            [z],
            [to_span, hidden_weight, extra_span, extra],
            scratch=total,
            name="split_span",
        )
        came = exchange_ways(sent, "level")
        piece, own_piece = call(
            join_span_kernel,
            [like((room, units), bf16)] * 2,
            [z],
            [from_span, *came],
            scratch=total,
            name="join_span",
        )
        boxes = jnp.stack([one[length : length + images].reshape(images, 8, regions) for one in came])
        pieces = [own_piece] + [swap(piece, "img", bit) for bit in (2, 4, 6)]
        order = [k * planes + at for at in range(planes) for k in range(size)]
        table = runs_of(order, length, part, size, room)
    else:
        boxes = exchange(jnp.broadcast_to(packed[None], (size,) + packed.shape), "level")
        boxes = jnp.stack([lax.dynamic_index_in_dim(boxes, z ^ way, 0, False) for way in range(size)])
        features = BINS * part
        whole = lax.all_gather(hidden_weight, AXES, axis=0, tiled=True)
        weight = lax.dynamic_index_in_dim(whole.reshape(features, size, units), z, 1, False)
        table = runs_of([0], features, part, 1, features)
    row = jnp.arange(8)[:, None]
    boxes = jnp.where(row == 4, boxes.astype(jnp.int32) ^ z, boxes.astype(jnp.int32)).astype(f32)

    spots = height * width
    by_class = picking(
        channels, channels, [(c % size * part + c // size, c) for c in range(channels)]
    ).reshape(size, part, channels)
    across_first = picking(
        spots, spots, [(y * width + x, x * height + y) for y in range(height) for x in range(width)]
    )
    picks = [
        pltpu.VMEM((channels, channels), bf16),
        pltpu.VMEM((channels, spots), bf16),
    ]
    small_rows = small.shape[0] // 2 * 3 if direct else 0
    maps = call(
        maps_kernel,
        [like((images * part + small_rows, spots), bf16)] * size,
        [z],
        [pyramid[0].reshape(images, spots, channels), by_class, across_first]
        + ([pack_rows(small)] if direct else []),
        scratch=picks[:1],
        name="maps",
    )
    if direct:
        maps = [maps[0], *tie(maps[1:], piece)]
    maps_came = exchange_ways(maps[:3], "level")
    maps_came.append(swap(tie([maps[3]], maps_came[1])[0], "level", 3))
    maps = call(
        functools.partial(arrange_kernel, sizes),
        [like((images, width * part, size * height), bf16)],
        [],
        maps_came,
        name="arrange",
    )[0]

    ways = (2, 3, 1, 0)
    crops, owns, came_sums = [], [], []
    for turn, way in enumerate(ways):
        if turn == 0:
            crop, turned = crop_block(table, sizes, features, boxes[way], maps)
            if direct:
                pieces = tie(pieces, crop)
                pieces = sum(([one, swap(one, "img", 1)] for one in pieces), [])
                weight = gather_pieces(jnp.full((1,), place, jnp.int32), pieces)
            owns += call(
                multiply_kernel, [like((block_rows, units), bf16)], [], [turned, weight], name="multiply"
            )
        else:
            crop, own = crop_block(
                table, sizes, features, boxes[way], maps, weight, bf16 if way else f32, owns[-1:]
            )
            owns.append(own)
        crops.append(crop)
        if way:
            came_sums.append(swap(owns[-1], "level", way))

    if direct:
        smalls = in_order(z, maps_came, images * part, owns[:1])
        smalls = in_order(
            place // 2, [smalls] + [swap(smalls, "img", bit) for bit in (2, 4, 6)], 0, owns[2:3]
        )
        full_inner, full_heads = call(
            functools.partial(full_small_kernel, small.shape[0]),
            [like((units, units), bf16), like((units, units // 2), bf16)],
            [core],
            [smalls, swap(smalls, "img", 1)],
            name="full_small",
        )
    else:
        smalls = lax.all_gather(small, AXES, axis=0, tiled=True)
        full_inner, full_heads = smalls[:, :units], smalls[:, units:]

    row_facts = jnp.concatenate(
        [
            labels.reshape(-1, 1).astype(f32),
            crowd_ignore.reshape(-1, 1).astype(f32),
            targets.reshape(-1, 4),
            jnp.zeros((block_rows, 2), f32),
        ],
        axis=1,
    )
    logits, deltas, first_act, second_act, slopes, second_grad, first_grad, first_again, bias_sums = head_block(
        owns[-1],
        came_sums,
        row_facts,
        hidden_bias[None],
        full_inner,
        inner_bias[None],
        full_heads,
        heads_bias,
    )

    near = swap(first_grad, "level", 1)
    far = swap(first_grad, "level", 2)
    grad_of = {0: first_grad, 1: near, 2: far}

    def take_up(way, held, earlier=()):
        return spread_block(table, sizes, boxes[way], grad_of[way], weight, held, earlier)

    if direct:
        count = small.shape[0]
        sent, kept = small_product(
            core, count, first_act, second_grad, second_act, slopes, bias_sums
        )
        held = take_up(0, None, [kept])
        sent, kept = fold_rows(x, count, kept, swap(sent, "img", 1), [held])
        grad_of[3] = swap(tie([first_again], far, kept)[0], "level", 3)
        held = take_up(1, held, [kept])
        sent, kept = fold_rows(y, count, kept, swap(sent, "img", 2), [held])
        held = take_up(2, held, [kept])
        smalls = call(
            functools.partial(last_fold_kernel, count),
            [like((small_rows + 16, units), bf16)] * size,
            [z],
            [kept, swap(sent, "img", 4)],
            [held],
            name="last_fold",
        )

        grads = [grad_of[way] for way in ways]
        parts, others = {}, {}

        def for_other(bits, earlier):
            at = [place ^ bit ^ 1 for bit in bits]
            products = piece_product(crops, grads, at, None, earlier)
            others[bits] = swap(products, "img", 1)
            return [products]

        def for_own(bits, earlier):
            at = [place ^ bit for bit in bits]
            own = piece_product(crops, grads, at, others[bits], earlier)
            for one, bit in zip(own, bits):
                parts[bit] = swap(one, "img", bit) if bit else one
            return own

        earlier = for_other((6,), smalls[:1])
        earlier = for_other((2, 4), earlier)
        earlier = for_own((6,), earlier)
        held = take_up(3, held, earlier)
        back = call(
            functools.partial(arrange_back_kernel, sizes),
            [like((images, part, spots), bf16)] * size,
            [],
            [held],
            name="arrange_back",
        )
        earlier = for_other((0,), back[:1])
        inner_sum, class_sum, delta_sum, bias_total = call(
            small_sum_kernel,
            [
                like((count, units), f32),
                like((count, CLS), f32),
                like((count, BOX), f32),
                like((8, units), f32),
            ],
            [],
            exchange_ways(smalls, "level"),
            earlier,
            name="small_sum",
        )
        earlier = for_own((2, 4), [inner_sum])
        earlier = for_own((0,), earlier)
    else:
        held = None
        grad_of[3] = swap(first_again, "level", 3)
        for way in range(size):
            held = take_up(way, held)
        back = call(
            functools.partial(arrange_back_kernel, sizes),
            [like((images, part, spots), bf16)] * size,
            [],
            [held],
            name="arrange_back",
        )
        bias_total = butterfly(bias_sums)
        small_sum = jnp.concatenate(
            [contract_rows(first_act, second_grad), contract_rows(second_act, slopes)], axis=1
        )
        small_sum = lax.psum_scatter(small_sum, AXES, scatter_dimension=0, tiled=True)
        inner_sum = small_sum[:, :units]
        class_sum = small_sum[:, units : units + CLS]
        delta_sum = small_sum[:, units + class_room : units + class_room + BOX]
        whole_grads = jnp.concatenate([grad_of[way] for way in ways])
        product = jnp.dot(
            jnp.concatenate(crops, axis=1), whole_grads, preferred_element_type=f32
        )
        own = (jnp.arange(size, dtype=jnp.int32) == z)[None, :, None]
        hidden_sum = lax.psum_scatter(
            jnp.where(own, product[:, None, :], 0.0).reshape(features * size, units),
            AXES,
            scatter_dimension=0,
            tiled=True,
        )

    map_grads = call(
        maps_back_kernel,
        [like((images, spots, channels), f32)],
        [z],
        [*exchange_ways(back, "level"), by_class, across_first],
        scratch=picks,
        name="maps_back",
    )[0].reshape(1, images, height, width, channels)

    if direct:
        sent = call(
            return_span_kernel,
            [like((span, units), bf16)] * size,
            [z],
            [from_span.T, *[parts[bit] for bit in (0, 2, 4, 6)]],
            scratch=total,
            name="return_span",
        )
        hidden_sum = call(
            join_span_kernel,
            [like((rows, units), f32)],
            [z],
            [to_span.T, *exchange_ways(sent, "level")],
            scratch=total,
            name="join_span",
        )[0]

    head_bias = bias_total[2, : class_room + delta_room]
    return (
        logits.reshape(images, regions, -1),
        deltas.reshape(images, regions, -1),
        map_grads,
        hidden_sum,
        bias_total[0],
        inner_sum,
        bias_total[1],
        class_sum,
        head_bias[:CLS],
        delta_sum,
        head_bias[class_room : class_room + BOX],
    )


def solution(mesh):
    return jax.shard_map(
        per_device,
        mesh=mesh,
        in_specs=(
            P("level", "img", None, None, None),
            P("img", "level", None),
            P("img", "level", None),
            P("img", "level"),
            P("img", "level"),
            P("img", "level", None),
            P(AXES, None),
            P(),
            P(AXES, None),
            P(),
            P(AXES, None),
            P(),
            P(AXES, None),
            P(),
        ),
        out_specs=(
            P("img", "level", None),
            P("img", "level", None),
            P("level", "img", None, None, None),
            P(AXES, None),
            P(),
            P(AXES, None),
            P(),
            P(AXES, None),
            P(),
            P(AXES, None),
            P(),
        ),
        check_vma=False,
    )
```

```python
import functools

import jax
import jax.numpy as jnp
import numpy as np
from jax import lax
from jax.experimental import pallas as pl
from jax.experimental.pallas import tpu as pltpu
from jax.sharding import PartitionSpec as P

POOL = 7
SAMPLES = 2
CLS = 81
BOX = 320
RPI = 512
BINS = POOL * POOL
LANES = 128
AXES = ("level", "img")
OFFSETS = (np.arange(SAMPLES * POOL, dtype=np.float32) + np.float32(0.5)) / np.float32(
    SAMPLES * POOL
)
SMALL_COST = pl.CostEstimate(flops=10**9, bytes_accessed=1, transcendentals=0)
LARGE_COST = pl.CostEstimate(flops=4 * 10**10, bytes_accessed=1, transcendentals=0)
f32 = jnp.float32
bf16 = jnp.bfloat16
FAR = pl.BlockSpec(memory_space=pl.ANY)
WHOLE = pl.BlockSpec(memory_space=pltpu.VMEM)
SCALAR = pl.BlockSpec(memory_space=pltpu.SMEM)
like = jax.ShapeDtypeStruct
SIGN = jax.ShapeDtypeStruct((8, LANES), jnp.float32)


def bin_weights(low, span, centres, at):
    first = jnp.maximum(1.0 - jnp.abs((low + OFFSETS[2 * at] * span) - centres), 0.0)
    second = jnp.maximum(1.0 - jnp.abs((low + OFFSETS[2 * at + 1] * span) - centres), 0.0)
    return ((first + second) * 0.5).astype(bf16)


def fill_weights(box_ref, down_ref, across_ref, height, width, level_count):
    x0, y0, x1, y1, level = [box_ref[k : k + 1, :] for k in range(5)]
    centres = lax.broadcasted_iota(jnp.int32, (width, LANES), 0).astype(f32)
    for q in range(POOL):
        across_ref[q] = bin_weights(x0, x1 - x0, centres, q).astype(f32)
    centres = lax.broadcasted_iota(jnp.int32, (height, LANES), 0).astype(f32)
    for p in range(POOL):
        weights = bin_weights(y0, y1 - y0, centres, p).astype(f32)
        for k in range(level_count):
            down_ref[k * height : (k + 1) * height, p * LANES : (p + 1) * LANES] = jnp.where(
                level == float(k), weights, 0.0
            ).astype(bf16)


def runs_of(order, length, part, group, room):
    place = {chunk: at // group * room + at % group * length for at, chunk in enumerate(order)}
    table = []
    for at in range(BINS):
        row, end, runs = at * part, (at + 1) * part, []
        while row < end:
            chunk = row // length
            stop = min(end, (chunk + 1) * length)
            runs.append((row - at * part, place[chunk] + row - chunk * length, stop - row))
            row = stop
        table.append(runs)
    return table


def gaps_of(table, features):
    held = sorted((kept, kept + count) for runs in table for row, kept, count in runs)
    gaps, last = [], 0
    for first, end in held + [(features, features)]:
        if first > last:
            gaps.append((last, first))
        last = end
    return gaps


def gather_kernel(number, seat_ref, *refs):
    kept_ref, sems = refs[-2:]
    rows = refs[0].shape[0]
    copies = []
    for k, ref in enumerate(refs[:number]):
        at = pl.multiple_of((seat_ref[0] ^ k) * rows, 16)
        copies.append(pltpu.make_async_copy(ref, kept_ref.at[pl.ds(at, rows)], sems.at[k]))
    for copy in copies:
        copy.start()
    for copy in copies:
        copy.wait()


def gather_pieces(seat, pieces):
    rows, units = pieces[0].shape
    number = len(pieces)
    return pl.pallas_call(
        functools.partial(gather_kernel, number),
        in_specs=[SCALAR] + [FAR for one in pieces],
        out_specs=WHOLE,
        out_shape=pltpu.VMEM((number * rows, units), bf16),
        scratch_shapes=[pltpu.SemaphoreType.DMA((number,))],
        compiler_params=pltpu.CompilerParams(vmem_limit_bytes=24 * 2**20),
        cost_estimate=LARGE_COST,
        name="gather_pieces",
    )(seat, *pieces)


def crop_kernel(table, sizes, product, box_ref, maps_ref, *refs):
    if product:
        weight_ref = refs[0]
        crop_ref, out_ref, sign_ref, down_ref, across_ref, sums_ref, rows_ref, turned_ref = refs[-8:]
    else:
        crop_ref, out_ref, sign_ref, down_ref, across_ref, sums_ref, rows_ref = refs[-7:]
    sign_ref[...] = jnp.zeros_like(sign_ref)
    height, width, part, level_count = sizes
    for first, end in gaps_of(table, rows_ref.shape[0]):
        rows_ref[first:end, :] = jnp.zeros((end - first, LANES), f32)
    fill_weights(box_ref, down_ref, across_ref, height, width, level_count)
    sums_ref[...] = jnp.dot(maps_ref[...], down_ref[...], preferred_element_type=f32)
    for p in range(POOL):
        lanes = slice(p * LANES, (p + 1) * LANES)
        for start in range(0, POOL, 2):
            bins = range(start, min(POOL, start + 2))
            totals = [None for q in bins]
            for x in range(width):
                piece = sums_ref[x * part : (x + 1) * part, lanes]
                for at, q in enumerate(bins):
                    term = across_ref[q, x : x + 1, :] * piece
                    totals[at] = term if x == 0 else totals[at] + term
            for at, q in enumerate(bins):
                for row, kept, count in table[p * POOL + q]:
                    rows_ref[kept : kept + count, :] = totals[at][row : row + count]
    crop = rows_ref[...].astype(bf16)
    crop_ref[...] = crop
    if not product:
        out_ref[...] = crop.T
        return
    turned_ref[pl.ds(pl.multiple_of(pl.program_id(0) * LANES, LANES), LANES), :] = crop.T

    @pl.when(pl.program_id(0) == pl.num_programs(0) - 1)
    def multiply():
        out_ref[...] = jnp.dot(
            turned_ref[...], weight_ref[...], preferred_element_type=f32
        ).astype(out_ref.dtype)


def spread_kernel(table, sizes, box_ref, grad_ref, weight_ref, *refs):
    total_ref, sign_ref, down_ref, across_ref, sums_ref, rows_ref, crop_ref = refs[-7:]
    sign_ref[...] = jnp.zeros_like(sign_ref)
    height, width, part, level_count = sizes
    images = box_ref.shape[0]
    for n in range(images):
        fill_weights(
            box_ref.at[n], down_ref.at[n], across_ref.at[n], height, width, level_count
        )
    crop_ref[...] = lax.dot_general(
        weight_ref[...], grad_ref[...], (((1,), (1,)), ((), ())), preferred_element_type=f32
    ).astype(bf16)
    for n in range(images):
        rows_ref[...] = crop_ref[:, n * LANES : (n + 1) * LANES].astype(f32)
        for p in range(POOL):
            lanes = slice(p * LANES, (p + 1) * LANES)
            pieces = []
            for q in range(POOL):
                runs = [rows_ref[kept : kept + count, :] for row, kept, count in table[p * POOL + q]]
                pieces.append(runs[0] if len(runs) == 1 else jnp.concatenate(runs, axis=0))
            for x in range(width):
                total = across_ref[n, 0, x : x + 1, :] * pieces[0]
                for q in range(1, POOL):
                    total = total + across_ref[n, q, x : x + 1, :] * pieces[q]
                sums_ref[x * part : (x + 1) * part, lanes] = total.astype(bf16)
        total_ref[n] = lax.dot_general(
            sums_ref[...], down_ref[n], (((1,), (1,)), ((), ())), preferred_element_type=f32
        ).astype(bf16)


def crop_block(table, sizes, features, boxes, maps, weight=None, out_type=bf16, earlier=(), kept_in=like):
    height, width, part, level_count = sizes
    images = boxes.shape[0]
    product = weight is not None
    first = [boxes, maps] + ([weight] if product else [])
    rows = images * LANES
    if product:
        units = weight.shape[1]
        out_spec = pl.BlockSpec((rows, units), lambda n: (0, 0))
        out_shape = like((rows, units), out_type)
        more = [pltpu.VMEM((rows, features), bf16)]
    else:
        out_spec = pl.BlockSpec((LANES, features), lambda n: (n, 0))
        out_shape = kept_in((rows, features), bf16)
        more = []
    return pl.pallas_call(
        functools.partial(crop_kernel, table, sizes, product),
        grid=(images,),
        in_specs=[
            pl.BlockSpec((None, 8, LANES), lambda n: (n, 0, 0)),
            pl.BlockSpec((None, width * part, level_count * height), lambda n: (n, 0, 0)),
        ]
        + [WHOLE for one in first[2:]]
        + [FAR for one in earlier],
        out_specs=[
            pl.BlockSpec((features, LANES), lambda n: (0, n)),
            out_spec,
            pl.BlockSpec((8, LANES), lambda n: (0, 0)),
        ],
        out_shape=[kept_in((features, rows), bf16), out_shape, SIGN],
        scratch_shapes=[
            pltpu.VMEM((level_count * height, POOL * LANES), bf16),
            pltpu.VMEM((POOL, width, LANES), f32),
            pltpu.VMEM((width * part, POOL * LANES), f32),
            pltpu.VMEM((features, LANES), f32),
        ]
        + more,
        compiler_params=pltpu.CompilerParams(vmem_limit_bytes=24 * 2**20),
        cost_estimate=LARGE_COST,
        name="crop_block",
    )(*first, *earlier)


def multiply_kernel(rows_ref, weight_ref, out_ref, sign_ref):
    out_ref[...] = jnp.dot(rows_ref[...], weight_ref[...], preferred_element_type=f32).astype(bf16)
    sign_ref[...] = jnp.zeros_like(sign_ref)


def multiply(rows, weight):
    return pl.pallas_call(
        multiply_kernel,
        in_specs=[WHOLE, WHOLE],
        out_specs=[WHOLE, WHOLE],
        out_shape=[like((rows.shape[0], weight.shape[1]), bf16), SIGN],
        compiler_params=pltpu.CompilerParams(vmem_limit_bytes=24 * 2**20),
        cost_estimate=LARGE_COST,
        name="multiply",
    )(rows, weight)


def spread_block(table, sizes, boxes, grads, weight, earlier=()):
    height, width, part, level_count = sizes
    images = boxes.shape[0]
    features = weight.shape[0]
    return pl.pallas_call(
        functools.partial(spread_kernel, table, sizes),
        in_specs=[WHOLE, WHOLE, WHOLE] + [FAR for one in earlier],
        out_specs=[WHOLE, WHOLE],
        out_shape=[like((images, width * part, level_count * height), bf16), SIGN],
        scratch_shapes=[
            pltpu.VMEM((images, level_count * height, POOL * LANES), bf16),
            pltpu.VMEM((images, POOL, width, LANES), f32),
            pltpu.VMEM((width * part, POOL * LANES), bf16),
            pltpu.VMEM((features, LANES), f32),
            pltpu.VMEM((features, images * LANES), bf16),
        ],
        compiler_params=pltpu.CompilerParams(vmem_limit_bytes=24 * 2**20),
        cost_estimate=LARGE_COST,
        name="spread_block",
    )(boxes, grads, weight, *earlier)


def call(kernel, outs, scalars, arrays, earlier=(), scratch=(), name=None):
    arrays = list(arrays)

    def body(*refs):
        at, end = len(scalars), len(scalars) + len(arrays)
        later = refs[end + len(earlier) :]
        later[len(outs)][...] = jnp.zeros(SIGN.shape, SIGN.dtype)
        kernel(refs[:at], refs[at:end], (*later[: len(outs)], *later[len(outs) + 1 :]))

    return pl.pallas_call(
        body,
        in_specs=[SCALAR for one in scalars] + [WHOLE for one in arrays] + [FAR for one in earlier],
        out_specs=[WHOLE for one in (*outs, SIGN)],
        out_shape=[*outs, SIGN],
        scratch_shapes=scratch,
        compiler_params=pltpu.CompilerParams(vmem_limit_bytes=24 * 2**20),
        cost_estimate=LARGE_COST,
        name=name,
    )(*[jnp.full((1,), one, jnp.int32) for one in scalars], *arrays, *earlier)


def tie_kernel(*refs):
    pass


def tie(arrays, *earlier):
    return pl.pallas_call(
        tie_kernel,
        in_specs=[FAR for one in (*arrays, *earlier)],
        out_specs=[FAR for one in arrays],
        out_shape=[like(one.shape, one.dtype) for one in arrays],
        input_output_aliases={k: k for k in range(len(arrays))},
        compiler_params=pltpu.CompilerParams(vmem_limit_bytes=2**20),
        cost_estimate=SMALL_COST,
        name="tie",
    )(*arrays, *earlier)


def order_kernel(scalars, arrays, outs):
    for k, ref in enumerate(arrays):
        outs[0][scalars[0][0] ^ k] = ref[...]


def in_order(at, arrays, earlier):
    shape = (len(arrays),) + arrays[0].shape
    return call(order_kernel, [like(shape, arrays[0].dtype)], [at], arrays, earlier, name="in_order")[0]


def full_small_kernel(rows, scalars, arrays, outs):
    units = outs[0].shape[1]
    for k, ref in enumerate(arrays):
        core = scalars[0][0] ^ k
        for chip in range(4):
            for level in range(ref.shape[2]):
                at = pl.multiple_of(((level * 4 + chip) * 2 + core) * rows, rows)
                outs[0][pl.ds(at, rows), :] = ref[chip // 2, chip % 2, level, :rows, :]
                for part in range(2):
                    outs[1][pl.ds(at + part * (rows // 2), rows // 2), :] = ref[
                        chip // 2, chip % 2, level, rows:, part * (units // 2) : (part + 1) * (units // 2)
                    ]


def split_rows(core, array, rows, sent, kept):
    for at in range(array.shape[0] // rows // 2):
        mine = pl.multiple_of((2 * at + core) * rows, rows)
        other = pl.multiple_of((2 * at + 1 - core) * rows, rows)
        kept[at * rows : (at + 1) * rows, :] = array[pl.ds(mine, rows), :].astype(bf16)
        sent[at * rows : (at + 1) * rows, :] = array[pl.ds(other, rows), :].astype(bf16)


def put_biases(biases, refs):
    high = biases.astype(bf16)
    low = (biases - high.astype(f32)).astype(bf16)
    for ref in refs:
        end = ref.shape[0]
        ref[end - 16 : end - 8, : high.shape[1]] = high
        ref[end - 8 : end, : high.shape[1]] = low


def get_biases(ref, units):
    end = ref.shape[0]
    last = ref[end - 16 :, :units].astype(f32)
    return last[:8] + last[8:]


def small_product_kernel(rows, core_ref, first_ref, second_grad_ref, second_ref, slopes_ref, bias_ref, sent_ref, kept_ref, sign_ref, total_ref):
    turned = (((0,), (0,)), ((), ()))
    units = first_ref.shape[1]
    total_ref[:, :units] = lax.dot_general(
        first_ref[...], second_grad_ref[...], turned, preferred_element_type=f32
    )
    total_ref[:, units:] = lax.dot_general(
        second_ref[...], slopes_ref[...], turned, preferred_element_type=f32
    )
    split_rows(core_ref[0], total_ref, rows, sent_ref, kept_ref)
    put_biases(bias_ref[...], [sent_ref, kept_ref])
    sign_ref[...] = jnp.zeros_like(sign_ref)


def small_product(core, rows, first_act, second_grad, second_act, slopes, biases):
    units = first_act.shape[1]
    wide = units + slopes.shape[1]
    half = like((units // 2 + 16, wide), bf16)
    return pl.pallas_call(
        functools.partial(small_product_kernel, rows),
        in_specs=[SCALAR] + [WHOLE] * 5,
        out_specs=[WHOLE] * 3,
        out_shape=[half, half, SIGN],
        scratch_shapes=[pltpu.VMEM((units, wide), f32)],
        compiler_params=pltpu.CompilerParams(vmem_limit_bytes=24 * 2**20),
        cost_estimate=LARGE_COST,
        name="small_product",
    )(jnp.full((1,), core, jnp.int32), first_act, second_grad, second_act, slopes, biases)


def fold_kernel(rows, chip_ref, kept_ref, come_ref, *refs):
    outs, sign_ref, total_ref = refs[-6:-2], refs[-2], refs[-1]
    sign_ref[...] = jnp.zeros_like(sign_ref)
    count, units = total_ref.shape[0], total_ref.shape[1] // 3 * 2
    total_ref[...] = kept_ref[:count, :].astype(f32) + come_ref[:count, :].astype(f32)
    for k, out in enumerate(outs):
        for at in range(count // rows // 4):
            first = pl.multiple_of((4 * at + (chip_ref[0] ^ k)) * rows, rows)
            out[at * rows : (at + 1) * rows, :] = total_ref[pl.ds(first, rows), :].astype(bf16)
    put_biases(get_biases(kept_ref, units) + get_biases(come_ref, units), outs)


def fold_rows(chip, rows, kept, come, earlier):
    count = kept.shape[0] - 16
    quarter = like((count // 4 + 16, kept.shape[1]), bf16)
    return pl.pallas_call(
        functools.partial(fold_kernel, rows),
        in_specs=[SCALAR, WHOLE, WHOLE] + [FAR for one in earlier],
        out_specs=[WHOLE] * 5,
        out_shape=[quarter] * 4 + [SIGN],
        scratch_shapes=[pltpu.VMEM((count, kept.shape[1]), f32)],
        compiler_params=pltpu.CompilerParams(vmem_limit_bytes=24 * 2**20),
        cost_estimate=LARGE_COST,
        name="fold_rows",
    )(jnp.full((1,), chip, jnp.int32), kept, come, *earlier)


def last_fold_kernel(rows, scalars, arrays, outs):
    units = outs[0].shape[2]
    biases = [get_biases(ref, units) for ref in arrays]
    biases = (biases[0] + biases[1]) + (biases[2] + biases[3])
    for place in range(outs[0].shape[0]):
        at = slice(place * rows, (place + 1) * rows)
        total = sum(ref[at, :].astype(f32) for ref in arrays).astype(bf16)
        out = outs[0].at[place]
        out[:rows, :] = total[:, :units]
        for part in range(2):
            out[rows : rows // 2 * 3, part * (units // 2) : (part + 1) * (units // 2)] = total[
                part * (rows // 2) : (part + 1) * (rows // 2), units:
            ]
        put_biases(biases, [out])


def small_sum_kernel(scalars, arrays, outs):
    came_ref = arrays[0]
    count = came_ref.shape[0]
    total = sum(came_ref[place].astype(f32) for place in range(count))
    rows, units = outs[0].shape
    outs[0][...] = total[:rows]
    outs[3][...] = sum(get_biases(came_ref.at[place], units) for place in range(count))
    for part in range(2):
        at = slice(part * (rows // 2), (part + 1) * (rows // 2))
        beside = total[rows : rows // 2 * 3, part * (units // 2) : (part + 1) * (units // 2)]
        outs[1][at, :] = beside[:, :CLS]
        outs[2][at, :] = beside[:, LANES : LANES + BOX]


def gelu_and_slope(values):
    normal = 0.5 * (1.0 + lax.erf(values * np.float32(np.sqrt(0.5))))
    density = jnp.exp(-0.5 * values * values) * np.float32(1.0 / np.sqrt(2.0 * np.pi))
    return values * normal, normal + values * density


def head_kernel(
    own_ref, one_ref, two_ref, three_ref, labels_ref, ignore_ref, targets_ref, hidden_bias_ref, inner_ref, inner_bias_ref, heads_ref, heads_bias_ref,
    logits_ref, deltas_ref, first_act_ref, second_act_ref, slopes_ref, second_grad_ref, first_grad_ref, again_ref, bias_ref, first_slope_ref, second_slope_ref,
):
    first_pre = own_ref[...] + hidden_bias_ref[...]
    for come_ref in (one_ref, two_ref, three_ref):
        first_pre = first_pre + come_ref[...].astype(f32)
    act, slope = gelu_and_slope(first_pre)
    first_slope_ref[...] = slope
    act = act.astype(bf16)
    first_act_ref[...] = act
    second_pre = jnp.dot(act, inner_ref[...], preferred_element_type=f32) + inner_bias_ref[...]
    act, slope = gelu_and_slope(second_pre)
    second_slope_ref[...] = slope
    act = act.astype(bf16)
    second_act_ref[...] = act
    heads = jnp.dot(act, heads_ref[...], preferred_element_type=f32) + heads_bias_ref[...]
    logits, deltas = heads[:, :LANES], heads[:, LANES:]
    facts = []
    for n in range(labels_ref.shape[0]):
        rows = slice(n * LANES, (n + 1) * LANES)
        logits_ref[:, n, :] = logits[rows].T[:CLS]
        deltas_ref[n] = deltas[rows].T[:BOX]
        fact = [labels_ref[n : n + 1, :].astype(f32), ignore_ref[n : n + 1, :].astype(f32)]
        fact += [targets_ref[n], jnp.zeros((2, LANES), f32)]
        facts.append(jnp.concatenate(fact, axis=0).T)
    facts = jnp.concatenate(facts, axis=0)
    label = facts[:, 0:1]
    kept = 1.0 - facts[:, 1:2]
    column = lax.broadcasted_iota(jnp.int32, logits.shape, 1)
    valid = column < CLS
    row_max = jnp.max(jnp.where(valid, logits, -jnp.inf), axis=1, keepdims=True)
    exponent = jnp.where(valid, jnp.exp(jnp.where(valid, logits - row_max, 0.0)), 0.0)
    softmax_rows = exponent / jnp.sum(exponent, axis=1, keepdims=True)
    hot = (column.astype(f32) == label).astype(f32)
    logit_slope = (softmax_rows - hot) * (kept * np.float32(1.0 / RPI))
    column = lax.broadcasted_iota(jnp.int32, deltas.shape, 1)
    target = facts[:, 2:3]
    for j in range(1, 4):
        target = jnp.where((column & 3) == j, facts[:, 2 + j : 3 + j], target)
    foreground = jnp.where(label < CLS - 1, kept, 0.0)
    hot = ((column >> 2).astype(f32) == label) & (column < BOX)
    delta_slope = jnp.where(
        hot,
        jnp.clip(deltas - target, -1.0, 1.0) * (foreground * np.float32(1.0 / RPI)),
        0.0,
    )
    slopes = jnp.concatenate([logit_slope, delta_slope], axis=1).astype(bf16)
    slopes_ref[...] = slopes
    turned = (((1,), (1,)), ((), ()))
    act_grad = lax.dot_general(slopes, heads_ref[...], turned, preferred_element_type=f32)
    second_grad = (act_grad * second_slope_ref[...]).astype(bf16)
    second_grad_ref[...] = second_grad
    act_grad = lax.dot_general(second_grad, inner_ref[...], turned, preferred_element_type=f32)
    first_grad = (act_grad * first_slope_ref[...]).astype(bf16)
    first_grad_ref[...] = first_grad
    again_ref[...] = first_grad
    units = first_grad.shape[1]
    bias_ref[...] = jnp.zeros_like(bias_ref)
    bias_ref[0:1, :] = jnp.sum(first_grad.astype(f32), axis=0, keepdims=True)
    bias_ref[1:2, :] = jnp.sum(second_grad.astype(f32), axis=0, keepdims=True)
    bias_ref[2:3, : slopes.shape[1]] = jnp.sum(slopes.astype(f32), axis=0, keepdims=True)


def head_block(own, come, labels, ignore, targets, hidden_bias, inner, inner_bias, heads, heads_bias):
    count, units = own.shape
    wide = heads.shape[1]
    images = labels.shape[0]
    return pl.pallas_call(
        head_kernel,
        in_specs=[pl.BlockSpec(memory_space=pltpu.VMEM)] * 12,
        out_specs=[pl.BlockSpec(memory_space=pltpu.VMEM)] * 9,
        out_shape=[
            like((CLS, images, LANES), f32),
            like((images, BOX, LANES), f32),
            like((count, units), bf16),
            like((count, units), bf16),
            like((count, wide), bf16),
            like((count, units), bf16),
            like((count, units), bf16),
            like((count, units), bf16),
            like((8, units), f32),
        ],
        scratch_shapes=[pltpu.VMEM((count, units), f32)] * 2,
        compiler_params=pltpu.CompilerParams(vmem_limit_bytes=24 * 2**20),
        cost_estimate=LARGE_COST,
        name="head_block",
    )(own, *come, labels, ignore, targets, hidden_bias, inner, inner_bias, heads, heads_bias)


def maps_kernel(scalars, arrays, outs):
    maps_ref, by_class_ref, across_first_ref = arrays
    pick_ref = outs[-1]
    size, part = by_class_ref.shape[:2]
    images = maps_ref.shape[0]
    for way in range(size):
        pick_ref[way * part : (way + 1) * part, :] = by_class_ref[scalars[0][0] ^ way]
    for n in range(images):
        flat = lax.dot_general(
            pick_ref[...], maps_ref[n], (((1,), (1,)), ((), ())), preferred_element_type=f32
        ).astype(bf16)
        flat = jnp.dot(flat, across_first_ref[...], preferred_element_type=f32).astype(bf16)
        for way in range(size):
            outs[way][n * part : (n + 1) * part, :] = flat[way * part : (way + 1) * part]


def maps_back_kernel(scalars, arrays, outs):
    came_ref, by_class_ref, across_first_ref = arrays
    out_ref, pick_ref, flat_ref = outs
    size, part = by_class_ref.shape[:2]
    for way in range(size):
        pick_ref[way * part : (way + 1) * part, :] = by_class_ref[scalars[0][0] ^ way]
    for n in range(out_ref.shape[0]):
        for way in range(size):
            flat_ref[way * part : (way + 1) * part, :] = came_ref[scalars[0][0] ^ way, n]
        cells = lax.dot_general(
            across_first_ref[...], flat_ref[...], (((1,), (1,)), ((), ())), preferred_element_type=f32
        ).astype(bf16)
        out_ref[n] = jnp.dot(cells, pick_ref[...], preferred_element_type=f32)


def arrange_kernel(sizes, scalars, arrays, outs):
    height, width, part, level_count = sizes
    for n in range(outs[0].shape[0]):
        for x in range(width):
            for k, ref in enumerate(arrays):
                outs[0][n, x * part : (x + 1) * part, k * height : (k + 1) * height] = ref[
                    n * part : (n + 1) * part, x * height : (x + 1) * height
                ]


def arrange_back_kernel(sizes, scalars, arrays, outs):
    height, width, part, level_count = sizes
    for n in range(arrays[0].shape[0]):
        for x in range(width):
            for k in range(level_count):
                outs[0][scalars[0][0] ^ k, n, :, x * height : (x + 1) * height] = sum(
                    ref[n, x * part : (x + 1) * part, k * height : (k + 1) * height].astype(f32)
                    for ref in arrays
                ).astype(bf16)


def split_span_kernel(scalars, arrays, outs):
    total_ref = outs[-1]
    span = outs[0].shape[0]
    total_ref[...] = sum(
        jnp.dot(arrays[k][...], arrays[k + 1][...], preferred_element_type=f32)
        for k in range(0, len(arrays), 2)
    )
    for way, out in enumerate(outs[:-1]):
        at = pl.multiple_of((scalars[0][0] ^ way) * span, 8)
        out[...] = total_ref[pl.ds(at, span), :].astype(bf16)


def join_span_kernel(scalars, arrays, outs):
    total_ref = outs[-1]
    span = arrays[1].shape[0]
    for way, ref in enumerate(arrays[1:]):
        at = pl.multiple_of((scalars[0][0] ^ way) * span, 8)
        total_ref[pl.ds(at, span), :] = ref[...].astype(f32)
    product = jnp.dot(arrays[0][...], total_ref[...].astype(bf16), preferred_element_type=f32)
    for out in outs[:-1]:
        out[...] = product.astype(out.dtype)


def return_span_kernel(scalars, arrays, outs):
    total_ref = outs[-1]
    span = outs[0].shape[0]
    piece = sum(ref[...].astype(f32) for ref in arrays[1:]).astype(bf16)
    total_ref[...] = jnp.dot(arrays[0][...], piece, preferred_element_type=f32)
    for way, out in enumerate(outs[:-1]):
        at = pl.multiple_of((scalars[0][0] ^ way) * span, 8)
        out[...] = total_ref[pl.ds(at, span), :].astype(bf16)


def picking(rows, columns, pairs):
    matrix = np.zeros((rows, columns), np.float32)
    for a, b in pairs:
        matrix[a, b] = 1.0
    return jnp.asarray(matrix, bf16)


def swap(array, axis, bit):
    size = lax.axis_size(axis)
    return lax.ppermute(array, axis, [(at, at ^ bit) for at in range(size)])


def exchange(array, axis):
    return lax.all_to_all(array, axis, split_axis=0, concat_axis=0, tiled=True)


def exchange_ways(arrays, axis):
    return [arrays[0]] + [swap(one, axis, way) for way, one in enumerate(arrays) if way]


def product_kernel(number, parts, with_sum, at_ref, *refs):
    grad_refs, crop_refs, refs = refs[:parts], refs[parts : 2 * parts], refs[2 * parts :]
    sign_ref, refs = refs[-1], refs[:-1]
    sign_ref[...] = jnp.zeros_like(sign_ref)
    outs = refs[-number:] if with_sum else [refs[-1].at[n] for n in range(number)]
    rows = crop_refs[0].shape[0] // 8
    for n in range(number):
        total = refs[0][n].astype(f32) if with_sum else 0.0
        at = pl.multiple_of(at_ref[n] * rows, 16)
        for grad_ref, crop_ref in zip(grad_refs, crop_refs):
            total = total + jnp.dot(
                crop_ref[pl.ds(at, rows), :], grad_ref[...], preferred_element_type=f32
            )
        outs[n][...] = total.astype(bf16)


def piece_product(crops, grads, pieces, come, earlier):
    features = crops[0].shape[0]
    units = grads[0].shape[1]
    rows = features // 8
    number = len(pieces)
    with_sum = come is not None
    come = [come] if with_sum else []
    outs = (
        [like((rows, units), bf16)] * number if with_sum else [like((number, rows, units), bf16)]
    )
    return pl.pallas_call(
        functools.partial(product_kernel, number, len(grads), with_sum),
        in_specs=[SCALAR]
        + [WHOLE for one in (*grads, *crops, *come)]
        + [FAR for one in earlier],
        out_specs=[WHOLE for one in (*outs, SIGN)],
        out_shape=[*outs, SIGN],
        compiler_params=pltpu.CompilerParams(vmem_limit_bytes=24 * 2**20),
        cost_estimate=LARGE_COST,
        name="piece_product",
    )(jnp.stack(pieces), *grads, *crops, *come, *earlier)


def butterfly(array):
    for axis in ("img", "level"):
        bit = 1
        while bit < lax.axis_size(axis):
            array = array + swap(array, axis, bit)
            bit *= 2
    return array


def contract_rows(left_side, right_side):
    return lax.dot_general(
        left_side, right_side, (((0,), (0,)), ((), ())), preferred_element_type=f32
    )


def pack_rows(array):
    rows, units = array.shape[-2], array.shape[-1] // 3 * 2
    beside = array[..., units:]
    below = jnp.concatenate([beside[..., : rows // 2, :], beside[..., rows // 2 :, :]], axis=-1)
    return jnp.concatenate([array[..., :units], below], axis=-2)


def per_device(
    pyramid,
    levels,
    region_boxes,
    labels,
    crowd_ignore,
    targets,
    hidden_weight,
    hidden_bias,
    inner_weight,
    inner_bias,
    class_weight,
    class_bias,
    delta_weight,
    delta_bias,
):
    size = lax.axis_size("level")
    planes = lax.axis_size("img")
    z = lax.axis_index("level")
    place = lax.axis_index("img")
    core, x, y = place % 2, place // 2 % 2, place // 4
    images, height, width, channels = pyramid.shape[1:]
    regions = levels.shape[1]
    part = channels // size
    sizes = (height, width, part, size)
    rows, units = hidden_weight.shape
    block_rows = images * regions
    direct = planes == 8 and rows % size == 0

    packed = jnp.concatenate(
        [
            jnp.transpose(region_boxes, (0, 2, 1)),
            jnp.transpose(levels, (0, 2, 1)),
            jnp.zeros((images, 3, regions), jnp.int32),
        ],
        axis=1,
    )
    class_room, delta_room = LANES, units // 2 - LANES
    small = jnp.concatenate(
        [
            inner_weight,
            jnp.pad(class_weight, ((0, 0), (0, class_room - CLS))),
            jnp.pad(delta_weight, ((0, 0), (0, delta_room - BOX))),
        ],
        axis=1,
    )
    heads_bias = jnp.concatenate(
        [
            jnp.pad(class_bias, (0, class_room - CLS)),
            jnp.pad(delta_bias, (0, delta_room - BOX)),
        ]
    )[None]

    if direct:
        length = rows // size
        span = -(-(length + images) // 8) * 8
        extra = jnp.concatenate(
            [packed.astype(bf16).reshape(images, units), jnp.zeros((16 - images, units), bf16)]
        )
        to_span = picking(
            size * span,
            rows,
            [(k * span + j, j * size + k) for k in range(size) for j in range(length)],
        )
        extra_span = picking(
            size * span,
            16,
            [(k * span + length + n, n) for k in range(size) for n in range(images)],
        )
        room = -(-rows // 16) * 16
        features = planes * room
        from_span = picking(
            room,
            size * span,
            [(k * length + j, k * span + j) for k in range(size) for j in range(length)],
        )
        total = [pltpu.VMEM((size * span, units), f32)]
        *sent, sign = call(
            split_span_kernel,
            [like((span, units), bf16)] * size,
            [z],
            [to_span, hidden_weight, extra_span, extra],
            scratch=total,
            name="split_span",
        )
        came = exchange_ways(sent, "level")
        piece, own_piece, sign = call(
            join_span_kernel,
            [like((room, units), bf16)] * 2,
            [z],
            [from_span, *came],
            scratch=total,
            name="join_span",
        )
        boxes = jnp.stack([one[length : length + images].reshape(images, 8, regions) for one in came])
        pieces = [own_piece] + [swap(piece, "img", bit) for bit in (2, 4, 6)]
        order = [k * planes + at for at in range(planes) for k in range(size)]
        table = runs_of(order, length, part, size, room)
    else:
        boxes = exchange(jnp.broadcast_to(packed[None], (size,) + packed.shape), "level")
        boxes = jnp.stack([lax.dynamic_index_in_dim(boxes, z ^ way, 0, False) for way in range(size)])
        features = BINS * part
        whole = lax.all_gather(hidden_weight, AXES, axis=0, tiled=True)
        weight = lax.dynamic_index_in_dim(whole.reshape(features, size, units), z, 1, False)
        table = runs_of([0], features, part, 1, features)
    row = jnp.arange(8)[:, None]
    boxes = jnp.where(row == 4, boxes.astype(jnp.int32) ^ z, boxes.astype(jnp.int32)).astype(f32)

    spots = height * width
    by_class = picking(
        channels, channels, [(c % size * part + c // size, c) for c in range(channels)]
    ).reshape(size, part, channels)
    across_first = picking(
        spots, spots, [(y * width + x, x * height + y) for y in range(height) for x in range(width)]
    )
    picks = [
        pltpu.VMEM((channels, channels), bf16),
        pltpu.VMEM((channels, spots), bf16),
    ]
    small_rows = small.shape[0] // 2 * 3
    maps = call(
        maps_kernel,
        [like((images * part, spots), bf16)] * size,
        [z],
        [pyramid[0].reshape(images, spots, channels), by_class, across_first],
        scratch=picks[:1],
        name="maps",
    )[:size]
    if direct:
        maps = [maps[0], *tie(maps[1:], sign)]
    maps_came = exchange_ways(maps[:3], "level")
    maps_came.append(swap(tie([maps[3]], maps_came[1])[0], "level", 3))
    maps, sign = call(
        functools.partial(arrange_kernel, sizes),
        [pltpu.VMEM((images, width * part, size * height), bf16)],
        [],
        maps_came,
        name="arrange",
    )

    ways = (2, 3, 1, 0)
    crops, owns, signs, came_sums = [], [], [], []
    crops_in = pltpu.VMEM if direct else like
    for turn, way in enumerate(ways):
        if turn == 0:
            crop, turned, sign = crop_block(
                table, sizes, features, boxes[way], maps, kept_in=crops_in
            )
            if direct:
                own_piece, smalls = tie([own_piece, pack_rows(small)], sign)
                smalls = exchange_ways([smalls] * size, "level")
                pieces = [own_piece, *pieces[1:]]
                pieces = sum(([one, swap(one, "img", 1)] for one in pieces), [])
                weight = gather_pieces(jnp.full((1,), place, jnp.int32), pieces)
            own, sign = multiply(turned, weight)
        else:
            crop, own, sign = crop_block(
                table, sizes, features, boxes[way], maps, weight, bf16 if way else f32, signs[-1:], crops_in
            )
        owns.append(own)
        signs.append(sign)
        crops.append(crop)
        if way:
            came_sums.append(swap(owns[-1], "level", way))

    if direct:
        smalls = in_order(z, smalls, signs[:1])
        smalls = in_order(x, [smalls, swap(smalls, "img", 2)], signs[1:2])
        smalls = in_order(y, [smalls, swap(smalls, "img", 4)], signs[2:3])
        full_inner, full_heads, sign = call(
            functools.partial(full_small_kernel, small.shape[0]),
            [pltpu.VMEM((units, units), bf16), pltpu.VMEM((units, units // 2), bf16)],
            [core],
            [smalls, swap(smalls, "img", 1)],
            name="full_small",
        )
    else:
        smalls = lax.all_gather(small, AXES, axis=0, tiled=True)
        full_inner, full_heads = smalls[:, :units], smalls[:, units:]

    logits, deltas, first_act, second_act, slopes, second_grad, first_grad, first_again, bias_sums = head_block(
        owns[-1],
        came_sums,
        labels,
        crowd_ignore,
        jnp.transpose(targets, (0, 2, 1)),
        hidden_bias[None],
        full_inner,
        inner_bias[None],
        full_heads,
        heads_bias,
    )

    near = swap(first_grad, "level", 1)
    far = swap(first_grad, "level", 2)
    grad_of = {0: first_grad, 1: near, 2: far}

    shares = []

    def take_up(way, earlier=()):
        share, sign = spread_block(table, sizes, boxes[way], grad_of[way], weight, earlier)
        shares.append(share)
        return sign

    if direct:
        count = small.shape[0]
        sent, kept, sign = small_product(
            core, count, first_act, second_grad, second_act, slopes, bias_sums
        )
        sign = take_up(0, [sign])
        *quarters, sign = fold_rows(place // 2, count, kept, swap(sent, "img", 1), [sign])
        quarters = [
            swap(one, "img", bit) if bit else one for one, bit in zip(quarters, (0, 2, 4, 6))
        ]
        grad_of[3] = swap(tie([first_again], far, sign)[0], "level", 3)
        sign = take_up(1, [sign])
        sign = take_up(2, [sign])

        grads = [grad_of[way] for way in ways]
        parts, others = {}, {}

        def for_other(bits, sign):
            at = [place ^ bit ^ 1 for bit in bits]
            products, sign = piece_product(crops, grads, at, None, [sign])
            others[bits] = swap(products, "img", 1)
            return sign

        def for_own(bits, sign):
            at = [place ^ bit for bit in bits]
            *own, sign = piece_product(crops, grads, at, others[bits], [sign])
            for one, bit in zip(own, bits):
                parts[bit] = swap(one, "img", bit) if bit else one
            return sign

        sign = for_other((6,), sign)
        sign = for_other((2, 4, 0), sign)
        sign = for_own((6,), sign)
        sign = for_own((2, 4, 0), sign)
        smalls, sign = call(
            functools.partial(last_fold_kernel, count),
            [like((size, small_rows + 16, units), bf16)],
            [z],
            quarters,
            [sign],
            name="last_fold",
        )
        sign = take_up(3, [sign])
        inner_sum, class_sum, delta_sum, bias_total, sign = call(
            small_sum_kernel,
            [
                like((count, units), f32),
                like((count, CLS), f32),
                like((count, BOX), f32),
                like((8, units), f32),
            ],
            [],
            [exchange(smalls, "level")],
            [sign],
            name="small_sum",
        )
        back, sign = call(
            functools.partial(arrange_back_kernel, sizes),
            [like((size, images, part, spots), bf16)],
            [z],
            shares,
            [sign],
            name="arrange_back",
        )
        *sent, sign = call(
            return_span_kernel,
            [like((span, units), bf16)] * size,
            [z],
            [from_span.T, *[parts[bit] for bit in (0, 2, 4, 6)]],
            [sign],
            scratch=total,
            name="return_span",
        )
    else:
        grad_of[3] = swap(first_again, "level", 3)
        for way in range(size):
            take_up(way)
        back, sign = call(
            functools.partial(arrange_back_kernel, sizes),
            [like((size, images, part, spots), bf16)],
            [z],
            shares,
            name="arrange_back",
        )
        bias_total = butterfly(bias_sums)
        small_sum = jnp.concatenate(
            [contract_rows(first_act, second_grad), contract_rows(second_act, slopes)], axis=1
        )
        small_sum = lax.psum_scatter(small_sum, AXES, scatter_dimension=0, tiled=True)
        inner_sum = small_sum[:, :units]
        class_sum = small_sum[:, units : units + CLS]
        delta_sum = small_sum[:, units + class_room : units + class_room + BOX]
        whole_grads = jnp.concatenate([grad_of[way] for way in ways])
        product = jnp.dot(
            jnp.concatenate(crops, axis=1), whole_grads, preferred_element_type=f32
        )
        own = (jnp.arange(size, dtype=jnp.int32) == z)[None, :, None]
        hidden_sum = lax.psum_scatter(
            jnp.where(own, product[:, None, :], 0.0).reshape(features * size, units),
            AXES,
            scatter_dimension=0,
            tiled=True,
        )

    map_grads, sign = call(
        maps_back_kernel,
        [like((images, spots, channels), f32)],
        [z],
        [exchange(back, "level"), by_class, across_first],
        [sign],
        scratch=picks,
        name="maps_back",
    )
    map_grads = map_grads.reshape(1, images, height, width, channels)

    if direct:
        hidden_sum = call(
            join_span_kernel,
            [like((rows, units), f32)],
            [z],
            [to_span.T, *exchange_ways(sent, "level")],
            [sign],
            scratch=total,
            name="join_span",
        )[0]

    head_bias = bias_total[2, : class_room + delta_room]
    return (
        jnp.transpose(logits, (1, 2, 0)),
        jnp.transpose(deltas, (0, 2, 1)),
        map_grads,
        hidden_sum,
        bias_total[0],
        inner_sum,
        bias_total[1],
        class_sum,
        head_bias[:CLS],
        delta_sum,
        head_bias[class_room : class_room + BOX],
    )


def solution(mesh):
    return jax.shard_map(
        per_device,
        mesh=mesh,
        in_specs=(
            P("level", "img", None, None, None),
            P("img", "level", None),
            P("img", "level", None),
            P("img", "level"),
            P("img", "level"),
            P("img", "level", None),
            P(AXES, None),
            P(),
            P(AXES, None),
            P(),
            P(AXES, None),
            P(),
            P(AXES, None),
            P(),
        ),
        out_specs=(
            P("img", "level", None),
            P("img", "level", None),
            P("level", "img", None, None, None),
            P(AXES, None),
            P(),
            P(AXES, None),
            P(),
            P(AXES, None),
            P(),
            P(AXES, None),
            P(),
        ),
        check_vma=False,
    )
```

```python
import functools

import jax
import jax.numpy as jnp
import numpy as np
from jax import lax
from jax.experimental import pallas as pl
from jax.experimental.pallas import tpu as pltpu
from jax.sharding import PartitionSpec as P

POOL = 7
SAMPLES = 2
CLS = 81
BOX = 320
RPI = 512
BINS = POOL * POOL
LANES = 128
AXES = ("level", "img")
OFFSETS = (np.arange(SAMPLES * POOL, dtype=np.float32) + np.float32(0.5)) / np.float32(
    SAMPLES * POOL
)
SMALL_COST = pl.CostEstimate(flops=10**9, bytes_accessed=1, transcendentals=0)
LARGE_COST = pl.CostEstimate(flops=4 * 10**10, bytes_accessed=1, transcendentals=0)
f32 = jnp.float32
bf16 = jnp.bfloat16
FAR = pl.BlockSpec(memory_space=pl.ANY)
WHOLE = pl.BlockSpec(memory_space=pltpu.VMEM)
SCALAR = pl.BlockSpec(memory_space=pltpu.SMEM)
like = jax.ShapeDtypeStruct
SIGN = jax.ShapeDtypeStruct((8, LANES), jnp.float32)


def bin_weights(low, span, centres, at):
    first = jnp.maximum(1.0 - jnp.abs((low + OFFSETS[2 * at] * span) - centres), 0.0)
    second = jnp.maximum(1.0 - jnp.abs((low + OFFSETS[2 * at + 1] * span) - centres), 0.0)
    return ((first + second) * 0.5).astype(bf16)


def fill_weights(box_ref, down_ref, across_ref, height, width, level_count):
    x0, y0, x1, y1, level = [box_ref[k : k + 1, :] for k in range(5)]
    centres = lax.broadcasted_iota(jnp.int32, (width, LANES), 0).astype(f32)
    for q in range(POOL):
        across_ref[q] = bin_weights(x0, x1 - x0, centres, q)
    centres = lax.broadcasted_iota(jnp.int32, (height, LANES), 0).astype(f32)
    for p in range(POOL):
        weights = bin_weights(y0, y1 - y0, centres, p).astype(f32)
        for k in range(level_count):
            down_ref[k * height : (k + 1) * height, p * LANES : (p + 1) * LANES] = jnp.where(
                level == float(k), weights, 0.0
            ).astype(bf16)


def runs_of(order, length, part, group, room):
    place = {chunk: at // group * room + at % group * length for at, chunk in enumerate(order)}
    table = []
    for at in range(BINS):
        row, end, runs = at * part, (at + 1) * part, []
        while row < end:
            chunk = row // length
            stop = min(end, (chunk + 1) * length)
            runs.append((row - at * part, place[chunk] + row - chunk * length, stop - row))
            row = stop
        table.append(runs)
    return table


def gaps_of(table, features):
    held = sorted((kept, kept + count) for runs in table for row, kept, count in runs)
    gaps, last = [], 0
    for first, end in held + [(features, features)]:
        if first > last:
            gaps.append((last, first))
        last = end
    return gaps


def gather_kernel(number, where_ref, *refs):
    kept_ref, sems = refs[-2:]
    rows = refs[0].shape[0]
    copies = []
    for k, ref in enumerate(refs[:number]):
        at = pl.multiple_of((where_ref[1] ^ k) * rows, 16)
        copies.append(pltpu.make_async_copy(ref, kept_ref.at[pl.ds(at, rows)], sems.at[k]))
    for copy in copies:
        copy.start()
    for copy in copies:
        copy.wait()


def gather_pieces(where, pieces):
    rows, units = pieces[0].shape
    number = len(pieces)
    return pl.pallas_call(
        functools.partial(gather_kernel, number),
        in_specs=[SCALAR] + [FAR for one in pieces],
        out_specs=WHOLE,
        out_shape=pltpu.VMEM((number * rows, units), bf16),
        scratch_shapes=[pltpu.SemaphoreType.DMA((number,))],
        compiler_params=pltpu.CompilerParams(vmem_limit_bytes=24 * 2**20),
        cost_estimate=LARGE_COST,
        name="gather_pieces",
    )(where, *pieces)


def crop_kernel(table, sizes, product, box_ref, maps_ref, *refs):
    if product:
        weight_ref = refs[0]
        crop_ref, out_ref, sign_ref, down_ref, across_ref, sums_ref, rows_ref, turned_ref = refs[-8:]
    else:
        crop_ref, out_ref, sign_ref, down_ref, across_ref, sums_ref, rows_ref = refs[-7:]
    sign_ref[...] = jnp.zeros_like(sign_ref)
    height, width, part, level_count = sizes
    for first, end in gaps_of(table, rows_ref.shape[0]):
        rows_ref[first:end, :] = jnp.zeros((end - first, LANES), f32)
    fill_weights(box_ref, down_ref, across_ref, height, width, level_count)
    sums_ref[...] = jnp.dot(maps_ref[...], down_ref[...], preferred_element_type=f32).astype(bf16)
    for p in range(POOL):
        lanes = slice(p * LANES, (p + 1) * LANES)
        for start in range(0, POOL, 2):
            bins = range(start, min(POOL, start + 2))
            totals = [None for q in bins]
            for x in range(width):
                piece = sums_ref[x * part : (x + 1) * part, lanes]
                for at, q in enumerate(bins):
                    term = across_ref[q, x : x + 1, :] * piece
                    totals[at] = term if x == 0 else totals[at] + term
            for at, q in enumerate(bins):
                for row, kept, count in table[p * POOL + q]:
                    rows_ref[kept : kept + count, :] = totals[at][row : row + count].astype(f32)
    crop = rows_ref[...].astype(bf16)
    crop_ref[...] = crop
    if not product:
        out_ref[...] = crop.T
        return
    turned_ref[pl.ds(pl.multiple_of(pl.program_id(0) * LANES, LANES), LANES), :] = crop.T

    @pl.when(pl.program_id(0) == pl.num_programs(0) - 1)
    def multiply():
        out_ref[...] = jnp.dot(
            turned_ref[...], weight_ref[...], preferred_element_type=f32
        ).astype(out_ref.dtype)


def spread_kernel(table, sizes, box_ref, grad_ref, weight_ref, *refs):
    total_ref, sign_ref, down_ref, across_ref, sums_ref, rows_ref, crop_ref = refs[-7:]
    sign_ref[...] = jnp.zeros_like(sign_ref)
    height, width, part, level_count = sizes
    images = box_ref.shape[0]
    for n in range(images):
        fill_weights(
            box_ref.at[n], down_ref.at[n], across_ref.at[n], height, width, level_count
        )
    crop_ref[...] = lax.dot_general(
        weight_ref[...], grad_ref[...], (((1,), (1,)), ((), ())), preferred_element_type=f32
    ).astype(bf16)
    for n in range(images):
        rows_ref[...] = crop_ref[:, n * LANES : (n + 1) * LANES].astype(f32)
        for p in range(POOL):
            lanes = slice(p * LANES, (p + 1) * LANES)
            pieces = []
            for q in range(POOL):
                runs = [rows_ref[kept : kept + count, :] for row, kept, count in table[p * POOL + q]]
                runs = runs[0] if len(runs) == 1 else jnp.concatenate(runs, axis=0)
                pieces.append(runs.astype(bf16))
            for x in range(width):
                total = across_ref[n, 0, x : x + 1, :] * pieces[0]
                for q in range(1, POOL):
                    total = total + across_ref[n, q, x : x + 1, :] * pieces[q]
                sums_ref[x * part : (x + 1) * part, lanes] = total
        total_ref[n] = lax.dot_general(
            sums_ref[...], down_ref[n], (((1,), (1,)), ((), ())), preferred_element_type=f32
        ).astype(bf16)


def crop_block(table, sizes, features, boxes, maps, weight=None, out_type=bf16, earlier=(), kept_in=like):
    height, width, part, level_count = sizes
    images = boxes.shape[0]
    product = weight is not None
    first = [boxes, maps] + ([weight] if product else [])
    rows = images * LANES
    if product:
        units = weight.shape[1]
        out_spec = pl.BlockSpec((rows, units), lambda n: (0, 0))
        out_shape = like((rows, units), out_type)
        more = [pltpu.VMEM((rows, features), bf16)]
    else:
        out_spec = pl.BlockSpec((LANES, features), lambda n: (n, 0))
        out_shape = kept_in((rows, features), bf16)
        more = []
    return pl.pallas_call(
        functools.partial(crop_kernel, table, sizes, product),
        grid=(images,),
        in_specs=[
            pl.BlockSpec((None, 8, LANES), lambda n: (n, 0, 0)),
            pl.BlockSpec((None, width * part, level_count * height), lambda n: (n, 0, 0)),
        ]
        + [WHOLE for one in first[2:]]
        + [FAR for one in earlier],
        out_specs=[
            pl.BlockSpec((features, LANES), lambda n: (0, n)),
            out_spec,
            pl.BlockSpec((8, LANES), lambda n: (0, 0)),
        ],
        out_shape=[kept_in((features, rows), bf16), out_shape, SIGN],
        scratch_shapes=[
            pltpu.VMEM((level_count * height, POOL * LANES), bf16),
            pltpu.VMEM((POOL, width, LANES), bf16),
            pltpu.VMEM((width * part, POOL * LANES), bf16),
            pltpu.VMEM((features, LANES), f32),
        ]
        + more,
        compiler_params=pltpu.CompilerParams(vmem_limit_bytes=24 * 2**20),
        cost_estimate=LARGE_COST,
        name="crop_block",
    )(*first, *earlier)


def multiply_kernel(rows_ref, weight_ref, out_ref, sign_ref):
    out_ref[...] = jnp.dot(rows_ref[...], weight_ref[...], preferred_element_type=f32).astype(bf16)
    sign_ref[...] = jnp.zeros_like(sign_ref)


def multiply(rows, weight):
    return pl.pallas_call(
        multiply_kernel,
        in_specs=[WHOLE, WHOLE],
        out_specs=[WHOLE, WHOLE],
        out_shape=[like((rows.shape[0], weight.shape[1]), bf16), SIGN],
        compiler_params=pltpu.CompilerParams(vmem_limit_bytes=24 * 2**20),
        cost_estimate=LARGE_COST,
        name="multiply",
    )(rows, weight)


def spread_block(table, sizes, boxes, grads, weight, earlier=()):
    height, width, part, level_count = sizes
    images = boxes.shape[0]
    features = weight.shape[0]
    return pl.pallas_call(
        functools.partial(spread_kernel, table, sizes),
        in_specs=[WHOLE, WHOLE, WHOLE] + [FAR for one in earlier],
        out_specs=[WHOLE, WHOLE],
        out_shape=[like((images, width * part, level_count * height), bf16), SIGN],
        scratch_shapes=[
            pltpu.VMEM((images, level_count * height, POOL * LANES), bf16),
            pltpu.VMEM((images, POOL, width, LANES), bf16),
            pltpu.VMEM((width * part, POOL * LANES), bf16),
            pltpu.VMEM((features, LANES), f32),
            pltpu.VMEM((features, images * LANES), bf16),
        ],
        compiler_params=pltpu.CompilerParams(vmem_limit_bytes=24 * 2**20),
        cost_estimate=LARGE_COST,
        name="spread_block",
    )(boxes, grads, weight, *earlier)


def call(kernel, outs, where, arrays, earlier=(), scratch=(), name=None):
    arrays = list(arrays)

    def body(*refs):
        end = 1 + len(arrays)
        later = refs[end + len(earlier) :]
        later[len(outs)][...] = jnp.zeros(SIGN.shape, SIGN.dtype)
        kernel(refs[0], refs[1:end], (*later[: len(outs)], *later[len(outs) + 1 :]))

    return pl.pallas_call(
        body,
        in_specs=[SCALAR] + [WHOLE for one in arrays] + [FAR for one in earlier],
        out_specs=[WHOLE for one in (*outs, SIGN)],
        out_shape=[*outs, SIGN],
        scratch_shapes=scratch,
        compiler_params=pltpu.CompilerParams(vmem_limit_bytes=24 * 2**20),
        cost_estimate=LARGE_COST,
        name=name,
    )(where, *arrays, *earlier)


def tie_kernel(*refs):
    pass


def tie(arrays, *earlier):
    return pl.pallas_call(
        tie_kernel,
        in_specs=[FAR for one in (*arrays, *earlier)],
        out_specs=[FAR for one in arrays],
        out_shape=[like(one.shape, one.dtype) for one in arrays],
        input_output_aliases={k: k for k in range(len(arrays))},
        compiler_params=pltpu.CompilerParams(vmem_limit_bytes=2**20),
        cost_estimate=SMALL_COST,
        name="tie",
    )(*arrays, *earlier)


def add_kernel(where, arrays, outs):
    outs[0][...] = sum(ref[...].astype(f32) for ref in arrays).astype(outs[0].dtype)


def pair_kernel(bit, where, arrays, outs):
    own = (where[bit[0]] >> bit[1]) & 1
    outs[0][own] = arrays[0][...]
    outs[0][1 - own] = arrays[1][...]


def pair_up(bit, where, own, earlier):
    come = swap(own, AXES[bit[0]], 1 << bit[1])
    out = like((2,) + own.shape, own.dtype)
    return call(functools.partial(pair_kernel, bit), [out], where, [own, come], earlier, name="pair_up")


def order_kernel(where, arrays, outs):
    for k, ref in enumerate(arrays):
        outs[0][(where[1] >> 1) ^ k] = ref[...]


def full_small_kernel(rows, where, arrays, outs):
    units = outs[0].shape[1]
    for k, ref in enumerate(arrays):
        core = (where[1] & 1) ^ k
        for chip in range(4):
            for level in range(ref.shape[1]):
                at = pl.multiple_of(((level * 4 + chip) * 2 + core) * rows, rows)
                outs[0][pl.ds(at, rows), :] = ref[chip, level, :rows, :]
                for part in range(2):
                    outs[1][pl.ds(at + part * (rows // 2), rows // 2), :] = ref[
                        chip, level, rows:, part * (units // 2) : (part + 1) * (units // 2)
                    ]


def split_rows(own, inner, array, rows, sent, kept):
    step = inner * rows
    for at in range((kept.shape[0] - 16) // step):
        mine = pl.multiple_of((2 * at + own) * step, rows)
        other = pl.multiple_of((2 * at + 1 - own) * step, rows)
        kept[at * step : (at + 1) * step, :] = array[pl.ds(mine, step), :].astype(bf16)
        sent[at * step : (at + 1) * step, :] = array[pl.ds(other, step), :].astype(bf16)


def put_biases(biases, refs):
    high = biases.astype(bf16)
    low = (biases - high.astype(f32)).astype(bf16)
    for ref in refs:
        end = ref.shape[0]
        ref[end - 16 : end - 8, : high.shape[1]] = high
        ref[end - 8 : end, : high.shape[1]] = low


def get_biases(ref, units):
    end = ref.shape[0]
    last = ref[end - 16 :, :units].astype(f32)
    return last[:8] + last[8:]


def small_product_kernel(rows, where_ref, first_ref, second_grad_ref, second_ref, slopes_ref, bias_ref, sent_ref, kept_ref, sign_ref, total_ref):
    turned = (((0,), (0,)), ((), ()))
    units = first_ref.shape[1]
    total_ref[:, :units] = lax.dot_general(
        first_ref[...], second_grad_ref[...], turned, preferred_element_type=f32
    )
    total_ref[:, units:] = lax.dot_general(
        second_ref[...], slopes_ref[...], turned, preferred_element_type=f32
    )
    split_rows(where_ref[1] & 1, 1, total_ref, rows, sent_ref, kept_ref)
    put_biases(bias_ref[...], [sent_ref, kept_ref])
    sign_ref[...] = jnp.zeros_like(sign_ref)


def small_product(where, rows, first_act, second_grad, second_act, slopes, biases):
    units = first_act.shape[1]
    wide = units + slopes.shape[1]
    half = like((units // 2 + 16, wide), bf16)
    return pl.pallas_call(
        functools.partial(small_product_kernel, rows),
        in_specs=[SCALAR] + [WHOLE] * 5,
        out_specs=[WHOLE] * 3,
        out_shape=[half, half, SIGN],
        scratch_shapes=[pltpu.VMEM((units, wide), f32)],
        compiler_params=pltpu.CompilerParams(vmem_limit_bytes=24 * 2**20),
        cost_estimate=LARGE_COST,
        name="small_product",
    )(where, first_act, second_grad, second_act, slopes, biases)


def quarter_kernel(rows, where_ref, kept_ref, come_ref, *refs):
    outs, sign_ref, total_ref = refs[-6:-2], refs[-2], refs[-1]
    sign_ref[...] = jnp.zeros_like(sign_ref)
    count, units = total_ref.shape[0], total_ref.shape[1] // 3 * 2
    total_ref[...] = kept_ref[:count, :].astype(f32) + come_ref[:count, :].astype(f32)
    for k, out in enumerate(outs):
        for at in range(count // rows // 4):
            first = pl.multiple_of((4 * at + ((where_ref[1] >> 1) ^ k)) * rows, rows)
            out[at * rows : (at + 1) * rows, :] = total_ref[pl.ds(first, rows), :].astype(bf16)
    put_biases(get_biases(kept_ref, units) + get_biases(come_ref, units), outs)


def quarter_rows(rows, where, kept, come, earlier):
    count = kept.shape[0] - 16
    quarter = like((count // 4 + 16, kept.shape[1]), bf16)
    return pl.pallas_call(
        functools.partial(quarter_kernel, rows),
        in_specs=[SCALAR, WHOLE, WHOLE] + [FAR for one in earlier],
        out_specs=[WHOLE] * 5,
        out_shape=[quarter] * 4 + [SIGN],
        scratch_shapes=[pltpu.VMEM((count, kept.shape[1]), f32)],
        compiler_params=pltpu.CompilerParams(vmem_limit_bytes=24 * 2**20),
        cost_estimate=LARGE_COST,
        name="quarter_rows",
    )(where, kept, come, *earlier)


def halve_kernel(bit, inner, rows, where, arrays, outs):
    sent_out, kept_out, total_ref = outs
    count, units = total_ref.shape[0], total_ref.shape[1] // 3 * 2
    total_ref[...] = sum(ref[:count, :].astype(f32) for ref in arrays)
    split_rows((where[bit[0]] >> bit[1]) & 1, inner, total_ref, rows, sent_out, kept_out)
    biases = [get_biases(ref, units) for ref in arrays]
    while len(biases) > 1:
        biases = [biases[k] + biases[k + 1] for k in range(0, len(biases), 2)]
    put_biases(biases[0], [sent_out, kept_out])


def halve_rows(bit, inner, rows, where, arrays, earlier):
    count, wide = arrays[0].shape[0] - 16, arrays[0].shape[1]
    return call(
        functools.partial(halve_kernel, bit, inner, rows),
        [like((count // 2 + 16, wide), bf16)] * 2,
        where,
        arrays,
        earlier,
        [pltpu.VMEM((count, wide), f32)],
        name="halve_rows",
    )


def small_sum_kernel(where, arrays, outs):
    rows, units = outs[0].shape
    total = sum(ref[:rows, :].astype(f32) for ref in arrays)
    outs[0][...] = total[:, :units]
    outs[1][...] = total[:, units : units + CLS]
    outs[2][...] = total[:, units + LANES : units + LANES + BOX]
    outs[3][...] = sum(get_biases(ref, units) for ref in arrays)


def gelu_and_slope(values):
    normal = 0.5 * (1.0 + lax.erf(values * np.float32(np.sqrt(0.5))))
    density = jnp.exp(-0.5 * values * values) * np.float32(1.0 / np.sqrt(2.0 * np.pi))
    return values * normal, normal + values * density


def head_kernel(
    own_ref, one_ref, two_ref, labels_ref, ignore_ref, targets_ref, hidden_bias_ref, inner_ref, inner_bias_ref, heads_ref, heads_bias_ref,
    logits_ref, deltas_ref, first_act_ref, second_act_ref, slopes_ref, second_grad_ref, first_grad_ref, bias_ref, first_slope_ref, second_slope_ref,
):
    first_pre = own_ref[...] + hidden_bias_ref[...]
    for come_ref in (one_ref, two_ref):
        first_pre = first_pre + come_ref[...].astype(f32)
    act, slope = gelu_and_slope(first_pre)
    first_slope_ref[...] = slope
    act = act.astype(bf16)
    first_act_ref[...] = act
    second_pre = jnp.dot(act, inner_ref[...], preferred_element_type=f32) + inner_bias_ref[...]
    act, slope = gelu_and_slope(second_pre)
    second_slope_ref[...] = slope
    act = act.astype(bf16)
    second_act_ref[...] = act
    heads = jnp.dot(act, heads_ref[...], preferred_element_type=f32) + heads_bias_ref[...]
    logits, deltas = heads[:, :LANES], heads[:, LANES:]
    facts = []
    for n in range(labels_ref.shape[0]):
        rows = slice(n * LANES, (n + 1) * LANES)
        logits_ref[:, n, :] = logits[rows].T[:CLS]
        deltas_ref[n] = deltas[rows].T[:BOX]
        fact = [labels_ref[n : n + 1, :].astype(f32), ignore_ref[n : n + 1, :].astype(f32)]
        fact += [targets_ref[n], jnp.zeros((2, LANES), f32)]
        facts.append(jnp.concatenate(fact, axis=0).T)
    facts = jnp.concatenate(facts, axis=0)
    label = facts[:, 0:1]
    kept = 1.0 - facts[:, 1:2]
    column = lax.broadcasted_iota(jnp.int32, logits.shape, 1)
    valid = column < CLS
    row_max = jnp.max(jnp.where(valid, logits, -jnp.inf), axis=1, keepdims=True)
    exponent = jnp.where(valid, jnp.exp(jnp.where(valid, logits - row_max, 0.0)), 0.0)
    softmax_rows = exponent / jnp.sum(exponent, axis=1, keepdims=True)
    hot = (column.astype(f32) == label).astype(f32)
    logit_slope = (softmax_rows - hot) * (kept * np.float32(1.0 / RPI))
    column = lax.broadcasted_iota(jnp.int32, deltas.shape, 1)
    target = facts[:, 2:3]
    for j in range(1, 4):
        target = jnp.where((column & 3) == j, facts[:, 2 + j : 3 + j], target)
    foreground = jnp.where(label < CLS - 1, kept, 0.0)
    hot = ((column >> 2).astype(f32) == label) & (column < BOX)
    delta_slope = jnp.where(
        hot,
        jnp.clip(deltas - target, -1.0, 1.0) * (foreground * np.float32(1.0 / RPI)),
        0.0,
    )
    slopes = jnp.concatenate([logit_slope, delta_slope], axis=1).astype(bf16)
    slopes_ref[...] = slopes
    turned = (((1,), (1,)), ((), ()))
    act_grad = lax.dot_general(slopes, heads_ref[...], turned, preferred_element_type=f32)
    second_grad = (act_grad * second_slope_ref[...]).astype(bf16)
    second_grad_ref[...] = second_grad
    act_grad = lax.dot_general(second_grad, inner_ref[...], turned, preferred_element_type=f32)
    first_grad = (act_grad * first_slope_ref[...]).astype(bf16)
    first_grad_ref[...] = first_grad
    units = first_grad.shape[1]
    bias_ref[...] = jnp.zeros_like(bias_ref)
    bias_ref[0:1, :] = jnp.sum(first_grad.astype(f32), axis=0, keepdims=True)
    bias_ref[1:2, :] = jnp.sum(second_grad.astype(f32), axis=0, keepdims=True)
    bias_ref[2:3, : slopes.shape[1]] = jnp.sum(slopes.astype(f32), axis=0, keepdims=True)


def head_block(own, come, labels, ignore, targets, hidden_bias, inner, inner_bias, heads, heads_bias):
    count, units = own.shape
    wide = heads.shape[1]
    images = labels.shape[0]
    return pl.pallas_call(
        head_kernel,
        in_specs=[pl.BlockSpec(memory_space=pltpu.VMEM)] * 11,
        out_specs=[pl.BlockSpec(memory_space=pltpu.VMEM)] * 8,
        out_shape=[
            like((CLS, images, LANES), f32),
            like((images, BOX, LANES), f32),
            like((count, units), bf16),
            like((count, units), bf16),
            like((count, wide), bf16),
            like((count, units), bf16),
            like((count, units), bf16),
            like((8, units), f32),
        ],
        scratch_shapes=[pltpu.VMEM((count, units), f32)] * 2,
        compiler_params=pltpu.CompilerParams(vmem_limit_bytes=24 * 2**20),
        cost_estimate=LARGE_COST,
        name="head_block",
    )(own, *come, labels, ignore, targets, hidden_bias, inner, inner_bias, heads, heads_bias)


def maps_kernel(where, arrays, outs):
    maps_ref, by_class_ref, across_first_ref = arrays
    pick_ref = outs[-1]
    size, part = by_class_ref.shape[:2]
    images = maps_ref.shape[0]
    for way in range(size):
        pick_ref[way * part : (way + 1) * part, :] = by_class_ref[where[0] ^ way]
    for n in range(images):
        flat = lax.dot_general(
            pick_ref[...], maps_ref[n], (((1,), (1,)), ((), ())), preferred_element_type=f32
        ).astype(bf16)
        flat = jnp.dot(flat, across_first_ref[...], preferred_element_type=f32).astype(bf16)
        for way in range(size):
            outs[way][n * part : (n + 1) * part, :] = flat[way * part : (way + 1) * part]


def maps_back_kernel(where, arrays, outs):
    came_refs, (by_class_ref, across_first_ref) = arrays[:-2], arrays[-2:]
    out_ref, pick_ref, flat_ref = outs
    size, part = by_class_ref.shape[:2]
    for way in range(size):
        pick_ref[way * part : (way + 1) * part, :] = by_class_ref[where[0] ^ way]
    for n in range(out_ref.shape[0]):
        for way in range(size):
            flat_ref[way * part : (way + 1) * part, :] = came_refs[way][n]
        cells = lax.dot_general(
            across_first_ref[...], flat_ref[...], (((1,), (1,)), ((), ())), preferred_element_type=f32
        ).astype(bf16)
        out_ref[n] = jnp.dot(cells, pick_ref[...], preferred_element_type=f32)


def arrange_kernel(sizes, where, arrays, outs):
    height, width, part, level_count = sizes
    for n in range(outs[0].shape[0]):
        for x in range(width):
            for k, ref in enumerate(arrays):
                outs[0][n, x * part : (x + 1) * part, k * height : (k + 1) * height] = ref[
                    n * part : (n + 1) * part, x * height : (x + 1) * height
                ]


def arrange_back_kernel(sizes, where, arrays, outs):
    height, width, part, level_count = sizes
    for n in range(arrays[0].shape[0]):
        for x in range(width):
            for k, out in enumerate(outs):
                out[n, :, x * height : (x + 1) * height] = sum(
                    ref[n, x * part : (x + 1) * part, k * height : (k + 1) * height].astype(f32)
                    for ref in arrays
                ).astype(bf16)


def split_span_kernel(length, where, arrays, outs):
    weight_ref, extra_ref = arrays
    total_ref = outs[-1]
    span, size = outs[0].shape[0], len(outs) - 1
    shape = (total_ref.shape[0], weight_ref.shape[0])
    row = lax.broadcasted_iota(jnp.int32, shape, 0)
    column = lax.broadcasted_iota(jnp.int32, shape, 1)
    kind = sum((row >= k * span).astype(jnp.int32) for k in range(1, size))
    matrix = jnp.where(column == (row - kind * span) * size + kind, 1.0, 0.0).astype(bf16)
    total_ref[...] = jnp.dot(matrix, weight_ref[...], preferred_element_type=f32)
    for k in range(size):
        at = k * span + length
        total_ref[at : at + extra_ref.shape[0], :] = extra_ref[...]
    for way, out in enumerate(outs[:-1]):
        at = pl.multiple_of((where[0] ^ way) * span, 8)
        out[...] = total_ref[pl.ds(at, span), :].astype(bf16)


def join_span_kernel(where, arrays, outs):
    total_ref = outs[-1]
    span = arrays[1].shape[0]
    for way, ref in enumerate(arrays[1:]):
        at = pl.multiple_of((where[0] ^ way) * span, 8)
        total_ref[pl.ds(at, span), :] = ref[...].astype(f32)
    product = jnp.dot(arrays[0][...], total_ref[...].astype(bf16), preferred_element_type=f32)
    for out in outs[:-1]:
        out[...] = product.astype(out.dtype)


def return_span_kernel(where, arrays, outs):
    total_ref = outs[-1]
    span = outs[0].shape[0]
    piece = sum(ref[...].astype(f32) for ref in arrays[1:]).astype(bf16)
    total_ref[...] = jnp.dot(arrays[0][...], piece, preferred_element_type=f32)
    for way, out in enumerate(outs[:-1]):
        at = pl.multiple_of((where[0] ^ way) * span, 8)
        out[...] = total_ref[pl.ds(at, span), :].astype(bf16)


def picking(rows, columns, pairs):
    matrix = np.zeros((rows, columns), np.float32)
    for a, b in pairs:
        matrix[a, b] = 1.0
    return jnp.asarray(matrix, bf16)


def swap(array, axis, bit):
    size = lax.axis_size(axis)
    return lax.ppermute(array, axis, [(at, at ^ bit) for at in range(size)])


def exchange(array, axis):
    return lax.all_to_all(array, axis, split_axis=0, concat_axis=0, tiled=True)


def exchange_ways(arrays, axis):
    return [arrays[0]] + [swap(one, axis, way) for way, one in enumerate(arrays) if way]


def product_kernel(bits, parts, with_sum, where_ref, *refs):
    number = len(bits)
    grad_refs, crop_refs, refs = refs[:parts], refs[parts : 2 * parts], refs[2 * parts :]
    sign_ref, refs = refs[-1], refs[:-1]
    sign_ref[...] = jnp.zeros_like(sign_ref)
    outs = refs[-number:] if with_sum else [refs[-1].at[n] for n in range(number)]
    rows = crop_refs[0].shape[0] // 8
    for n in range(number):
        total = refs[0][n].astype(f32) if with_sum else 0.0
        at = pl.multiple_of((where_ref[1] ^ bits[n]) * rows, 16)
        for grad_ref, crop_ref in zip(grad_refs, crop_refs):
            total = total + jnp.dot(
                crop_ref[pl.ds(at, rows), :], grad_ref[...], preferred_element_type=f32
            )
        outs[n][...] = total.astype(bf16)


def piece_product(crops, grads, where, bits, come, earlier):
    features = crops[0].shape[0]
    units = grads[0].shape[1]
    rows = features // 8
    number = len(bits)
    with_sum = come is not None
    come = [come] if with_sum else []
    outs = (
        [like((rows, units), bf16)] * number if with_sum else [like((number, rows, units), bf16)]
    )
    return pl.pallas_call(
        functools.partial(product_kernel, bits, len(grads), with_sum),
        in_specs=[SCALAR]
        + [WHOLE for one in (*grads, *crops, *come)]
        + [FAR for one in earlier],
        out_specs=[WHOLE for one in (*outs, SIGN)],
        out_shape=[*outs, SIGN],
        compiler_params=pltpu.CompilerParams(vmem_limit_bytes=24 * 2**20),
        cost_estimate=LARGE_COST,
        name="piece_product",
    )(where, *grads, *crops, *come, *earlier)


def butterfly(array):
    for axis in ("img", "level"):
        bit = 1
        while bit < lax.axis_size(axis):
            array = array + swap(array, axis, bit)
            bit *= 2
    return array


def contract_rows(left_side, right_side):
    return lax.dot_general(
        left_side, right_side, (((0,), (0,)), ((), ())), preferred_element_type=f32
    )


def pack_rows(array):
    rows, units = array.shape[-2], array.shape[-1] // 3 * 2
    beside = array[..., units:]
    below = jnp.concatenate([beside[..., : rows // 2, :], beside[..., rows // 2 :, :]], axis=-1)
    return jnp.concatenate([array[..., :units], below], axis=-2)


def per_device(
    pyramid,
    levels,
    region_boxes,
    labels,
    crowd_ignore,
    targets,
    hidden_weight,
    hidden_bias,
    inner_weight,
    inner_bias,
    class_weight,
    class_bias,
    delta_weight,
    delta_bias,
):
    size = lax.axis_size("level")
    planes = lax.axis_size("img")
    z = lax.axis_index("level")
    where = jnp.stack([z, lax.axis_index("img")]).astype(jnp.int32)
    images, height, width, channels = pyramid.shape[1:]
    regions = levels.shape[1]
    part = channels // size
    sizes = (height, width, part, size)
    rows, units = hidden_weight.shape
    block_rows = images * regions
    direct = planes == 8 and rows % size == 0

    packed = jnp.concatenate(
        [
            jnp.transpose(region_boxes, (0, 2, 1)),
            jnp.transpose(levels, (0, 2, 1)),
            jnp.zeros((images, 3, regions), jnp.int32),
        ],
        axis=1,
    )
    class_room, delta_room = LANES, units // 2 - LANES
    small = jnp.concatenate(
        [
            inner_weight,
            jnp.pad(class_weight, ((0, 0), (0, class_room - CLS))),
            jnp.pad(delta_weight, ((0, 0), (0, delta_room - BOX))),
        ],
        axis=1,
    )
    heads_bias = jnp.concatenate(
        [
            jnp.pad(class_bias, (0, class_room - CLS)),
            jnp.pad(delta_bias, (0, delta_room - BOX)),
        ]
    )[None]

    if direct:
        length = rows // size
        span = -(-(length + images) // 8) * 8
        to_span = picking(
            size * span,
            rows,
            [(k * span + j, j * size + k) for k in range(size) for j in range(length)],
        )
        room = -(-rows // 16) * 16
        features = planes * room
        from_span = picking(
            room,
            size * span,
            [(k * length + j, k * span + j) for k in range(size) for j in range(length)],
        )
        total = [pltpu.VMEM((size * span, units), f32)]
        *sent, sign = call(
            functools.partial(split_span_kernel, length),
            [like((span, units), bf16)] * size,
            where,
            [hidden_weight, packed.astype(f32).reshape(images, units)],
            scratch=total,
            name="split_span",
        )
        came = exchange_ways(sent, "level")
        piece, own_piece, sign = call(
            join_span_kernel,
            [like((room, units), bf16)] * 2,
            where,
            [from_span, *came],
            scratch=total,
            name="join_span",
        )
        boxes = jnp.stack([one[length : length + images].reshape(images, 8, regions) for one in came])
        pieces = [own_piece] + [swap(piece, "img", bit) for bit in (2, 4, 6)]
        order = [k * planes + at for at in range(planes) for k in range(size)]
        table = runs_of(order, length, part, size, room)
    else:
        boxes = exchange(jnp.broadcast_to(packed[None], (size,) + packed.shape), "level")
        boxes = jnp.stack([lax.dynamic_index_in_dim(boxes, z ^ way, 0, False) for way in range(size)])
        features = BINS * part
        whole = lax.all_gather(hidden_weight, AXES, axis=0, tiled=True)
        weight = lax.dynamic_index_in_dim(whole.reshape(features, size, units), z, 1, False)
        table = runs_of([0], features, part, 1, features)
    row = jnp.arange(8)[:, None]
    boxes = jnp.where(row == 4, boxes.astype(jnp.int32) ^ z, boxes.astype(jnp.int32)).astype(f32)

    spots = height * width
    by_class = picking(
        channels, channels, [(c % size * part + c // size, c) for c in range(channels)]
    ).reshape(size, part, channels)
    across_first = picking(
        spots, spots, [(y * width + x, x * height + y) for y in range(height) for x in range(width)]
    )
    picks = [
        pltpu.VMEM((channels, channels), bf16),
        pltpu.VMEM((channels, spots), bf16),
    ]
    small_rows = small.shape[0] // 2 * 3
    maps = call(
        maps_kernel,
        [like((images * part, spots), bf16)] * size,
        where,
        [pyramid[0].reshape(images, spots, channels), by_class, across_first],
        scratch=picks[:1],
        name="maps",
    )[:size]
    if direct:
        maps = [maps[0], *tie(maps[1:], sign)]
    maps_came = exchange_ways(maps[:3], "level")
    maps_came.append(swap(tie([maps[3]], maps_came[1])[0], "level", 3))
    if direct:
        smalls = tie([pack_rows(small)], maps_came[3])[0]
    maps, sign = call(
        functools.partial(arrange_kernel, sizes),
        [pltpu.VMEM((images, width * part, size * height), bf16)],
        where,
        maps_came,
        name="arrange",
    )

    ways = (3, 2, 1, 0)
    crops, signs, came_sums = [], [], []
    for turn, way in enumerate(ways):
        if turn == 0:
            crop, turned, sign = crop_block(table, sizes, features, boxes[way], maps)
            if direct:
                smalls, unused = pair_up((0, 0), where, smalls, [sign])
                own_piece = tie([own_piece], sign)[0]
                pieces = [own_piece, *pieces[1:]]
                pieces = sum(([one, swap(one, "img", 1)] for one in pieces), [])
                weight = gather_pieces(where, pieces)
            own, sign = multiply(turned, weight)
            relayed = swap(own, "level", 1)
        else:
            crop, own, sign = crop_block(
                table, sizes, features, boxes[way], maps, weight, bf16 if way == 1 else f32, signs[-1:]
            )
        if way == 2 and direct:
            smalls, sign = pair_up((0, 1), where, smalls, [sign])
            smalls = smalls.reshape(size, small_rows, units)
            smalls = [swap(smalls, "img", bit) if bit else smalls for bit in (0, 2, 4, 6)]
        if way == 2:
            own, sign = call(add_kernel, [like(own.shape, bf16)], where, [own, relayed], [sign], name="add")
        if way in (1, 2):
            came_sums.append(swap(own, "level", way))
        crops.append(crop)
        signs.append(sign)

    if direct:
        smalls, unused = call(
            order_kernel,
            [like((4, size, small_rows, units), bf16)],
            where,
            smalls,
            signs[2:3],
            name="in_order",
        )
        full_inner, full_heads, sign = call(
            functools.partial(full_small_kernel, small.shape[0]),
            [pltpu.VMEM((units, units), bf16), pltpu.VMEM((units, units // 2), bf16)],
            where,
            [smalls, swap(smalls, "img", 1)],
            name="full_small",
        )
    else:
        smalls = lax.all_gather(small, AXES, axis=0, tiled=True)
        full_inner, full_heads = smalls[:, :units], smalls[:, units:]

    logits, deltas, first_act, second_act, slopes, second_grad, first_grad, bias_sums = head_block(
        own,
        came_sums,
        labels,
        crowd_ignore,
        jnp.transpose(targets, (0, 2, 1)),
        hidden_bias[None],
        full_inner,
        inner_bias[None],
        full_heads,
        heads_bias,
    )

    near = swap(first_grad, "level", 1)
    far = swap(first_grad, "level", 2)
    grad_of = {0: first_grad, 1: near}

    shares = []

    def take_up(way, earlier=()):
        share, sign = spread_block(table, sizes, boxes[way], grad_of[way], weight, earlier)
        shares.append(share)
        return sign

    if direct:
        count = small.shape[0]
        sent, kept, sign = small_product(
            where, count, first_act, second_grad, second_act, slopes, bias_sums
        )
        sign = take_up(0, [sign])
        *quarters, sign = quarter_rows(count, where, kept, swap(sent, "img", 1), [sign])
        quarters = [
            swap(one, "img", bit) if bit else one for one, bit in zip(quarters, (0, 2, 4, 6))
        ]
        grad_of[2] = tie([far], sign)[0]
        grad_of[3] = swap(grad_of[2], "level", 1)
        sign = take_up(1, [sign])
        sign = take_up(2, [sign])

        grads = [grad_of[way] for way in ways]
        parts, others = {}, {}

        def for_other(bits, sign):
            theirs = tuple(bit ^ 1 for bit in bits)
            products, sign = piece_product(crops, grads, where, theirs, None, [sign])
            others[bits] = swap(products, "img", 1)
            return sign

        def for_own(bits, sign):
            *own, sign = piece_product(crops, grads, where, bits, others[bits], [sign])
            for one, bit in zip(own, bits):
                parts[bit] = swap(one, "img", bit) if bit else one
            return sign

        sign = for_other((6,), sign)
        sign = for_other((2, 4), sign)
        sign = for_own((6,), sign)
        sent, kept, sign = halve_rows((0, 1), 2, count, where, quarters, [sign])
        sign = for_own((2, 4), sign)
        sign = for_other((0,), sign)
        sign = take_up(3, [sign])
        sent, kept, sign = halve_rows(
            (0, 0), 1, count, where, [kept, swap(sent, "level", 2)], [sign]
        )
        sign = for_own((0,), sign)
        inner_sum, class_sum, delta_sum, bias_total, sign = call(
            small_sum_kernel,
            [
                like((count, units), f32),
                like((count, CLS), f32),
                like((count, BOX), f32),
                like((8, units), f32),
            ],
            where,
            [kept, swap(sent, "level", 1)],
            [sign],
            name="small_sum",
        )
        half, sign = call(
            add_kernel, [like(parts[0].shape, f32)], where, [parts[0], parts[6]], [sign], name="add"
        )
        *back, sign = call(
            functools.partial(arrange_back_kernel, sizes),
            [like((images, part, spots), bf16)] * size,
            where,
            shares,
            [sign],
            name="arrange_back",
        )
        *out, sign = call(
            return_span_kernel,
            [like((span, units), bf16)] * size,
            where,
            [from_span.T, half, parts[2], parts[4]],
            [sign],
            scratch=total,
            name="return_span",
        )
    else:
        grad_of[2], grad_of[3] = far, swap(far, "level", 1)
        for way in range(size):
            take_up(way)
        *back, sign = call(
            functools.partial(arrange_back_kernel, sizes),
            [like((images, part, spots), bf16)] * size,
            where,
            shares,
            name="arrange_back",
        )
        bias_total = butterfly(bias_sums)
        small_sum = jnp.concatenate(
            [contract_rows(first_act, second_grad), contract_rows(second_act, slopes)], axis=1
        )
        small_sum = lax.psum_scatter(small_sum, AXES, scatter_dimension=0, tiled=True)
        inner_sum = small_sum[:, :units]
        class_sum = small_sum[:, units : units + CLS]
        delta_sum = small_sum[:, units + class_room : units + class_room + BOX]
        whole_grads = jnp.concatenate([grad_of[way] for way in ways])
        product = jnp.dot(
            jnp.concatenate(crops, axis=1), whole_grads, preferred_element_type=f32
        )
        own = (jnp.arange(size, dtype=jnp.int32) == z)[None, :, None]
        hidden_sum = lax.psum_scatter(
            jnp.where(own, product[:, None, :], 0.0).reshape(features * size, units),
            AXES,
            scatter_dimension=0,
            tiled=True,
        )

    map_grads, sign = call(
        maps_back_kernel,
        [like((images, spots, channels), f32)],
        where,
        [*exchange_ways(back, "level"), by_class, across_first],
        [sign],
        scratch=picks,
        name="maps_back",
    )
    map_grads = map_grads.reshape(1, images, height, width, channels)
    if direct:
        hidden_sum = call(
            join_span_kernel,
            [like((rows, units), f32)],
            where,
            [to_span.T, *exchange_ways(out, "level")],
            [sign],
            scratch=total,
            name="join_span",
        )[0]

    head_bias = bias_total[2, : class_room + delta_room]
    return (
        jnp.transpose(logits, (1, 2, 0)),
        jnp.transpose(deltas, (0, 2, 1)),
        map_grads,
        hidden_sum,
        bias_total[0],
        inner_sum,
        bias_total[1],
        class_sum,
        head_bias[:CLS],
        delta_sum,
        head_bias[class_room : class_room + BOX],
    )


def solution(mesh):
    return jax.shard_map(
        per_device,
        mesh=mesh,
        in_specs=(
            P("level", "img", None, None, None),
            P("img", "level", None),
            P("img", "level", None),
            P("img", "level"),
            P("img", "level"),
            P("img", "level", None),
            P(AXES, None),
            P(),
            P(AXES, None),
            P(),
            P(AXES, None),
            P(),
            P(AXES, None),
            P(),
        ),
        out_specs=(
            P("img", "level", None),
            P("img", "level", None),
            P("level", "img", None, None, None),
            P(AXES, None),
            P(),
            P(AXES, None),
            P(),
            P(AXES, None),
            P(),
            P(AXES, None),
            P(),
        ),
        check_vma=False,
    )
```

```python
import functools

import jax
import jax.numpy as jnp
import numpy as np
from jax import lax
from jax.experimental import pallas as pl
from jax.experimental.pallas import tpu as pltpu
from jax.sharding import PartitionSpec as P

POOL = 7
SAMPLES = 2
CLS = 81
BOX = 320
RPI = 512
BINS = POOL * POOL
LANES = 128
AXES = ("level", "img")
OFFSETS = (np.arange(SAMPLES * POOL, dtype=np.float32) + np.float32(0.5)) / np.float32(
    SAMPLES * POOL
)
SMALL_COST = pl.CostEstimate(flops=10**9, bytes_accessed=1, transcendentals=0)
LARGE_COST = pl.CostEstimate(flops=2 * 10**10, bytes_accessed=1, transcendentals=0)
f32 = jnp.float32
bf16 = jnp.bfloat16
FAR = pl.BlockSpec(memory_space=pl.ANY)
WHOLE = pl.BlockSpec(memory_space=pltpu.VMEM)
SCALAR = pl.BlockSpec(memory_space=pltpu.SMEM)
like = jax.ShapeDtypeStruct
SIGN = jax.ShapeDtypeStruct((8, LANES), jnp.float32)


def bin_weights(low, span, centres, at):
    first = jnp.maximum(1.0 - jnp.abs((low + OFFSETS[2 * at] * span) - centres), 0.0)
    second = jnp.maximum(1.0 - jnp.abs((low + OFFSETS[2 * at + 1] * span) - centres), 0.0)
    return ((first + second) * 0.5).astype(bf16)


def fill_weights(box_ref, down_ref, across_ref, height, width, level_count):
    x0, y0, x1, y1, level = [box_ref[k : k + 1, :] for k in range(5)]
    centres = lax.broadcasted_iota(jnp.int32, (width, LANES), 0).astype(f32)
    for q in range(POOL):
        across_ref[q] = bin_weights(x0, x1 - x0, centres, q)
    centres = lax.broadcasted_iota(jnp.int32, (height, LANES), 0).astype(f32)
    for p in range(POOL):
        weights = bin_weights(y0, y1 - y0, centres, p).astype(f32)
        for k in range(level_count):
            down_ref[k * height : (k + 1) * height, p * LANES : (p + 1) * LANES] = jnp.where(
                level == float(k), weights, 0.0
            ).astype(bf16)


def runs_of(order, length, part, group, room):
    place = {chunk: at // group * room + at % group * length for at, chunk in enumerate(order)}
    table = []
    for at in range(BINS):
        row, end, runs = at * part, (at + 1) * part, []
        while row < end:
            chunk = row // length
            stop = min(end, (chunk + 1) * length)
            runs.append((row - at * part, place[chunk] + row - chunk * length, stop - row))
            row = stop
        table.append(runs)
    return table


def gaps_of(table, features):
    held = sorted((kept, kept + count) for runs in table for row, kept, count in runs)
    gaps, last = [], 0
    for first, end in held + [(features, features)]:
        if first > last:
            gaps.append((last, first))
        last = end
    return gaps


def gather_kernel(number, where_ref, *refs):
    kept_ref, sems = refs[-2:]
    rows = refs[0].shape[0]
    copies = []
    for k, ref in enumerate(refs[:number]):
        at = pl.multiple_of((where_ref[1] ^ k) * rows, 16)
        copies.append(pltpu.make_async_copy(ref, kept_ref.at[pl.ds(at, rows)], sems.at[k]))
    for copy in copies:
        copy.start()
    for copy in copies:
        copy.wait()


def gather_pieces(where, pieces):
    rows, units = pieces[0].shape
    number = len(pieces)
    return pl.pallas_call(
        functools.partial(gather_kernel, number),
        in_specs=[SCALAR] + [FAR for one in pieces],
        out_specs=WHOLE,
        out_shape=pltpu.VMEM((number * rows, units), bf16),
        scratch_shapes=[pltpu.SemaphoreType.DMA((number,))],
        compiler_params=pltpu.CompilerParams(vmem_limit_bytes=24 * 2**20),
        cost_estimate=LARGE_COST,
        name="gather_pieces",
    )(where, *pieces)


def crop_kernel(table, sizes, product, box_ref, maps_ref, *refs):
    if product:
        weight_ref = refs[0]
        crop_ref, out_ref, sign_ref, down_ref, across_ref, sums_ref, rows_ref, turned_ref = refs[-8:]
    else:
        crop_ref, out_ref, sign_ref, down_ref, across_ref, sums_ref, rows_ref = refs[-7:]
    sign_ref[...] = jnp.zeros_like(sign_ref)
    height, width, part, level_count = sizes
    for first, end in gaps_of(table, rows_ref.shape[0]):
        rows_ref[first:end, :] = jnp.zeros((end - first, LANES), f32)
    fill_weights(box_ref, down_ref, across_ref, height, width, level_count)
    sums_ref[...] = jnp.dot(maps_ref[...], down_ref[...], preferred_element_type=f32).astype(bf16)
    for p in range(POOL):
        lanes = slice(p * LANES, (p + 1) * LANES)
        for start in range(0, POOL, 2):
            bins = range(start, min(POOL, start + 2))
            totals = [None for q in bins]
            for x in range(width):
                piece = sums_ref[x * part : (x + 1) * part, lanes]
                for at, q in enumerate(bins):
                    term = across_ref[q, x : x + 1, :] * piece
                    totals[at] = term if x == 0 else totals[at] + term
            for at, q in enumerate(bins):
                for row, kept, count in table[p * POOL + q]:
                    rows_ref[kept : kept + count, :] = totals[at][row : row + count].astype(f32)
    crop = rows_ref[...].astype(bf16)
    crop_ref[...] = crop
    if not product:
        out_ref[...] = crop.T
        return
    turned_ref[pl.ds(pl.multiple_of(pl.program_id(0) * LANES, LANES), LANES), :] = crop.T

    @pl.when(pl.program_id(0) == pl.num_programs(0) - 1)
    def multiply():
        out_ref[...] = jnp.dot(
            turned_ref[...], weight_ref[...], preferred_element_type=f32
        ).astype(out_ref.dtype)


def spread_kernel(table, sizes, box_ref, grad_ref, weight_ref, *refs):
    total_ref, sign_ref, down_ref, across_ref, sums_ref, rows_ref, crop_ref = refs[-7:]
    sign_ref[...] = jnp.zeros_like(sign_ref)
    height, width, part, level_count = sizes
    images = box_ref.shape[0]
    for n in range(images):
        fill_weights(
            box_ref.at[n], down_ref.at[n], across_ref.at[n], height, width, level_count
        )
    crop_ref[...] = lax.dot_general(
        weight_ref[...], grad_ref[...], (((1,), (1,)), ((), ())), preferred_element_type=f32
    ).astype(bf16)
    for n in range(images):
        rows_ref[...] = crop_ref[:, n * LANES : (n + 1) * LANES].astype(f32)
        for p in range(POOL):
            lanes = slice(p * LANES, (p + 1) * LANES)
            pieces = []
            for q in range(POOL):
                runs = [rows_ref[kept : kept + count, :] for row, kept, count in table[p * POOL + q]]
                runs = runs[0] if len(runs) == 1 else jnp.concatenate(runs, axis=0)
                pieces.append(runs.astype(bf16))
            for x in range(width):
                total = across_ref[n, 0, x : x + 1, :] * pieces[0]
                for q in range(1, POOL):
                    total = total + across_ref[n, q, x : x + 1, :] * pieces[q]
                sums_ref[x * part : (x + 1) * part, lanes] = total
        total_ref[n] = lax.dot_general(
            sums_ref[...], down_ref[n], (((1,), (1,)), ((), ())), preferred_element_type=f32
        ).astype(bf16)


def crop_block(table, sizes, features, boxes, maps, weight=None, out_type=bf16, earlier=(), cost=LARGE_COST):
    height, width, part, level_count = sizes
    images = boxes.shape[0]
    product = weight is not None
    first = [boxes, maps] + ([weight] if product else [])
    rows = images * LANES
    if product:
        units = weight.shape[1]
        out_spec = pl.BlockSpec((rows, units), lambda n: (0, 0))
        out_shape = like((rows, units), out_type)
        more = [pltpu.VMEM((rows, features), bf16)]
    else:
        out_spec = pl.BlockSpec((LANES, features), lambda n: (n, 0))
        out_shape = like((rows, features), bf16)
        more = []
    return pl.pallas_call(
        functools.partial(crop_kernel, table, sizes, product),
        grid=(images,),
        in_specs=[
            pl.BlockSpec((None, 8, LANES), lambda n: (n, 0, 0)),
            pl.BlockSpec((None, width * part, level_count * height), lambda n: (n, 0, 0)),
        ]
        + [WHOLE for one in first[2:]]
        + [FAR for one in earlier],
        out_specs=[
            pl.BlockSpec((features, LANES), lambda n: (0, n)),
            out_spec,
            pl.BlockSpec((8, LANES), lambda n: (0, 0)),
        ],
        out_shape=[like((features, rows), bf16), out_shape, SIGN],
        scratch_shapes=[
            pltpu.VMEM((level_count * height, POOL * LANES), bf16),
            pltpu.VMEM((POOL, width, LANES), bf16),
            pltpu.VMEM((width * part, POOL * LANES), bf16),
            pltpu.VMEM((features, LANES), f32),
        ]
        + more,
        compiler_params=pltpu.CompilerParams(vmem_limit_bytes=24 * 2**20),
        cost_estimate=cost,
        name="crop_block",
    )(*first, *earlier)


def multiply_kernel(rows_ref, weight_ref, out_ref, sign_ref):
    out_ref[...] = jnp.dot(rows_ref[...], weight_ref[...], preferred_element_type=f32).astype(bf16)
    sign_ref[...] = jnp.zeros_like(sign_ref)


def multiply(rows, weight):
    return pl.pallas_call(
        multiply_kernel,
        in_specs=[WHOLE, WHOLE],
        out_specs=[WHOLE, WHOLE],
        out_shape=[like((rows.shape[0], weight.shape[1]), bf16), SIGN],
        compiler_params=pltpu.CompilerParams(vmem_limit_bytes=24 * 2**20),
        cost_estimate=LARGE_COST,
        name="multiply",
    )(rows, weight)


def spread_block(table, sizes, boxes, grads, weight, earlier=()):
    height, width, part, level_count = sizes
    images = boxes.shape[0]
    features = weight.shape[0]
    return pl.pallas_call(
        functools.partial(spread_kernel, table, sizes),
        in_specs=[WHOLE, WHOLE, WHOLE] + [FAR for one in earlier],
        out_specs=[WHOLE, WHOLE],
        out_shape=[like((images, width * part, level_count * height), bf16), SIGN],
        scratch_shapes=[
            pltpu.VMEM((images, level_count * height, POOL * LANES), bf16),
            pltpu.VMEM((images, POOL, width, LANES), bf16),
            pltpu.VMEM((width * part, POOL * LANES), bf16),
            pltpu.VMEM((features, LANES), f32),
            pltpu.VMEM((features, images * LANES), bf16),
        ],
        compiler_params=pltpu.CompilerParams(vmem_limit_bytes=24 * 2**20),
        cost_estimate=LARGE_COST,
        name="spread_block",
    )(boxes, grads, weight, *earlier)


def call(kernel, outs, where, arrays, earlier=(), scratch=(), name=None, cost=LARGE_COST):
    arrays = list(arrays)

    def body(*refs):
        end = 1 + len(arrays)
        later = refs[end + len(earlier) :]
        later[len(outs)][...] = jnp.zeros(SIGN.shape, SIGN.dtype)
        kernel(refs[0], refs[1:end], (*later[: len(outs)], *later[len(outs) + 1 :]))

    return pl.pallas_call(
        body,
        in_specs=[SCALAR] + [WHOLE for one in arrays] + [FAR for one in earlier],
        out_specs=[WHOLE for one in (*outs, SIGN)],
        out_shape=[*outs, SIGN],
        scratch_shapes=scratch,
        compiler_params=pltpu.CompilerParams(vmem_limit_bytes=24 * 2**20),
        cost_estimate=cost,
        name=name,
    )(where, *arrays, *earlier)


def tie_kernel(*refs):
    pass


def tie(arrays, *earlier):
    return pl.pallas_call(
        tie_kernel,
        in_specs=[FAR for one in (*arrays, *earlier)],
        out_specs=[FAR for one in arrays],
        out_shape=[like(one.shape, one.dtype) for one in arrays],
        input_output_aliases={k: k for k in range(len(arrays))},
        compiler_params=pltpu.CompilerParams(vmem_limit_bytes=2**20),
        cost_estimate=SMALL_COST,
        name="tie",
    )(*arrays, *earlier)


def add_kernel(where, arrays, outs):
    outs[0][...] = sum(ref[...].astype(f32) for ref in arrays).astype(outs[0].dtype)


def pair_kernel(bit, where, arrays, outs):
    own = (where[bit[0]] >> bit[1]) & 1
    outs[0][own] = arrays[0][...]
    outs[0][1 - own] = arrays[1][...]


def pair_up(bit, where, own, earlier):
    come = swap(own, AXES[bit[0]], 1 << bit[1])
    out = like((2,) + own.shape, own.dtype)
    return call(functools.partial(pair_kernel, bit), [out], where, [own, come], earlier, name="pair_up")


def order_kernel(where, arrays, outs):
    for k, ref in enumerate(arrays):
        outs[0][(where[1] >> 1) ^ k] = ref[...]


def full_small_kernel(rows, where, arrays, outs):
    units = outs[0].shape[1]
    for k, ref in enumerate(arrays):
        core = (where[1] & 1) ^ k
        for chip in range(4):
            for level in range(ref.shape[1]):
                at = pl.multiple_of(((level * 4 + chip) * 2 + core) * rows, rows)
                outs[0][pl.ds(at, rows), :] = ref[chip, level, :rows, :]
                for part in range(2):
                    outs[1][pl.ds(at + part * (rows // 2), rows // 2), :] = ref[
                        chip, level, rows:, part * (units // 2) : (part + 1) * (units // 2)
                    ]


def split_rows(own, inner, array, rows, sent, kept):
    step = inner * rows
    for at in range((kept.shape[0] - 16) // step):
        mine = pl.multiple_of((2 * at + own) * step, rows)
        other = pl.multiple_of((2 * at + 1 - own) * step, rows)
        kept[at * step : (at + 1) * step, :] = array[pl.ds(mine, step), :].astype(bf16)
        sent[at * step : (at + 1) * step, :] = array[pl.ds(other, step), :].astype(bf16)


def put_biases(biases, refs):
    high = biases.astype(bf16)
    low = (biases - high.astype(f32)).astype(bf16)
    for ref in refs:
        end = ref.shape[0]
        ref[end - 16 : end - 8, : high.shape[1]] = high
        ref[end - 8 : end, : high.shape[1]] = low


def get_biases(ref, units):
    end = ref.shape[0]
    last = ref[end - 16 :, :units].astype(f32)
    return last[:8] + last[8:]


def small_product_kernel(rows, where_ref, first_ref, second_grad_ref, second_ref, slopes_ref, bias_ref, sent_ref, kept_ref, sign_ref, total_ref):
    turned = (((0,), (0,)), ((), ()))
    units = first_ref.shape[1]
    total_ref[:, :units] = lax.dot_general(
        first_ref[...], second_grad_ref[...], turned, preferred_element_type=f32
    )
    total_ref[:, units:] = lax.dot_general(
        second_ref[...], slopes_ref[...], turned, preferred_element_type=f32
    )
    split_rows(where_ref[1] & 1, 1, total_ref, rows, sent_ref, kept_ref)
    put_biases(bias_ref[...], [sent_ref, kept_ref])
    sign_ref[...] = jnp.zeros_like(sign_ref)


def small_product(where, rows, first_act, second_grad, second_act, slopes, biases):
    units = first_act.shape[1]
    wide = units + slopes.shape[1]
    half = like((units // 2 + 16, wide), bf16)
    return pl.pallas_call(
        functools.partial(small_product_kernel, rows),
        in_specs=[SCALAR] + [WHOLE] * 5,
        out_specs=[WHOLE] * 3,
        out_shape=[half, half, SIGN],
        scratch_shapes=[pltpu.VMEM((units, wide), f32)],
        compiler_params=pltpu.CompilerParams(vmem_limit_bytes=24 * 2**20),
        cost_estimate=LARGE_COST,
        name="small_product",
    )(where, first_act, second_grad, second_act, slopes, biases)


def quarter_kernel(rows, where_ref, kept_ref, come_ref, *refs):
    outs, sign_ref, total_ref = refs[-6:-2], refs[-2], refs[-1]
    sign_ref[...] = jnp.zeros_like(sign_ref)
    count, units = total_ref.shape[0], total_ref.shape[1] // 3 * 2
    total_ref[...] = kept_ref[:count, :].astype(f32) + come_ref[:count, :].astype(f32)
    for k, out in enumerate(outs):
        for at in range(count // rows // 4):
            first = pl.multiple_of((4 * at + ((where_ref[1] >> 1) ^ k)) * rows, rows)
            out[at * rows : (at + 1) * rows, :] = total_ref[pl.ds(first, rows), :].astype(bf16)
    put_biases(get_biases(kept_ref, units) + get_biases(come_ref, units), outs)


def quarter_rows(rows, where, kept, come, earlier):
    count = kept.shape[0] - 16
    quarter = like((count // 4 + 16, kept.shape[1]), bf16)
    return pl.pallas_call(
        functools.partial(quarter_kernel, rows),
        in_specs=[SCALAR, WHOLE, WHOLE] + [FAR for one in earlier],
        out_specs=[WHOLE] * 5,
        out_shape=[quarter] * 4 + [SIGN],
        scratch_shapes=[pltpu.VMEM((count, kept.shape[1]), f32)],
        compiler_params=pltpu.CompilerParams(vmem_limit_bytes=24 * 2**20),
        cost_estimate=LARGE_COST,
        name="quarter_rows",
    )(where, kept, come, *earlier)


def halve_kernel(bit, inner, rows, where, arrays, outs):
    sent_out, kept_out, total_ref = outs
    count, units = total_ref.shape[0], total_ref.shape[1] // 3 * 2
    total_ref[...] = sum(ref[:count, :].astype(f32) for ref in arrays)
    split_rows((where[bit[0]] >> bit[1]) & 1, inner, total_ref, rows, sent_out, kept_out)
    biases = [get_biases(ref, units) for ref in arrays]
    while len(biases) > 1:
        biases = [biases[k] + biases[k + 1] for k in range(0, len(biases), 2)]
    put_biases(biases[0], [sent_out, kept_out])


def halve_rows(bit, inner, rows, where, arrays, earlier):
    count, wide = arrays[0].shape[0] - 16, arrays[0].shape[1]
    return call(
        functools.partial(halve_kernel, bit, inner, rows),
        [like((count // 2 + 16, wide), bf16)] * 2,
        where,
        arrays,
        earlier,
        [pltpu.VMEM((count, wide), f32)],
        name="halve_rows",
        cost=SMALL_COST,
    )


def small_sum_kernel(where, arrays, outs):
    rows, units = outs[0].shape
    total = sum(ref[:rows, :].astype(f32) for ref in arrays)
    outs[0][...] = total[:, :units]
    outs[1][...] = total[:, units : units + CLS]
    outs[2][...] = total[:, units + LANES : units + LANES + BOX]
    outs[3][...] = sum(get_biases(ref, units) for ref in arrays)


def gelu_and_slope(values):
    normal = 0.5 * (1.0 + lax.erf(values * np.float32(np.sqrt(0.5))))
    density = jnp.exp(-0.5 * values * values) * np.float32(1.0 / np.sqrt(2.0 * np.pi))
    return values * normal, normal + values * density


def head_kernel(
    own_ref, one_ref, two_ref, labels_ref, ignore_ref, targets_ref, hidden_bias_ref, inner_ref, inner_bias_ref, heads_ref, heads_bias_ref,
    logits_ref, deltas_ref, first_act_ref, second_act_ref, slopes_ref, second_grad_ref, first_grad_ref, bias_ref, first_slope_ref, second_slope_ref,
):
    first_pre = own_ref[...] + hidden_bias_ref[...]
    for come_ref in (one_ref, two_ref):
        first_pre = first_pre + come_ref[...].astype(f32)
    act, slope = gelu_and_slope(first_pre)
    first_slope_ref[...] = slope
    act = act.astype(bf16)
    first_act_ref[...] = act
    second_pre = jnp.dot(act, inner_ref[...], preferred_element_type=f32) + inner_bias_ref[...]
    act, slope = gelu_and_slope(second_pre)
    second_slope_ref[...] = slope
    act = act.astype(bf16)
    second_act_ref[...] = act
    heads = jnp.dot(act, heads_ref[...], preferred_element_type=f32) + heads_bias_ref[...]
    logits, deltas = heads[:, :LANES], heads[:, LANES:]
    facts = []
    for n in range(labels_ref.shape[0]):
        rows = slice(n * LANES, (n + 1) * LANES)
        logits_ref[:, n, :] = logits[rows].T[:CLS]
        deltas_ref[n] = deltas[rows].T[:BOX]
        fact = [labels_ref[n : n + 1, :].astype(f32), ignore_ref[n : n + 1, :].astype(f32)]
        fact += [targets_ref[n], jnp.zeros((2, LANES), f32)]
        facts.append(jnp.concatenate(fact, axis=0).T)
    facts = jnp.concatenate(facts, axis=0)
    label = facts[:, 0:1]
    kept = 1.0 - facts[:, 1:2]
    column = lax.broadcasted_iota(jnp.int32, logits.shape, 1)
    valid = column < CLS
    row_max = jnp.max(jnp.where(valid, logits, -jnp.inf), axis=1, keepdims=True)
    exponent = jnp.where(valid, jnp.exp(jnp.where(valid, logits - row_max, 0.0)), 0.0)
    softmax_rows = exponent / jnp.sum(exponent, axis=1, keepdims=True)
    hot = (column.astype(f32) == label).astype(f32)
    logit_slope = (softmax_rows - hot) * (kept * np.float32(1.0 / RPI))
    column = lax.broadcasted_iota(jnp.int32, deltas.shape, 1)
    target = facts[:, 2:3]
    for j in range(1, 4):
        target = jnp.where((column & 3) == j, facts[:, 2 + j : 3 + j], target)
    foreground = jnp.where(label < CLS - 1, kept, 0.0)
    hot = ((column >> 2).astype(f32) == label) & (column < BOX)
    delta_slope = jnp.where(
        hot,
        jnp.clip(deltas - target, -1.0, 1.0) * (foreground * np.float32(1.0 / RPI)),
        0.0,
    )
    slopes = jnp.concatenate([logit_slope, delta_slope], axis=1).astype(bf16)
    slopes_ref[...] = slopes
    turned = (((1,), (1,)), ((), ()))
    act_grad = lax.dot_general(slopes, heads_ref[...], turned, preferred_element_type=f32)
    second_grad = (act_grad * second_slope_ref[...]).astype(bf16)
    second_grad_ref[...] = second_grad
    act_grad = lax.dot_general(second_grad, inner_ref[...], turned, preferred_element_type=f32)
    first_grad = (act_grad * first_slope_ref[...]).astype(bf16)
    first_grad_ref[...] = first_grad
    units = first_grad.shape[1]
    bias_ref[...] = jnp.zeros_like(bias_ref)
    bias_ref[0:1, :] = jnp.sum(first_grad.astype(f32), axis=0, keepdims=True)
    bias_ref[1:2, :] = jnp.sum(second_grad.astype(f32), axis=0, keepdims=True)
    bias_ref[2:3, : slopes.shape[1]] = jnp.sum(slopes.astype(f32), axis=0, keepdims=True)


def head_block(own, come, labels, ignore, targets, hidden_bias, inner, inner_bias, heads, heads_bias):
    count, units = own.shape
    wide = heads.shape[1]
    images = labels.shape[0]
    return pl.pallas_call(
        head_kernel,
        in_specs=[pl.BlockSpec(memory_space=pltpu.VMEM)] * 11,
        out_specs=[pl.BlockSpec(memory_space=pltpu.VMEM)] * 8,
        out_shape=[
            like((CLS, images, LANES), f32),
            like((images, BOX, LANES), f32),
            like((count, units), bf16),
            like((count, units), bf16),
            like((count, wide), bf16),
            like((count, units), bf16),
            like((count, units), bf16),
            like((8, units), f32),
        ],
        scratch_shapes=[pltpu.VMEM((count, units), f32)] * 2,
        compiler_params=pltpu.CompilerParams(vmem_limit_bytes=24 * 2**20),
        cost_estimate=LARGE_COST,
        name="head_block",
    )(own, *come, labels, ignore, targets, hidden_bias, inner, inner_bias, heads, heads_bias)


def maps_kernel(where, arrays, outs):
    maps_ref, by_class_ref, across_first_ref = arrays
    pick_ref = outs[-1]
    size, part = by_class_ref.shape[:2]
    images = maps_ref.shape[0]
    for way in range(size):
        pick_ref[way * part : (way + 1) * part, :] = by_class_ref[where[0] ^ way]
    for n in range(images):
        flat = lax.dot_general(
            pick_ref[...], maps_ref[n], (((1,), (1,)), ((), ())), preferred_element_type=f32
        ).astype(bf16)
        flat = jnp.dot(flat, across_first_ref[...], preferred_element_type=f32).astype(bf16)
        for way in range(size):
            outs[way][n * part : (n + 1) * part, :] = flat[way * part : (way + 1) * part]


def maps_back_kernel(where, arrays, outs):
    came_refs, (by_class_ref, across_first_ref) = arrays[:-2], arrays[-2:]
    out_ref, pick_ref, flat_ref = outs
    size, part = by_class_ref.shape[:2]
    for way in range(size):
        pick_ref[way * part : (way + 1) * part, :] = by_class_ref[where[0] ^ way]
    for n in range(out_ref.shape[0]):
        for way in range(size):
            flat_ref[way * part : (way + 1) * part, :] = came_refs[way][n]
        cells = lax.dot_general(
            across_first_ref[...], flat_ref[...], (((1,), (1,)), ((), ())), preferred_element_type=f32
        ).astype(bf16)
        out_ref[n] = jnp.dot(cells, pick_ref[...], preferred_element_type=f32)


def arrange_kernel(sizes, where, arrays, outs):
    height, width, part, level_count = sizes
    for n in range(outs[0].shape[0]):
        for x in range(width):
            for k, ref in enumerate(arrays):
                outs[0][n, x * part : (x + 1) * part, k * height : (k + 1) * height] = ref[
                    n * part : (n + 1) * part, x * height : (x + 1) * height
                ]


def arrange_back_kernel(sizes, where, arrays, outs):
    height, width, part, level_count = sizes
    for n in range(arrays[0].shape[0]):
        for x in range(width):
            for k, out in enumerate(outs):
                out[n, :, x * height : (x + 1) * height] = sum(
                    ref[n, x * part : (x + 1) * part, k * height : (k + 1) * height].astype(f32)
                    for ref in arrays
                ).astype(bf16)


def split_span_kernel(length, where, arrays, outs):
    weight_ref, extra_ref = arrays
    total_ref = outs[-1]
    span, size = outs[0].shape[0], len(outs) - 1
    shape = (total_ref.shape[0], weight_ref.shape[0])
    row = lax.broadcasted_iota(jnp.int32, shape, 0)
    column = lax.broadcasted_iota(jnp.int32, shape, 1)
    kind = sum((row >= k * span).astype(jnp.int32) for k in range(1, size))
    matrix = jnp.where(column == (row - kind * span) * size + kind, 1.0, 0.0).astype(bf16)
    total_ref[...] = jnp.dot(matrix, weight_ref[...], preferred_element_type=f32)
    for k in range(size):
        at = k * span + length
        total_ref[at : at + extra_ref.shape[0], :] = extra_ref[...]
    for way, out in enumerate(outs[:-1]):
        at = pl.multiple_of((where[0] ^ way) * span, 8)
        out[...] = total_ref[pl.ds(at, span), :].astype(bf16)


def join_span_kernel(where, arrays, outs):
    total_ref = outs[-1]
    span = arrays[1].shape[0]
    for way, ref in enumerate(arrays[1:]):
        at = pl.multiple_of((where[0] ^ way) * span, 8)
        total_ref[pl.ds(at, span), :] = ref[...].astype(f32)
    product = jnp.dot(arrays[0][...], total_ref[...].astype(bf16), preferred_element_type=f32)
    for out in outs[:-1]:
        out[...] = product.astype(out.dtype)


def return_span_kernel(where, arrays, outs):
    total_ref = outs[-1]
    span = outs[0].shape[0]
    piece = sum(ref[...].astype(f32) for ref in arrays[1:]).astype(bf16)
    total_ref[...] = jnp.dot(arrays[0][...], piece, preferred_element_type=f32)
    for way, out in enumerate(outs[:-1]):
        at = pl.multiple_of((where[0] ^ way) * span, 8)
        out[...] = total_ref[pl.ds(at, span), :].astype(bf16)


def picking(rows, columns, pairs):
    matrix = np.zeros((rows, columns), np.float32)
    for a, b in pairs:
        matrix[a, b] = 1.0
    return jnp.asarray(matrix, bf16)


def swap(array, axis, bit):
    size = lax.axis_size(axis)
    return lax.ppermute(array, axis, [(at, at ^ bit) for at in range(size)])


def exchange(array, axis):
    return lax.all_to_all(array, axis, split_axis=0, concat_axis=0, tiled=True)


def exchange_ways(arrays, axis):
    return [arrays[0]] + [swap(one, axis, way) for way, one in enumerate(arrays) if way]


def product_kernel(bits, parts, with_sum, where_ref, *refs):
    number = len(bits)
    grad_refs, crop_refs, refs = refs[:parts], refs[parts : 2 * parts], refs[2 * parts :]
    sign_ref, refs = refs[-1], refs[:-1]
    sign_ref[...] = jnp.zeros_like(sign_ref)
    outs = refs[-number:] if with_sum else [refs[-1].at[n] for n in range(number)]
    rows = crop_refs[0].shape[0] // 8
    for n in range(number):
        total = refs[0][n].astype(f32) if with_sum else 0.0
        at = pl.multiple_of((where_ref[1] ^ bits[n]) * rows, 16)
        for grad_ref, crop_ref in zip(grad_refs, crop_refs):
            total = total + jnp.dot(
                crop_ref[pl.ds(at, rows), :], grad_ref[...], preferred_element_type=f32
            )
        outs[n][...] = total.astype(bf16)


def piece_product(crops, grads, where, bits, come, earlier):
    features = crops[0].shape[0]
    units = grads[0].shape[1]
    rows = features // 8
    number = len(bits)
    with_sum = come is not None
    come = [come] if with_sum else []
    outs = (
        [like((rows, units), bf16)] * number if with_sum else [like((number, rows, units), bf16)]
    )
    return pl.pallas_call(
        functools.partial(product_kernel, bits, len(grads), with_sum),
        in_specs=[SCALAR]
        + [WHOLE for one in (*grads, *crops, *come)]
        + [FAR for one in earlier],
        out_specs=[WHOLE for one in (*outs, SIGN)],
        out_shape=[*outs, SIGN],
        compiler_params=pltpu.CompilerParams(vmem_limit_bytes=24 * 2**20),
        cost_estimate=LARGE_COST,
        name="piece_product",
    )(where, *grads, *crops, *come, *earlier)


def butterfly(array):
    for axis in ("img", "level"):
        bit = 1
        while bit < lax.axis_size(axis):
            array = array + swap(array, axis, bit)
            bit *= 2
    return array


def contract_rows(left_side, right_side):
    return lax.dot_general(
        left_side, right_side, (((0,), (0,)), ((), ())), preferred_element_type=f32
    )


def pack_rows(array):
    rows, units = array.shape[-2], array.shape[-1] // 3 * 2
    beside = array[..., units:]
    below = jnp.concatenate([beside[..., : rows // 2, :], beside[..., rows // 2 :, :]], axis=-1)
    return jnp.concatenate([array[..., :units], below], axis=-2)


def per_device(
    pyramid,
    levels,
    region_boxes,
    labels,
    crowd_ignore,
    targets,
    hidden_weight,
    hidden_bias,
    inner_weight,
    inner_bias,
    class_weight,
    class_bias,
    delta_weight,
    delta_bias,
):
    size = lax.axis_size("level")
    planes = lax.axis_size("img")
    z = lax.axis_index("level")
    where = jnp.stack([z, lax.axis_index("img")]).astype(jnp.int32)
    images, height, width, channels = pyramid.shape[1:]
    regions = levels.shape[1]
    part = channels // size
    sizes = (height, width, part, size)
    rows, units = hidden_weight.shape
    block_rows = images * regions
    direct = planes == 8 and rows % size == 0

    packed = jnp.concatenate(
        [
            jnp.transpose(region_boxes, (0, 2, 1)),
            jnp.transpose(levels, (0, 2, 1)),
            jnp.zeros((images, 3, regions), jnp.int32),
        ],
        axis=1,
    )
    class_room, delta_room = LANES, units // 2 - LANES
    small = jnp.concatenate(
        [
            inner_weight,
            jnp.pad(class_weight, ((0, 0), (0, class_room - CLS))),
            jnp.pad(delta_weight, ((0, 0), (0, delta_room - BOX))),
        ],
        axis=1,
    )
    heads_bias = jnp.concatenate(
        [
            jnp.pad(class_bias, (0, class_room - CLS)),
            jnp.pad(delta_bias, (0, delta_room - BOX)),
        ]
    )[None]

    if direct:
        length = rows // size
        span = -(-(length + images) // 8) * 8
        to_span = picking(
            size * span,
            rows,
            [(k * span + j, j * size + k) for k in range(size) for j in range(length)],
        )
        room = -(-rows // 16) * 16
        features = planes * room
        from_span = picking(
            room,
            size * span,
            [(k * length + j, k * span + j) for k in range(size) for j in range(length)],
        )
        total = [pltpu.VMEM((size * span, units), f32)]
        *sent, sign = call(
            functools.partial(split_span_kernel, length),
            [like((span, units), bf16)] * size,
            where,
            [hidden_weight, packed.astype(f32).reshape(images, units)],
            scratch=total,
            name="split_span",
        )
        came = exchange_ways(sent, "level")
        piece, own_piece, sign = call(
            join_span_kernel,
            [like((room, units), bf16)] * 2,
            where,
            [from_span, *came],
            scratch=total,
            name="join_span",
        )
        boxes = jnp.stack([one[length : length + images].reshape(images, 8, regions) for one in came])
        pieces = [own_piece] + [swap(piece, "img", bit) for bit in (2, 4, 6)]
        order = [k * planes + at for at in range(planes) for k in range(size)]
        table = runs_of(order, length, part, size, room)
    else:
        boxes = exchange(jnp.broadcast_to(packed[None], (size,) + packed.shape), "level")
        boxes = jnp.stack([lax.dynamic_index_in_dim(boxes, z ^ way, 0, False) for way in range(size)])
        features = BINS * part
        whole = lax.all_gather(hidden_weight, AXES, axis=0, tiled=True)
        weight = lax.dynamic_index_in_dim(whole.reshape(features, size, units), z, 1, False)
        table = runs_of([0], features, part, 1, features)
    row = jnp.arange(8)[:, None]
    boxes = jnp.where(row == 4, boxes.astype(jnp.int32) ^ z, boxes.astype(jnp.int32)).astype(f32)

    spots = height * width
    by_class = picking(
        channels, channels, [(c % size * part + c // size, c) for c in range(channels)]
    ).reshape(size, part, channels)
    across_first = picking(
        spots, spots, [(y * width + x, x * height + y) for y in range(height) for x in range(width)]
    )
    picks = [
        pltpu.VMEM((channels, channels), bf16),
        pltpu.VMEM((channels, spots), bf16),
    ]
    small_rows = small.shape[0] // 2 * 3
    maps = call(
        maps_kernel,
        [like((images * part, spots), bf16)] * size,
        where,
        [pyramid[0].reshape(images, spots, channels), by_class, across_first],
        scratch=picks[:1],
        name="maps",
    )[:size]
    if direct:
        maps = [maps[0], *tie(maps[1:], sign)]
    maps_came = exchange_ways(maps[:3], "level")
    maps_came.append(swap(tie([maps[3]], maps_came[1])[0], "level", 3))
    if direct:
        smalls = tie([pack_rows(small)], maps_came[3])[0]
    maps, sign = call(
        functools.partial(arrange_kernel, sizes),
        [pltpu.VMEM((images, width * part, size * height), bf16)],
        where,
        maps_came,
        name="arrange",
    )

    ways = (3, 2, 1, 0)
    crops = []
    came_sums = {}
    for turn, way in enumerate(ways):
        if turn == 0:
            crop, turned, sign = crop_block(table, sizes, features, boxes[way], maps)
            if direct:
                smalls, unused = pair_up((0, 0), where, smalls, [sign])
                own_piece = tie([own_piece], sign)[0]
                pieces = [own_piece, *pieces[1:]]
                pieces = sum(([one, swap(one, "img", 1)] for one in pieces), [])
                weight = gather_pieces(where, pieces)
            own, sign = multiply(turned, weight)
            relayed = swap(own, "level", 1)
        else:
            crop, own, sign = crop_block(
                table,
                sizes,
                features,
                boxes[way],
                maps,
                weight,
                bf16 if way == 1 else f32,
                [sign],
                SMALL_COST if way == 1 else LARGE_COST,
            )
        crops.append(crop)
        if way == 2:
            middle = own
            if direct:
                smalls, sign = pair_up((0, 1), where, smalls, [sign])
                smalls = smalls.reshape(size, small_rows, units)
                smalls = [swap(smalls, "img", bit) if bit else smalls for bit in (0, 2, 4, 6)]
        if way == 1:
            came_sums[1] = swap(own, "level", 1)
            middle, sign = call(
                add_kernel, [like(middle.shape, bf16)], where, [middle, relayed], [sign], name="add"
            )
            came_sums[2] = swap(middle, "level", 2)
            before = sign
    came_sums = [came_sums[2], came_sums[1]]

    if direct:
        smalls, unused = call(
            order_kernel,
            [like((4, size, small_rows, units), bf16)],
            where,
            smalls,
            [before],
            name="in_order",
        )
        full_inner, full_heads, sign = call(
            functools.partial(full_small_kernel, small.shape[0]),
            [pltpu.VMEM((units, units), bf16), pltpu.VMEM((units, units // 2), bf16)],
            where,
            [smalls, swap(smalls, "img", 1)],
            name="full_small",
        )
    else:
        smalls = lax.all_gather(small, AXES, axis=0, tiled=True)
        full_inner, full_heads = smalls[:, :units], smalls[:, units:]

    logits, deltas, first_act, second_act, slopes, second_grad, first_grad, bias_sums = head_block(
        own,
        came_sums,
        labels,
        crowd_ignore,
        jnp.transpose(targets, (0, 2, 1)),
        hidden_bias[None],
        full_inner,
        inner_bias[None],
        full_heads,
        heads_bias,
    )

    near = swap(first_grad, "level", 1)
    far = swap(first_grad, "level", 2)
    grad_of = {0: first_grad, 1: near}

    shares = []

    def take_up(way, earlier=()):
        share, sign = spread_block(table, sizes, boxes[way], grad_of[way], weight, earlier)
        shares.append(share)
        return sign

    if direct:
        count = small.shape[0]
        sent, kept, sign = small_product(
            where, count, first_act, second_grad, second_act, slopes, bias_sums
        )
        sign = take_up(0, [sign])
        *quarters, sign = quarter_rows(count, where, kept, swap(sent, "img", 1), [sign])
        quarters = [
            swap(one, "img", bit) if bit else one for one, bit in zip(quarters, (0, 2, 4, 6))
        ]
        grad_of[2] = tie([far], sign)[0]
        grad_of[3] = swap(grad_of[2], "level", 1)
        sign = take_up(1, [sign])
        sign = take_up(2, [sign])

        grads = [grad_of[way] for way in ways]
        parts, others = {}, {}

        def for_other(bits, sign):
            theirs = tuple(bit ^ 1 for bit in bits)
            products, sign = piece_product(crops, grads, where, theirs, None, [sign])
            others[bits] = swap(products, "img", 1)
            return sign

        def for_own(bits, sign):
            *own, sign = piece_product(crops, grads, where, bits, others[bits], [sign])
            for one, bit in zip(own, bits):
                parts[bit] = swap(one, "img", bit) if bit else one
            return sign

        sign = for_other((6,), sign)
        sign = for_other((2, 4), sign)
        sent, kept, sign = halve_rows((0, 1), 2, count, where, quarters, [sign])
        sign = for_own((6,), sign)
        sign = for_own((2, 4), sign)
        sign = for_other((0,), sign)
        sent, kept, sign = halve_rows(
            (0, 0), 1, count, where, [kept, swap(sent, "level", 2)], [sign]
        )
        sign = take_up(3, [sign])
        sign = for_own((0,), sign)
        inner_sum, class_sum, delta_sum, bias_total, sign = call(
            small_sum_kernel,
            [
                like((count, units), f32),
                like((count, CLS), f32),
                like((count, BOX), f32),
                like((8, units), f32),
            ],
            where,
            [kept, swap(sent, "level", 1)],
            [sign],
            name="small_sum",
            cost=SMALL_COST,
        )
        *back, sign = call(
            functools.partial(arrange_back_kernel, sizes),
            [like((images, part, spots), bf16)] * size,
            where,
            shares,
            [sign],
            name="arrange_back",
        )
        half, sign = call(
            add_kernel, [like(parts[0].shape, f32)], where, [parts[0], parts[6]], [sign], name="add", cost=SMALL_COST
        )
        back[3] = tie(back[3:], sign)[0]
        *out, sign = call(
            return_span_kernel,
            [like((span, units), bf16)] * size,
            where,
            [from_span.T, half, parts[2], parts[4]],
            [sign],
            scratch=total,
            name="return_span",
        )
    else:
        grad_of[2], grad_of[3] = far, swap(far, "level", 1)
        for way in range(size):
            take_up(way)
        *back, sign = call(
            functools.partial(arrange_back_kernel, sizes),
            [like((images, part, spots), bf16)] * size,
            where,
            shares,
            name="arrange_back",
        )
        bias_total = butterfly(bias_sums)
        small_sum = jnp.concatenate(
            [contract_rows(first_act, second_grad), contract_rows(second_act, slopes)], axis=1
        )
        small_sum = lax.psum_scatter(small_sum, AXES, scatter_dimension=0, tiled=True)
        inner_sum = small_sum[:, :units]
        class_sum = small_sum[:, units : units + CLS]
        delta_sum = small_sum[:, units + class_room : units + class_room + BOX]
        whole_grads = jnp.concatenate([grad_of[way] for way in ways])
        product = jnp.dot(
            jnp.concatenate(crops, axis=1), whole_grads, preferred_element_type=f32
        )
        own = (jnp.arange(size, dtype=jnp.int32) == z)[None, :, None]
        hidden_sum = lax.psum_scatter(
            jnp.where(own, product[:, None, :], 0.0).reshape(features * size, units),
            AXES,
            scatter_dimension=0,
            tiled=True,
        )

    map_grads, sign = call(
        maps_back_kernel,
        [like((images, spots, channels), f32)],
        where,
        [*exchange_ways(back, "level"), by_class, across_first],
        [sign],
        scratch=picks,
        name="maps_back",
    )
    map_grads = map_grads.reshape(1, images, height, width, channels)
    if direct:
        hidden_sum = call(
            join_span_kernel,
            [like((rows, units), f32)],
            where,
            [to_span.T, *exchange_ways(out, "level")],
            [sign],
            scratch=total,
            name="join_span",
        )[0]

    head_bias = bias_total[2, : class_room + delta_room]
    return (
        jnp.transpose(logits, (1, 2, 0)),
        jnp.transpose(deltas, (0, 2, 1)),
        map_grads,
        hidden_sum,
        bias_total[0],
        inner_sum,
        bias_total[1],
        class_sum,
        head_bias[:CLS],
        delta_sum,
        head_bias[class_room : class_room + BOX],
    )


def solution(mesh):
    return jax.shard_map(
        per_device,
        mesh=mesh,
        in_specs=(
            P("level", "img", None, None, None),
            P("img", "level", None),
            P("img", "level", None),
            P("img", "level"),
            P("img", "level"),
            P("img", "level", None),
            P(AXES, None),
            P(),
            P(AXES, None),
            P(),
            P(AXES, None),
            P(),
            P(AXES, None),
            P(),
        ),
        out_specs=(
            P("img", "level", None),
            P("img", "level", None),
            P("level", "img", None, None, None),
            P(AXES, None),
            P(),
            P(AXES, None),
            P(),
            P(AXES, None),
            P(),
            P(AXES, None),
            P(),
        ),
        check_vma=False,
    )
```

```python
import functools

import jax
import jax.numpy as jnp
import numpy as np
from jax import lax
from jax.experimental import pallas as pl
from jax.experimental.pallas import tpu as pltpu
from jax.sharding import PartitionSpec as P

POOL = 7
SAMPLES = 2
CLS = 81
BOX = 320
RPI = 512
BINS = POOL * POOL
LANES = 128
AXES = ("level", "img")
OFFSETS = (np.arange(SAMPLES * POOL, dtype=np.float32) + np.float32(0.5)) / np.float32(
    SAMPLES * POOL
)
SMALL_COST = pl.CostEstimate(flops=10**9, bytes_accessed=1, transcendentals=0)
LARGE_COST = pl.CostEstimate(flops=3 * 10**10, bytes_accessed=1, transcendentals=0)
f32 = jnp.float32
bf16 = jnp.bfloat16
FAR = pl.BlockSpec(memory_space=pl.ANY)
WHOLE = pl.BlockSpec(memory_space=pltpu.VMEM)
SCALAR = pl.BlockSpec(memory_space=pltpu.SMEM)
like = jax.ShapeDtypeStruct
SIGN = jax.ShapeDtypeStruct((8, LANES), jnp.float32)


def bin_weights(low, span, centres, at):
    first = jnp.maximum(1.0 - jnp.abs((low + OFFSETS[2 * at] * span) - centres), 0.0)
    second = jnp.maximum(1.0 - jnp.abs((low + OFFSETS[2 * at + 1] * span) - centres), 0.0)
    return ((first + second) * 0.5).astype(bf16)


def fill_weights(box_ref, down_ref, across_ref, height, width, level_count):
    x0, y0, x1, y1, level = [box_ref[k : k + 1, :] for k in range(5)]
    centres = lax.broadcasted_iota(jnp.int32, (width, LANES), 0).astype(f32)
    for q in range(POOL):
        across_ref[q] = bin_weights(x0, x1 - x0, centres, q).astype(across_ref.dtype)
    centres = lax.broadcasted_iota(jnp.int32, (height, LANES), 0).astype(f32)
    for p in range(POOL):
        weights = bin_weights(y0, y1 - y0, centres, p).astype(f32)
        for k in range(level_count):
            down_ref[k * height : (k + 1) * height, p * LANES : (p + 1) * LANES] = jnp.where(
                level == float(k), weights, 0.0
            ).astype(bf16)


def runs_of(order, length, part, group, room):
    place = {chunk: at // group * room + at % group * length for at, chunk in enumerate(order)}
    table = []
    for at in range(BINS):
        row, end, runs = at * part, (at + 1) * part, []
        while row < end:
            chunk = row // length
            stop = min(end, (chunk + 1) * length)
            runs.append((row - at * part, place[chunk] + row - chunk * length, stop - row))
            row = stop
        table.append(runs)
    return table


def gaps_of(table, features):
    held = sorted((kept, kept + count) for runs in table for row, kept, count in runs)
    gaps, last = [], 0
    for first, end in held + [(features, features)]:
        if first > last:
            gaps.append((last, first))
        last = end
    return gaps


def gather_kernel(number, where_ref, *refs):
    kept_ref, sems = refs[-2:]
    rows = refs[0].shape[0]
    copies = []
    for k, ref in enumerate(refs[:number]):
        at = pl.multiple_of((where_ref[1] ^ k) * rows, 16)
        copies.append(pltpu.make_async_copy(ref, kept_ref.at[pl.ds(at, rows)], sems.at[k]))
    for copy in copies:
        copy.start()
    for copy in copies:
        copy.wait()


def gather_pieces(where, pieces):
    rows, units = pieces[0].shape
    number = len(pieces)
    return pl.pallas_call(
        functools.partial(gather_kernel, number),
        in_specs=[SCALAR] + [FAR for one in pieces],
        out_specs=WHOLE,
        out_shape=pltpu.VMEM((number * rows, units), bf16),
        scratch_shapes=[pltpu.SemaphoreType.DMA((number,))],
        compiler_params=pltpu.CompilerParams(vmem_limit_bytes=24 * 2**20),
        cost_estimate=LARGE_COST,
        name="gather_pieces",
    )(where, *pieces)


def crop_kernel(table, sizes, product, box_ref, maps_ref, *refs):
    if product:
        weight_ref = refs[0]
        crop_ref, out_ref, sign_ref, down_ref, across_ref, sums_ref, rows_ref, turned_ref = refs[-8:]
    else:
        crop_ref, out_ref, sign_ref, down_ref, across_ref, sums_ref, rows_ref = refs[-7:]
    sign_ref[...] = jnp.zeros_like(sign_ref)
    height, width, part, level_count = sizes
    for first, end in gaps_of(table, rows_ref.shape[0]):
        rows_ref[first:end, :] = jnp.zeros((end - first, LANES), f32)
    fill_weights(box_ref, down_ref, across_ref, height, width, level_count)
    sums_ref[...] = jnp.dot(maps_ref[...], down_ref[...], preferred_element_type=f32).astype(
        sums_ref.dtype
    )
    for p in range(POOL):
        lanes = slice(p * LANES, (p + 1) * LANES)
        for start in range(0, POOL, 2):
            bins = range(start, min(POOL, start + 2))
            totals = [None for q in bins]
            for x in range(width):
                piece = sums_ref[x * part : (x + 1) * part, lanes]
                for at, q in enumerate(bins):
                    term = across_ref[q, x : x + 1, :] * piece
                    totals[at] = term if x == 0 else totals[at] + term
            for at, q in enumerate(bins):
                for row, kept, count in table[p * POOL + q]:
                    rows_ref[kept : kept + count, :] = totals[at][row : row + count].astype(f32)
    crop = rows_ref[...].astype(bf16)
    crop_ref[...] = crop
    if not product:
        out_ref[...] = crop.T
        return
    turned_ref[pl.ds(pl.multiple_of(pl.program_id(0) * LANES, LANES), LANES), :] = crop.T

    @pl.when(pl.program_id(0) == pl.num_programs(0) - 1)
    def multiply():
        out_ref[...] = jnp.dot(
            turned_ref[...], weight_ref[...], preferred_element_type=f32
        ).astype(out_ref.dtype)


def spread_kernel(table, sizes, box_ref, grad_ref, weight_ref, *refs):
    total_ref, sign_ref, down_ref, across_ref, sums_ref, rows_ref, crop_ref = refs[-7:]
    sign_ref[...] = jnp.zeros_like(sign_ref)
    height, width, part, level_count = sizes
    images = box_ref.shape[0]
    for n in range(images):
        fill_weights(
            box_ref.at[n], down_ref.at[n], across_ref.at[n], height, width, level_count
        )
    crop_ref[...] = lax.dot_general(
        weight_ref[...], grad_ref[...], (((1,), (1,)), ((), ())), preferred_element_type=f32
    ).astype(bf16)
    for n in range(images):
        rows_ref[...] = crop_ref[:, n * LANES : (n + 1) * LANES].astype(f32)
        for p in range(POOL):
            lanes = slice(p * LANES, (p + 1) * LANES)
            pieces = []
            for q in range(POOL):
                runs = [rows_ref[kept : kept + count, :] for row, kept, count in table[p * POOL + q]]
                runs = runs[0] if len(runs) == 1 else jnp.concatenate(runs, axis=0)
                pieces.append(runs.astype(bf16))
            for x in range(width):
                total = across_ref[n, 0, x : x + 1, :] * pieces[0]
                for q in range(1, POOL):
                    total = total + across_ref[n, q, x : x + 1, :] * pieces[q]
                sums_ref[x * part : (x + 1) * part, lanes] = total
        total_ref[n] = lax.dot_general(
            sums_ref[...], down_ref[n], (((1,), (1,)), ((), ())), preferred_element_type=f32
        ).astype(bf16)


def crop_block(table, sizes, features, boxes, maps, weight=None, out_type=bf16, earlier=(), cost=LARGE_COST, sum_type=bf16):
    height, width, part, level_count = sizes
    images = boxes.shape[0]
    product = weight is not None
    first = [boxes, maps] + ([weight] if product else [])
    rows = images * LANES
    if product:
        units = weight.shape[1]
        out_spec = pl.BlockSpec((rows, units), lambda n: (0, 0))
        out_shape = like((rows, units), out_type)
        more = [pltpu.VMEM((rows, features), bf16)]
    else:
        out_spec = pl.BlockSpec((LANES, features), lambda n: (n, 0))
        out_shape = like((rows, features), bf16)
        more = []
    return pl.pallas_call(
        functools.partial(crop_kernel, table, sizes, product),
        grid=(images,),
        in_specs=[
            pl.BlockSpec((None, 8, LANES), lambda n: (n, 0, 0)),
            pl.BlockSpec((None, width * part, level_count * height), lambda n: (n, 0, 0)),
        ]
        + [WHOLE for one in first[2:]]
        + [FAR for one in earlier],
        out_specs=[
            pl.BlockSpec((features, LANES), lambda n: (0, n)),
            out_spec,
            pl.BlockSpec((8, LANES), lambda n: (0, 0)),
        ],
        out_shape=[like((features, rows), bf16), out_shape, SIGN],
        scratch_shapes=[
            pltpu.VMEM((level_count * height, POOL * LANES), bf16),
            pltpu.VMEM((POOL, width, LANES), sum_type),
            pltpu.VMEM((width * part, POOL * LANES), sum_type),
            pltpu.VMEM((features, LANES), f32),
        ]
        + more,
        compiler_params=pltpu.CompilerParams(vmem_limit_bytes=24 * 2**20),
        cost_estimate=cost,
        name="crop_block",
    )(*first, *earlier)


def multiply_kernel(rows_ref, weight_ref, out_ref, sign_ref):
    out_ref[...] = jnp.dot(rows_ref[...], weight_ref[...], preferred_element_type=f32).astype(bf16)
    sign_ref[...] = jnp.zeros_like(sign_ref)


def multiply(rows, weight):
    return pl.pallas_call(
        multiply_kernel,
        in_specs=[WHOLE, WHOLE],
        out_specs=[WHOLE, WHOLE],
        out_shape=[like((rows.shape[0], weight.shape[1]), bf16), SIGN],
        compiler_params=pltpu.CompilerParams(vmem_limit_bytes=24 * 2**20),
        cost_estimate=LARGE_COST,
        name="multiply",
    )(rows, weight)


def spread_block(table, sizes, boxes, grads, weight, earlier=()):
    height, width, part, level_count = sizes
    images = boxes.shape[0]
    features = weight.shape[0]
    return pl.pallas_call(
        functools.partial(spread_kernel, table, sizes),
        in_specs=[WHOLE, WHOLE, WHOLE] + [FAR for one in earlier],
        out_specs=[WHOLE, WHOLE],
        out_shape=[like((images, width * part, level_count * height), bf16), SIGN],
        scratch_shapes=[
            pltpu.VMEM((images, level_count * height, POOL * LANES), bf16),
            pltpu.VMEM((images, POOL, width, LANES), bf16),
            pltpu.VMEM((width * part, POOL * LANES), bf16),
            pltpu.VMEM((features, LANES), f32),
            pltpu.VMEM((features, images * LANES), bf16),
        ],
        compiler_params=pltpu.CompilerParams(vmem_limit_bytes=24 * 2**20),
        cost_estimate=LARGE_COST,
        name="spread_block",
    )(boxes, grads, weight, *earlier)


def call(kernel, outs, where, arrays, earlier=(), scratch=(), name=None, cost=LARGE_COST):
    arrays = list(arrays)

    def body(*refs):
        end = 1 + len(arrays)
        later = refs[end + len(earlier) :]
        later[len(outs)][...] = jnp.zeros(SIGN.shape, SIGN.dtype)
        kernel(refs[0], refs[1:end], (*later[: len(outs)], *later[len(outs) + 1 :]))

    return pl.pallas_call(
        body,
        in_specs=[SCALAR] + [WHOLE for one in arrays] + [FAR for one in earlier],
        out_specs=[WHOLE for one in (*outs, SIGN)],
        out_shape=[*outs, SIGN],
        scratch_shapes=scratch,
        compiler_params=pltpu.CompilerParams(vmem_limit_bytes=24 * 2**20),
        cost_estimate=cost,
        name=name,
    )(where, *arrays, *earlier)


def tie_kernel(*refs):
    pass


def tie(arrays, *earlier):
    return pl.pallas_call(
        tie_kernel,
        in_specs=[FAR for one in (*arrays, *earlier)],
        out_specs=[FAR for one in arrays],
        out_shape=[like(one.shape, one.dtype) for one in arrays],
        input_output_aliases={k: k for k in range(len(arrays))},
        compiler_params=pltpu.CompilerParams(vmem_limit_bytes=2**20),
        cost_estimate=SMALL_COST,
        name="tie",
    )(*arrays, *earlier)


def add_kernel(where, arrays, outs):
    outs[0][...] = sum(ref[...].astype(f32) for ref in arrays).astype(outs[0].dtype)


def pair_kernel(bit, where, arrays, outs):
    own = (where[bit[0]] >> bit[1]) & 1
    outs[0][own] = arrays[0][...]
    outs[0][1 - own] = arrays[1][...]


def pair_up(bit, where, own, earlier):
    come = swap(own, AXES[bit[0]], 1 << bit[1])
    out = like((2,) + own.shape, own.dtype)
    return call(functools.partial(pair_kernel, bit), [out], where, [own, come], earlier, name="pair_up")


def order_kernel(where, arrays, outs):
    for k, ref in enumerate(arrays):
        outs[0][(where[1] >> 1) ^ k] = ref[...]


def full_small_kernel(rows, where, arrays, outs):
    units = outs[0].shape[1]
    for k, ref in enumerate(arrays):
        core = (where[1] & 1) ^ k
        for chip in range(4):
            for level in range(ref.shape[1]):
                at = pl.multiple_of(((level * 4 + chip) * 2 + core) * rows, rows)
                outs[0][pl.ds(at, rows), :] = ref[chip, level, :rows, :]
                for part in range(2):
                    outs[1][pl.ds(at + part * (rows // 2), rows // 2), :] = ref[
                        chip, level, rows:, part * (units // 2) : (part + 1) * (units // 2)
                    ]


def split_rows(own, inner, array, rows, sent, kept):
    step = inner * rows
    for at in range((kept.shape[0] - 16) // step):
        mine = pl.multiple_of((2 * at + own) * step, rows)
        other = pl.multiple_of((2 * at + 1 - own) * step, rows)
        kept[at * step : (at + 1) * step, :] = array[pl.ds(mine, step), :].astype(bf16)
        sent[at * step : (at + 1) * step, :] = array[pl.ds(other, step), :].astype(bf16)


def put_biases(biases, refs):
    high = biases.astype(bf16)
    low = (biases - high.astype(f32)).astype(bf16)
    for ref in refs:
        end = ref.shape[0]
        ref[end - 16 : end - 8, : high.shape[1]] = high
        ref[end - 8 : end, : high.shape[1]] = low


def get_biases(ref, units):
    end = ref.shape[0]
    last = ref[end - 16 :, :units].astype(f32)
    return last[:8] + last[8:]


def small_product_kernel(rows, where_ref, first_ref, second_grad_ref, second_ref, slopes_ref, bias_ref, sent_ref, kept_ref, sign_ref, total_ref):
    turned = (((0,), (0,)), ((), ()))
    units = first_ref.shape[1]
    total_ref[:, :units] = lax.dot_general(
        first_ref[...], second_grad_ref[...], turned, preferred_element_type=f32
    )
    total_ref[:, units:] = lax.dot_general(
        second_ref[...], slopes_ref[...], turned, preferred_element_type=f32
    )
    split_rows(where_ref[1] & 1, 1, total_ref, rows, sent_ref, kept_ref)
    put_biases(bias_ref[...], [sent_ref, kept_ref])
    sign_ref[...] = jnp.zeros_like(sign_ref)


def small_product(where, rows, first_act, second_grad, second_act, slopes, biases):
    units = first_act.shape[1]
    wide = units + slopes.shape[1]
    half = like((units // 2 + 16, wide), bf16)
    return pl.pallas_call(
        functools.partial(small_product_kernel, rows),
        in_specs=[SCALAR] + [WHOLE] * 5,
        out_specs=[WHOLE] * 3,
        out_shape=[half, half, SIGN],
        scratch_shapes=[pltpu.VMEM((units, wide), f32)],
        compiler_params=pltpu.CompilerParams(vmem_limit_bytes=24 * 2**20),
        cost_estimate=LARGE_COST,
        name="small_product",
    )(where, first_act, second_grad, second_act, slopes, biases)


def quarter_kernel(rows, where_ref, kept_ref, come_ref, *refs):
    outs, sign_ref, total_ref = refs[-6:-2], refs[-2], refs[-1]
    sign_ref[...] = jnp.zeros_like(sign_ref)
    count, units = total_ref.shape[0], total_ref.shape[1] // 3 * 2
    total_ref[...] = kept_ref[:count, :].astype(f32) + come_ref[:count, :].astype(f32)
    for k, out in enumerate(outs):
        for at in range(count // rows // 4):
            first = pl.multiple_of((4 * at + ((where_ref[1] >> 1) ^ k)) * rows, rows)
            out[at * rows : (at + 1) * rows, :] = total_ref[pl.ds(first, rows), :].astype(bf16)
    put_biases(get_biases(kept_ref, units) + get_biases(come_ref, units), outs)


def quarter_rows(rows, where, kept, come, earlier):
    count = kept.shape[0] - 16
    quarter = like((count // 4 + 16, kept.shape[1]), bf16)
    return pl.pallas_call(
        functools.partial(quarter_kernel, rows),
        in_specs=[SCALAR, WHOLE, WHOLE] + [FAR for one in earlier],
        out_specs=[WHOLE] * 5,
        out_shape=[quarter] * 4 + [SIGN],
        scratch_shapes=[pltpu.VMEM((count, kept.shape[1]), f32)],
        compiler_params=pltpu.CompilerParams(vmem_limit_bytes=24 * 2**20),
        cost_estimate=LARGE_COST,
        name="quarter_rows",
    )(where, kept, come, *earlier)


def halve_kernel(bit, inner, rows, where, arrays, outs):
    sent_out, kept_out, total_ref = outs
    count, units = total_ref.shape[0], total_ref.shape[1] // 3 * 2
    total_ref[...] = sum(ref[:count, :].astype(f32) for ref in arrays)
    split_rows((where[bit[0]] >> bit[1]) & 1, inner, total_ref, rows, sent_out, kept_out)
    biases = [get_biases(ref, units) for ref in arrays]
    while len(biases) > 1:
        biases = [biases[k] + biases[k + 1] for k in range(0, len(biases), 2)]
    put_biases(biases[0], [sent_out, kept_out])


def halve_rows(bit, inner, rows, where, arrays, earlier):
    count, wide = arrays[0].shape[0] - 16, arrays[0].shape[1]
    return call(
        functools.partial(halve_kernel, bit, inner, rows),
        [like((count // 2 + 16, wide), bf16)] * 2,
        where,
        arrays,
        earlier,
        [pltpu.VMEM((count, wide), f32)],
        name="halve_rows",
        cost=SMALL_COST,
    )


def small_sum_kernel(where, arrays, outs):
    rows, units = outs[0].shape
    total = sum(ref[:rows, :].astype(f32) for ref in arrays)
    outs[0][...] = total[:, :units]
    outs[1][...] = total[:, units : units + CLS]
    outs[2][...] = total[:, units + LANES : units + LANES + BOX]
    outs[3][...] = sum(get_biases(ref, units) for ref in arrays)


def gelu_and_slope(values):
    normal = 0.5 * (1.0 + lax.erf(values * np.float32(np.sqrt(0.5))))
    density = jnp.exp(-0.5 * values * values) * np.float32(1.0 / np.sqrt(2.0 * np.pi))
    return values * normal, normal + values * density


def head_kernel(
    own_ref, one_ref, two_ref, labels_ref, ignore_ref, targets_ref, hidden_bias_ref, inner_ref, inner_bias_ref, heads_ref, heads_bias_ref,
    logits_ref, deltas_ref, first_act_ref, second_act_ref, slopes_ref, second_grad_ref, first_grad_ref, bias_ref, first_slope_ref, second_slope_ref,
):
    first_pre = own_ref[...] + hidden_bias_ref[...]
    for come_ref in (one_ref, two_ref):
        first_pre = first_pre + come_ref[...].astype(f32)
    act, slope = gelu_and_slope(first_pre)
    first_slope_ref[...] = slope
    act = act.astype(bf16)
    first_act_ref[...] = act
    second_pre = jnp.dot(act, inner_ref[...], preferred_element_type=f32) + inner_bias_ref[...]
    act, slope = gelu_and_slope(second_pre)
    second_slope_ref[...] = slope
    act = act.astype(bf16)
    second_act_ref[...] = act
    heads = jnp.dot(act, heads_ref[...], preferred_element_type=f32) + heads_bias_ref[...]
    logits, deltas = heads[:, :LANES], heads[:, LANES:]
    facts = []
    for n in range(labels_ref.shape[0]):
        rows = slice(n * LANES, (n + 1) * LANES)
        logits_ref[:, n, :] = logits[rows].T[:CLS]
        deltas_ref[n] = deltas[rows].T[:BOX]
        fact = [labels_ref[n : n + 1, :].astype(f32), ignore_ref[n : n + 1, :].astype(f32)]
        fact += [targets_ref[n], jnp.zeros((2, LANES), f32)]
        facts.append(jnp.concatenate(fact, axis=0).T)
    facts = jnp.concatenate(facts, axis=0)
    label = facts[:, 0:1]
    kept = 1.0 - facts[:, 1:2]
    column = lax.broadcasted_iota(jnp.int32, logits.shape, 1)
    valid = column < CLS
    row_max = jnp.max(jnp.where(valid, logits, -jnp.inf), axis=1, keepdims=True)
    exponent = jnp.where(valid, jnp.exp(jnp.where(valid, logits - row_max, 0.0)), 0.0)
    softmax_rows = exponent / jnp.sum(exponent, axis=1, keepdims=True)
    hot = (column.astype(f32) == label).astype(f32)
    logit_slope = (softmax_rows - hot) * (kept * np.float32(1.0 / RPI))
    column = lax.broadcasted_iota(jnp.int32, deltas.shape, 1)
    target = facts[:, 2:3]
    for j in range(1, 4):
        target = jnp.where((column & 3) == j, facts[:, 2 + j : 3 + j], target)
    foreground = jnp.where(label < CLS - 1, kept, 0.0)
    hot = ((column >> 2).astype(f32) == label) & (column < BOX)
    delta_slope = jnp.where(
        hot,
        jnp.clip(deltas - target, -1.0, 1.0) * (foreground * np.float32(1.0 / RPI)),
        0.0,
    )
    slopes = jnp.concatenate([logit_slope, delta_slope], axis=1).astype(bf16)
    slopes_ref[...] = slopes
    turned = (((1,), (1,)), ((), ()))
    act_grad = lax.dot_general(slopes, heads_ref[...], turned, preferred_element_type=f32)
    second_grad = (act_grad * second_slope_ref[...]).astype(bf16)
    second_grad_ref[...] = second_grad
    act_grad = lax.dot_general(second_grad, inner_ref[...], turned, preferred_element_type=f32)
    first_grad = (act_grad * first_slope_ref[...]).astype(bf16)
    first_grad_ref[...] = first_grad
    units = first_grad.shape[1]
    bias_ref[...] = jnp.zeros_like(bias_ref)
    bias_ref[0:1, :] = jnp.sum(first_grad.astype(f32), axis=0, keepdims=True)
    bias_ref[1:2, :] = jnp.sum(second_grad.astype(f32), axis=0, keepdims=True)
    bias_ref[2:3, : slopes.shape[1]] = jnp.sum(slopes.astype(f32), axis=0, keepdims=True)


def head_block(own, come, labels, ignore, targets, hidden_bias, inner, inner_bias, heads, heads_bias):
    count, units = own.shape
    wide = heads.shape[1]
    images = labels.shape[0]
    return pl.pallas_call(
        head_kernel,
        in_specs=[pl.BlockSpec(memory_space=pltpu.VMEM)] * 11,
        out_specs=[pl.BlockSpec(memory_space=pltpu.VMEM)] * 8,
        out_shape=[
            like((CLS, images, LANES), f32),
            like((images, BOX, LANES), f32),
            like((count, units), bf16),
            like((count, units), bf16),
            like((count, wide), bf16),
            like((count, units), bf16),
            like((count, units), bf16),
            like((8, units), f32),
        ],
        scratch_shapes=[pltpu.VMEM((count, units), f32)] * 2,
        compiler_params=pltpu.CompilerParams(vmem_limit_bytes=24 * 2**20),
        cost_estimate=LARGE_COST,
        name="head_block",
    )(own, *come, labels, ignore, targets, hidden_bias, inner, inner_bias, heads, heads_bias)


def maps_kernel(where, arrays, outs):
    maps_ref, by_class_ref, across_first_ref = arrays
    pick_ref = outs[-1]
    size, part = by_class_ref.shape[:2]
    images = maps_ref.shape[0]
    for way in range(size):
        pick_ref[way * part : (way + 1) * part, :] = by_class_ref[where[0] ^ way]
    for n in range(images):
        flat = lax.dot_general(
            pick_ref[...], maps_ref[n], (((1,), (1,)), ((), ())), preferred_element_type=f32
        ).astype(bf16)
        flat = jnp.dot(flat, across_first_ref[...], preferred_element_type=f32).astype(bf16)
        for way in range(size):
            outs[way][n * part : (n + 1) * part, :] = flat[way * part : (way + 1) * part]


def maps_back_kernel(where, arrays, outs):
    came_refs, (by_class_ref, across_first_ref) = arrays[:-2], arrays[-2:]
    out_ref, pick_ref, flat_ref = outs
    size, part = by_class_ref.shape[:2]
    for way in range(size):
        pick_ref[way * part : (way + 1) * part, :] = by_class_ref[where[0] ^ way]
    for n in range(out_ref.shape[0]):
        for way in range(size):
            flat_ref[way * part : (way + 1) * part, :] = came_refs[way][n]
        cells = lax.dot_general(
            across_first_ref[...], flat_ref[...], (((1,), (1,)), ((), ())), preferred_element_type=f32
        ).astype(bf16)
        out_ref[n] = jnp.dot(cells, pick_ref[...], preferred_element_type=f32)


def arrange_kernel(sizes, where, arrays, outs):
    height, width, part, level_count = sizes
    for n in range(outs[0].shape[0]):
        for x in range(width):
            for k, ref in enumerate(arrays):
                outs[0][n, x * part : (x + 1) * part, k * height : (k + 1) * height] = ref[
                    n * part : (n + 1) * part, x * height : (x + 1) * height
                ]


def arrange_back_kernel(sizes, where, arrays, outs):
    height, width, part, level_count = sizes
    for n in range(arrays[0].shape[0]):
        for x in range(width):
            for k, out in enumerate(outs):
                out[n, :, x * height : (x + 1) * height] = sum(
                    ref[n, x * part : (x + 1) * part, k * height : (k + 1) * height].astype(f32)
                    for ref in arrays
                ).astype(bf16)


def split_span_kernel(length, where, arrays, outs):
    weight_ref, extra_ref = arrays
    total_ref = outs[-1]
    span, size = outs[0].shape[0], len(outs) - 1
    shape = (total_ref.shape[0], weight_ref.shape[0])
    row = lax.broadcasted_iota(jnp.int32, shape, 0)
    column = lax.broadcasted_iota(jnp.int32, shape, 1)
    kind = sum((row >= k * span).astype(jnp.int32) for k in range(1, size))
    matrix = jnp.where(column == (row - kind * span) * size + kind, 1.0, 0.0).astype(bf16)
    total_ref[...] = jnp.dot(matrix, weight_ref[...], preferred_element_type=f32)
    for k in range(size):
        at = k * span + length
        total_ref[at : at + extra_ref.shape[0], :] = extra_ref[...]
    for way, out in enumerate(outs[:-1]):
        at = pl.multiple_of((where[0] ^ way) * span, 8)
        out[...] = total_ref[pl.ds(at, span), :].astype(bf16)


def join_span_kernel(where, arrays, outs):
    total_ref = outs[-1]
    span = arrays[1].shape[0]
    for way, ref in enumerate(arrays[1:]):
        at = pl.multiple_of((where[0] ^ way) * span, 8)
        total_ref[pl.ds(at, span), :] = ref[...].astype(f32)
    product = jnp.dot(arrays[0][...], total_ref[...].astype(bf16), preferred_element_type=f32)
    for out in outs[:-1]:
        out[...] = product.astype(out.dtype)


def return_span_kernel(where, arrays, outs):
    total_ref = outs[-1]
    span = outs[0].shape[0]
    piece = sum(ref[...].astype(f32) for ref in arrays[1:]).astype(bf16)
    total_ref[...] = jnp.dot(arrays[0][...], piece, preferred_element_type=f32)
    for way, out in enumerate(outs[:-1]):
        at = pl.multiple_of((where[0] ^ way) * span, 8)
        out[...] = total_ref[pl.ds(at, span), :].astype(bf16)


def picking(rows, columns, pairs):
    matrix = np.zeros((rows, columns), np.float32)
    for a, b in pairs:
        matrix[a, b] = 1.0
    return jnp.asarray(matrix, bf16)


def swap(array, axis, bit):
    size = lax.axis_size(axis)
    return lax.ppermute(array, axis, [(at, at ^ bit) for at in range(size)])


def exchange(array, axis):
    return lax.all_to_all(array, axis, split_axis=0, concat_axis=0, tiled=True)


def exchange_ways(arrays, axis):
    return [arrays[0]] + [swap(one, axis, way) for way, one in enumerate(arrays) if way]


def product_kernel(bits, parts, with_sum, where_ref, *refs):
    number = len(bits)
    grad_refs, crop_refs, refs = refs[:parts], refs[parts : 2 * parts], refs[2 * parts :]
    sign_ref, refs = refs[-1], refs[:-1]
    sign_ref[...] = jnp.zeros_like(sign_ref)
    outs = refs[-number:] if with_sum else [refs[-1].at[n] for n in range(number)]
    rows = crop_refs[0].shape[0] // 8
    for n in range(number):
        total = refs[0][n].astype(f32) if with_sum else 0.0
        at = pl.multiple_of((where_ref[1] ^ bits[n]) * rows, 16)
        for grad_ref, crop_ref in zip(grad_refs, crop_refs):
            total = total + jnp.dot(
                crop_ref[pl.ds(at, rows), :], grad_ref[...], preferred_element_type=f32
            )
        outs[n][...] = total.astype(bf16)


def piece_product(crops, grads, where, bits, come, earlier):
    features = crops[0].shape[0]
    units = grads[0].shape[1]
    rows = features // 8
    number = len(bits)
    with_sum = come is not None
    come = [come] if with_sum else []
    outs = (
        [like((rows, units), bf16)] * number if with_sum else [like((number, rows, units), bf16)]
    )
    return pl.pallas_call(
        functools.partial(product_kernel, bits, len(grads), with_sum),
        in_specs=[SCALAR]
        + [WHOLE for one in (*grads, *crops, *come)]
        + [FAR for one in earlier],
        out_specs=[WHOLE for one in (*outs, SIGN)],
        out_shape=[*outs, SIGN],
        compiler_params=pltpu.CompilerParams(vmem_limit_bytes=24 * 2**20),
        cost_estimate=LARGE_COST,
        name="piece_product",
    )(where, *grads, *crops, *come, *earlier)


def butterfly(array):
    for axis in ("img", "level"):
        bit = 1
        while bit < lax.axis_size(axis):
            array = array + swap(array, axis, bit)
            bit *= 2
    return array


def contract_rows(left_side, right_side):
    return lax.dot_general(
        left_side, right_side, (((0,), (0,)), ((), ())), preferred_element_type=f32
    )


def pack_rows(array):
    rows, units = array.shape[-2], array.shape[-1] // 3 * 2
    beside = array[..., units:]
    below = jnp.concatenate([beside[..., : rows // 2, :], beside[..., rows // 2 :, :]], axis=-1)
    return jnp.concatenate([array[..., :units], below], axis=-2)


def per_device(
    pyramid,
    levels,
    region_boxes,
    labels,
    crowd_ignore,
    targets,
    hidden_weight,
    hidden_bias,
    inner_weight,
    inner_bias,
    class_weight,
    class_bias,
    delta_weight,
    delta_bias,
):
    size = lax.axis_size("level")
    planes = lax.axis_size("img")
    z = lax.axis_index("level")
    where = jnp.stack([z, lax.axis_index("img")]).astype(jnp.int32)
    images, height, width, channels = pyramid.shape[1:]
    regions = levels.shape[1]
    part = channels // size
    sizes = (height, width, part, size)
    rows, units = hidden_weight.shape
    block_rows = images * regions
    direct = planes == 8 and rows % size == 0

    packed = jnp.concatenate(
        [
            jnp.transpose(region_boxes, (0, 2, 1)),
            jnp.transpose(levels, (0, 2, 1)),
            jnp.zeros((images, 3, regions), jnp.int32),
        ],
        axis=1,
    )
    class_room, delta_room = LANES, units // 2 - LANES
    small = jnp.concatenate(
        [
            inner_weight,
            jnp.pad(class_weight, ((0, 0), (0, class_room - CLS))),
            jnp.pad(delta_weight, ((0, 0), (0, delta_room - BOX))),
        ],
        axis=1,
    )
    heads_bias = jnp.concatenate(
        [
            jnp.pad(class_bias, (0, class_room - CLS)),
            jnp.pad(delta_bias, (0, delta_room - BOX)),
        ]
    )[None]

    if direct:
        length = rows // size
        span = -(-(length + images) // 8) * 8
        to_span = picking(
            size * span,
            rows,
            [(k * span + j, j * size + k) for k in range(size) for j in range(length)],
        )
        room = -(-rows // 16) * 16
        features = planes * room
        from_span = picking(
            room,
            size * span,
            [(k * length + j, k * span + j) for k in range(size) for j in range(length)],
        )
        total = [pltpu.VMEM((size * span, units), f32)]
        *sent, sign = call(
            functools.partial(split_span_kernel, length),
            [like((span, units), bf16)] * size,
            where,
            [hidden_weight, packed.astype(f32).reshape(images, units)],
            scratch=total,
            name="split_span",
        )
        came = exchange_ways(sent, "level")
        piece, own_piece, sign = call(
            join_span_kernel,
            [like((room, units), bf16)] * 2,
            where,
            [from_span, *came],
            scratch=total,
            name="join_span",
        )
        boxes = jnp.stack([one[length : length + images].reshape(images, 8, regions) for one in came])
        pieces = [own_piece] + [swap(piece, "img", bit) for bit in (2, 4, 6)]
        order = [k * planes + at for at in range(planes) for k in range(size)]
        table = runs_of(order, length, part, size, room)
    else:
        boxes = exchange(jnp.broadcast_to(packed[None], (size,) + packed.shape), "level")
        boxes = jnp.stack([lax.dynamic_index_in_dim(boxes, z ^ way, 0, False) for way in range(size)])
        features = BINS * part
        whole = lax.all_gather(hidden_weight, AXES, axis=0, tiled=True)
        weight = lax.dynamic_index_in_dim(whole.reshape(features, size, units), z, 1, False)
        table = runs_of([0], features, part, 1, features)
    row = jnp.arange(8)[:, None]
    boxes = jnp.where(row == 4, boxes.astype(jnp.int32) ^ z, boxes.astype(jnp.int32)).astype(f32)

    spots = height * width
    by_class = picking(
        channels, channels, [(c % size * part + c // size, c) for c in range(channels)]
    ).reshape(size, part, channels)
    across_first = picking(
        spots, spots, [(y * width + x, x * height + y) for y in range(height) for x in range(width)]
    )
    picks = [
        pltpu.VMEM((channels, channels), bf16),
        pltpu.VMEM((channels, spots), bf16),
    ]
    small_rows = small.shape[0] // 2 * 3
    maps = call(
        maps_kernel,
        [like((images * part, spots), bf16)] * size,
        where,
        [pyramid[0].reshape(images, spots, channels), by_class, across_first],
        scratch=picks[:1],
        name="maps",
    )[:size]
    if direct:
        maps = [maps[0], *tie(maps[1:], sign)]
    maps_came = exchange_ways(maps[:3], "level")
    maps_came.append(swap(tie([maps[3]], maps_came[1])[0], "level", 3))
    if direct:
        smalls = tie([pack_rows(small)], maps_came[3])[0]
    maps, sign = call(
        functools.partial(arrange_kernel, sizes),
        [pltpu.VMEM((images, width * part, size * height), bf16)],
        where,
        maps_came,
        name="arrange",
    )

    ways = (3, 2, 1, 0)
    crops = []
    came_sums = {}
    for turn, way in enumerate(ways):
        if turn == 0:
            crop, turned, sign = crop_block(table, sizes, features, boxes[way], maps)
            if direct:
                smalls, unused = pair_up((0, 0), where, smalls, [sign])
                own_piece = tie([own_piece], sign)[0]
                pieces = [own_piece, *pieces[1:]]
                pieces = sum(([one, swap(one, "img", 1)] for one in pieces), [])
                weight = gather_pieces(where, pieces)
            own, sign = multiply(turned, weight)
            relayed = swap(own, "level", 1)
        else:
            crop, own, sign = crop_block(
                table,
                sizes,
                features,
                boxes[way],
                maps,
                weight,
                bf16 if way == 1 else f32,
                [sign],
                SMALL_COST if way == 1 else LARGE_COST,
                bf16 if way else f32,
            )
        crops.append(crop)
        if way == 2:
            middle = own
            if direct:
                smalls, sign = pair_up((0, 1), where, smalls, [sign])
                smalls = smalls.reshape(size, small_rows, units)
                smalls = [swap(smalls, "img", bit) if bit else smalls for bit in (0, 2, 4, 6)]
        if way == 1:
            came_sums[1] = swap(own, "level", 1)
            middle, sign = call(
                add_kernel, [like(middle.shape, bf16)], where, [middle, relayed], [sign], name="add"
            )
            came_sums[2] = swap(middle, "level", 2)
            before = sign
    came_sums = [came_sums[2], came_sums[1]]

    if direct:
        smalls, unused = call(
            order_kernel,
            [like((4, size, small_rows, units), bf16)],
            where,
            smalls,
            [before],
            name="in_order",
        )
        full_inner, full_heads, sign = call(
            functools.partial(full_small_kernel, small.shape[0]),
            [pltpu.VMEM((units, units), bf16), pltpu.VMEM((units, units // 2), bf16)],
            where,
            [smalls, swap(smalls, "img", 1)],
            name="full_small",
        )
    else:
        smalls = lax.all_gather(small, AXES, axis=0, tiled=True)
        full_inner, full_heads = smalls[:, :units], smalls[:, units:]

    logits, deltas, first_act, second_act, slopes, second_grad, first_grad, bias_sums = head_block(
        own,
        came_sums,
        labels,
        crowd_ignore,
        jnp.transpose(targets, (0, 2, 1)),
        hidden_bias[None],
        full_inner,
        inner_bias[None],
        full_heads,
        heads_bias,
    )

    near = swap(first_grad, "level", 1)
    far = swap(first_grad, "level", 2)
    grad_of = {0: first_grad, 1: near}

    shares = []

    def take_up(way, earlier=()):
        share, sign = spread_block(table, sizes, boxes[way], grad_of[way], weight, earlier)
        shares.append(share)
        return sign

    if direct:
        count = small.shape[0]
        sent, kept, sign = small_product(
            where, count, first_act, second_grad, second_act, slopes, bias_sums
        )
        sign = take_up(0, [sign])
        *quarters, sign = quarter_rows(count, where, kept, swap(sent, "img", 1), [sign])
        quarters = [
            swap(one, "img", bit) if bit else one for one, bit in zip(quarters, (0, 2, 4, 6))
        ]
        grad_of[2] = tie([far], sign)[0]
        grad_of[3] = swap(grad_of[2], "level", 1)
        sign = take_up(1, [sign])
        sign = take_up(2, [sign])

        grads = [grad_of[way] for way in ways]
        parts, others = {}, {}

        def for_other(bits, sign):
            theirs = tuple(bit ^ 1 for bit in bits)
            products, sign = piece_product(crops, grads, where, theirs, None, [sign])
            others[bits] = swap(products, "img", 1)
            return sign

        def for_own(bits, sign):
            *own, sign = piece_product(crops, grads, where, bits, others[bits], [sign])
            for one, bit in zip(own, bits):
                parts[bit] = swap(one, "img", bit) if bit else one
            return sign

        sign = for_other((6,), sign)
        sign = for_other((2, 4, 0), sign)
        sign = for_own((6,), sign)
        sent, kept, sign = halve_rows((0, 1), 2, count, where, quarters, [sign])
        sign = for_own((2, 4, 0), sign)
        sign = take_up(3, [sign])
        sent, kept, sign = halve_rows(
            (0, 0), 1, count, where, [kept, swap(sent, "level", 2)], [sign]
        )
        *back, sign = call(
            functools.partial(arrange_back_kernel, sizes),
            [like((images, part, spots), bf16)] * size,
            where,
            shares,
            [sign],
            name="arrange_back",
        )
        inner_sum, class_sum, delta_sum, bias_total, sign = call(
            small_sum_kernel,
            [
                like((count, units), f32),
                like((count, CLS), f32),
                like((count, BOX), f32),
                like((8, units), f32),
            ],
            where,
            [kept, swap(sent, "level", 1)],
            [sign],
            name="small_sum",
            cost=SMALL_COST,
        )
        back[3] = tie(back[3:], sign)[0]
        half, sign = call(
            add_kernel, [like(parts[0].shape, f32)], where, [parts[0], parts[6]], [sign], name="add", cost=SMALL_COST
        )
        back[1] = tie(back[1:2], sign)[0]
        *out, sign = call(
            return_span_kernel,
            [like((span, units), bf16)] * size,
            where,
            [from_span.T, half, parts[2], parts[4]],
            [sign],
            scratch=total,
            name="return_span",
        )
    else:
        grad_of[2], grad_of[3] = far, swap(far, "level", 1)
        for way in range(size):
            take_up(way)
        *back, sign = call(
            functools.partial(arrange_back_kernel, sizes),
            [like((images, part, spots), bf16)] * size,
            where,
            shares,
            name="arrange_back",
        )
        bias_total = butterfly(bias_sums)
        small_sum = jnp.concatenate(
            [contract_rows(first_act, second_grad), contract_rows(second_act, slopes)], axis=1
        )
        small_sum = lax.psum_scatter(small_sum, AXES, scatter_dimension=0, tiled=True)
        inner_sum = small_sum[:, :units]
        class_sum = small_sum[:, units : units + CLS]
        delta_sum = small_sum[:, units + class_room : units + class_room + BOX]
        whole_grads = jnp.concatenate([grad_of[way] for way in ways])
        product = jnp.dot(
            jnp.concatenate(crops, axis=1), whole_grads, preferred_element_type=f32
        )
        own = (jnp.arange(size, dtype=jnp.int32) == z)[None, :, None]
        hidden_sum = lax.psum_scatter(
            jnp.where(own, product[:, None, :], 0.0).reshape(features * size, units),
            AXES,
            scatter_dimension=0,
            tiled=True,
        )

    map_grads, sign = call(
        maps_back_kernel,
        [like((images, spots, channels), f32)],
        where,
        [*exchange_ways(back, "level"), by_class, across_first],
        [sign],
        scratch=picks,
        name="maps_back",
    )
    map_grads = map_grads.reshape(1, images, height, width, channels)
    if direct:
        hidden_sum = call(
            join_span_kernel,
            [like((rows, units), f32)],
            where,
            [to_span.T, *exchange_ways(out, "level")],
            [sign],
            scratch=total,
            name="join_span",
        )[0]

    head_bias = bias_total[2, : class_room + delta_room]
    return (
        jnp.transpose(logits, (1, 2, 0)),
        jnp.transpose(deltas, (0, 2, 1)),
        map_grads,
        hidden_sum,
        bias_total[0],
        inner_sum,
        bias_total[1],
        class_sum,
        head_bias[:CLS],
        delta_sum,
        head_bias[class_room : class_room + BOX],
    )


def solution(mesh):
    return jax.shard_map(
        per_device,
        mesh=mesh,
        in_specs=(
            P("level", "img", None, None, None),
            P("img", "level", None),
            P("img", "level", None),
            P("img", "level"),
            P("img", "level"),
            P("img", "level", None),
            P(AXES, None),
            P(),
            P(AXES, None),
            P(),
            P(AXES, None),
            P(),
            P(AXES, None),
            P(),
        ),
        out_specs=(
            P("img", "level", None),
            P("img", "level", None),
            P("level", "img", None, None, None),
            P(AXES, None),
            P(),
            P(AXES, None),
            P(),
            P(AXES, None),
            P(),
            P(AXES, None),
            P(),
        ),
        check_vma=False,
    )
```

```python
import functools

import jax
import jax.numpy as jnp
import numpy as np
from jax import lax
from jax.experimental import pallas as pl
from jax.experimental.pallas import tpu as pltpu
from jax.sharding import PartitionSpec as P

POOL = 7
SAMPLES = 2
CLS = 81
BOX = 320
RPI = 512
BINS = POOL * POOL
LANES = 128
AXES = ("level", "img")
OFFSETS = (np.arange(SAMPLES * POOL, dtype=np.float32) + np.float32(0.5)) / np.float32(
    SAMPLES * POOL
)
SMALL_COST = pl.CostEstimate(flops=10**9, bytes_accessed=1, transcendentals=0)
TINY_COST = pl.CostEstimate(flops=1, bytes_accessed=1, transcendentals=0)
LARGE_COST = pl.CostEstimate(flops=3 * 10**10, bytes_accessed=1, transcendentals=0)
f32 = jnp.float32
bf16 = jnp.bfloat16
FAR = pl.BlockSpec(memory_space=pl.ANY)
WHOLE = pl.BlockSpec(memory_space=pltpu.VMEM)
SCALAR = pl.BlockSpec(memory_space=pltpu.SMEM)
like = jax.ShapeDtypeStruct
SIGN = jax.ShapeDtypeStruct((8, LANES), jnp.float32)


def bin_weights(low, span, centres, at):
    first = jnp.maximum(1.0 - jnp.abs((low + OFFSETS[2 * at] * span) - centres), 0.0)
    second = jnp.maximum(1.0 - jnp.abs((low + OFFSETS[2 * at + 1] * span) - centres), 0.0)
    return ((first + second) * 0.5).astype(bf16)


def fill_weights(box_ref, down_ref, across_ref, height, width, level_count):
    x0, y0, x1, y1, level = [box_ref[k : k + 1, :] for k in range(5)]
    centres = lax.broadcasted_iota(jnp.int32, (width, LANES), 0).astype(f32)
    for q in range(POOL):
        across_ref[q] = bin_weights(x0, x1 - x0, centres, q).astype(across_ref.dtype)
    centres = lax.broadcasted_iota(jnp.int32, (height, LANES), 0).astype(f32)
    for p in range(POOL):
        weights = bin_weights(y0, y1 - y0, centres, p).astype(f32)
        for k in range(level_count):
            down_ref[k * height : (k + 1) * height, p * LANES : (p + 1) * LANES] = jnp.where(
                level == float(k), weights, 0.0
            ).astype(bf16)


def runs_of(order, length, part, group, room):
    place = {chunk: at // group * room + at % group * length for at, chunk in enumerate(order)}
    table = []
    for at in range(BINS):
        row, end, runs = at * part, (at + 1) * part, []
        while row < end:
            chunk = row // length
            stop = min(end, (chunk + 1) * length)
            runs.append((row - at * part, place[chunk] + row - chunk * length, stop - row))
            row = stop
        table.append(runs)
    return table


def gaps_of(table, features):
    held = sorted((kept, kept + count) for runs in table for row, kept, count in runs)
    gaps, last = [], 0
    for first, end in held + [(features, features)]:
        if first > last:
            gaps.append((last, first))
        last = end
    return gaps


def gather_kernel(number, where_ref, *refs):
    kept_ref, sems = refs[-2:]
    rows = refs[0].shape[0]
    copies = []
    for k, ref in enumerate(refs[:number]):
        at = pl.multiple_of((where_ref[1] ^ k) * rows, 16)
        copies.append(pltpu.make_async_copy(ref, kept_ref.at[pl.ds(at, rows)], sems.at[k]))
    for copy in copies:
        copy.start()
    for copy in copies:
        copy.wait()


def gather_pieces(where, pieces):
    rows, units = pieces[0].shape
    number = len(pieces)
    return pl.pallas_call(
        functools.partial(gather_kernel, number),
        in_specs=[SCALAR] + [FAR for one in pieces],
        out_specs=WHOLE,
        out_shape=pltpu.VMEM((number * rows, units), bf16),
        scratch_shapes=[pltpu.SemaphoreType.DMA((number,))],
        compiler_params=pltpu.CompilerParams(vmem_limit_bytes=24 * 2**20),
        cost_estimate=LARGE_COST,
        name="gather_pieces",
    )(where, *pieces)


def crop_kernel(table, sizes, product, box_ref, maps_ref, *refs):
    if product:
        weight_ref = refs[0]
        crop_ref, out_ref, sign_ref, down_ref, across_ref, sums_ref, rows_ref, turned_ref = refs[-8:]
    else:
        crop_ref, out_ref, sign_ref, down_ref, across_ref, sums_ref, rows_ref = refs[-7:]
    sign_ref[...] = jnp.zeros_like(sign_ref)
    height, width, part, level_count = sizes
    for first, end in gaps_of(table, rows_ref.shape[0]):
        rows_ref[first:end, :] = jnp.zeros((end - first, LANES), f32)
    fill_weights(box_ref, down_ref, across_ref, height, width, level_count)
    sums_ref[...] = jnp.dot(maps_ref[...], down_ref[...], preferred_element_type=f32).astype(
        sums_ref.dtype
    )
    for p in range(POOL):
        lanes = slice(p * LANES, (p + 1) * LANES)
        for start in range(0, POOL, 2):
            bins = range(start, min(POOL, start + 2))
            totals = [None for q in bins]
            for x in range(width):
                piece = sums_ref[x * part : (x + 1) * part, lanes]
                for at, q in enumerate(bins):
                    term = across_ref[q, x : x + 1, :] * piece
                    totals[at] = term if x == 0 else totals[at] + term
            for at, q in enumerate(bins):
                for row, kept, count in table[p * POOL + q]:
                    rows_ref[kept : kept + count, :] = totals[at][row : row + count].astype(f32)
    crop = rows_ref[...].astype(bf16)
    crop_ref[...] = crop
    if not product:
        out_ref[...] = crop.T
        return
    turned_ref[pl.ds(pl.multiple_of(pl.program_id(0) * LANES, LANES), LANES), :] = crop.T

    @pl.when(pl.program_id(0) == pl.num_programs(0) - 1)
    def multiply():
        out_ref[...] = jnp.dot(
            turned_ref[...], weight_ref[...], preferred_element_type=f32
        ).astype(out_ref.dtype)


def spread_kernel(table, sizes, box_ref, grad_ref, weight_ref, *refs):
    total_ref, sign_ref, down_ref, across_ref, sums_ref, rows_ref, crop_ref = refs[-7:]
    sign_ref[...] = jnp.zeros_like(sign_ref)
    height, width, part, level_count = sizes
    images = box_ref.shape[0]
    for n in range(images):
        fill_weights(
            box_ref.at[n], down_ref.at[n], across_ref.at[n], height, width, level_count
        )
    crop_ref[...] = lax.dot_general(
        weight_ref[...], grad_ref[...], (((1,), (1,)), ((), ())), preferred_element_type=f32
    ).astype(bf16)
    for n in range(images):
        rows_ref[...] = crop_ref[:, n * LANES : (n + 1) * LANES].astype(f32)
        for p in range(POOL):
            lanes = slice(p * LANES, (p + 1) * LANES)
            pieces = []
            for q in range(POOL):
                runs = [rows_ref[kept : kept + count, :] for row, kept, count in table[p * POOL + q]]
                runs = runs[0] if len(runs) == 1 else jnp.concatenate(runs, axis=0)
                pieces.append(runs.astype(bf16))
            for x in range(width):
                total = across_ref[n, 0, x : x + 1, :] * pieces[0]
                for q in range(1, POOL):
                    total = total + across_ref[n, q, x : x + 1, :] * pieces[q]
                sums_ref[x * part : (x + 1) * part, lanes] = total
        total_ref[n] = lax.dot_general(
            sums_ref[...], down_ref[n], (((1,), (1,)), ((), ())), preferred_element_type=f32
        ).astype(bf16)


def crop_block(table, sizes, features, boxes, maps, weight=None, out_type=bf16, earlier=(), cost=LARGE_COST, sum_type=bf16):
    height, width, part, level_count = sizes
    images = boxes.shape[0]
    product = weight is not None
    first = [boxes, maps] + ([weight] if product else [])
    rows = images * LANES
    if product:
        units = weight.shape[1]
        out_spec = pl.BlockSpec((rows, units), lambda n: (0, 0))
        out_shape = like((rows, units), out_type)
        more = [pltpu.VMEM((rows, features), bf16)]
    else:
        out_spec = pl.BlockSpec((LANES, features), lambda n: (n, 0))
        out_shape = like((rows, features), bf16)
        more = []
    return pl.pallas_call(
        functools.partial(crop_kernel, table, sizes, product),
        grid=(images,),
        in_specs=[
            pl.BlockSpec((None, 8, LANES), lambda n: (n, 0, 0)),
            pl.BlockSpec((None, width * part, level_count * height), lambda n: (n, 0, 0)),
        ]
        + [WHOLE for one in first[2:]]
        + [FAR for one in earlier],
        out_specs=[
            pl.BlockSpec((features, LANES), lambda n: (0, n)),
            out_spec,
            pl.BlockSpec((8, LANES), lambda n: (0, 0)),
        ],
        out_shape=[like((features, rows), bf16), out_shape, SIGN],
        scratch_shapes=[
            pltpu.VMEM((level_count * height, POOL * LANES), bf16),
            pltpu.VMEM((POOL, width, LANES), sum_type),
            pltpu.VMEM((width * part, POOL * LANES), sum_type),
            pltpu.VMEM((features, LANES), f32),
        ]
        + more,
        compiler_params=pltpu.CompilerParams(vmem_limit_bytes=24 * 2**20),
        cost_estimate=cost,
        name="crop_block",
    )(*first, *earlier)


def multiply_kernel(rows_ref, weight_ref, out_ref, sign_ref):
    out_ref[...] = jnp.dot(rows_ref[...], weight_ref[...], preferred_element_type=f32).astype(bf16)
    sign_ref[...] = jnp.zeros_like(sign_ref)


def multiply(rows, weight):
    return pl.pallas_call(
        multiply_kernel,
        in_specs=[WHOLE, WHOLE],
        out_specs=[WHOLE, WHOLE],
        out_shape=[like((rows.shape[0], weight.shape[1]), bf16), SIGN],
        compiler_params=pltpu.CompilerParams(vmem_limit_bytes=24 * 2**20),
        cost_estimate=LARGE_COST,
        name="multiply",
    )(rows, weight)


def spread_block(table, sizes, boxes, grads, weight, earlier=()):
    height, width, part, level_count = sizes
    images = boxes.shape[0]
    features = weight.shape[0]
    return pl.pallas_call(
        functools.partial(spread_kernel, table, sizes),
        in_specs=[WHOLE, WHOLE, WHOLE] + [FAR for one in earlier],
        out_specs=[WHOLE, WHOLE],
        out_shape=[like((images, width * part, level_count * height), bf16), SIGN],
        scratch_shapes=[
            pltpu.VMEM((images, level_count * height, POOL * LANES), bf16),
            pltpu.VMEM((images, POOL, width, LANES), bf16),
            pltpu.VMEM((width * part, POOL * LANES), bf16),
            pltpu.VMEM((features, LANES), f32),
            pltpu.VMEM((features, images * LANES), bf16),
        ],
        compiler_params=pltpu.CompilerParams(vmem_limit_bytes=24 * 2**20),
        cost_estimate=LARGE_COST,
        name="spread_block",
    )(boxes, grads, weight, *earlier)


def call(kernel, outs, where, arrays, earlier=(), scratch=(), name=None, cost=LARGE_COST):
    arrays = list(arrays)

    def body(*refs):
        end = 1 + len(arrays)
        later = refs[end + len(earlier) :]
        later[len(outs)][...] = jnp.zeros(SIGN.shape, SIGN.dtype)
        kernel(refs[0], refs[1:end], (*later[: len(outs)], *later[len(outs) + 1 :]))

    return pl.pallas_call(
        body,
        in_specs=[SCALAR] + [WHOLE for one in arrays] + [FAR for one in earlier],
        out_specs=[WHOLE for one in (*outs, SIGN)],
        out_shape=[*outs, SIGN],
        scratch_shapes=scratch,
        compiler_params=pltpu.CompilerParams(vmem_limit_bytes=24 * 2**20),
        cost_estimate=cost,
        name=name,
    )(where, *arrays, *earlier)


def tie_kernel(*refs):
    pass


def tie(arrays, *earlier):
    return pl.pallas_call(
        tie_kernel,
        in_specs=[FAR for one in (*arrays, *earlier)],
        out_specs=[FAR for one in arrays],
        out_shape=[like(one.shape, one.dtype) for one in arrays],
        input_output_aliases={k: k for k in range(len(arrays))},
        compiler_params=pltpu.CompilerParams(vmem_limit_bytes=2**20),
        cost_estimate=TINY_COST,
        name="tie",
    )(*arrays, *earlier)


def add_kernel(where, arrays, outs):
    outs[0][...] = sum(ref[...].astype(f32) for ref in arrays).astype(outs[0].dtype)


def pair_kernel(bit, where, arrays, outs):
    own = (where[bit[0]] >> bit[1]) & 1
    outs[0][own] = arrays[0][...]
    outs[0][1 - own] = arrays[1][...]


def pair_up(bit, where, own, earlier):
    come = swap(own, AXES[bit[0]], 1 << bit[1])
    out = like((2,) + own.shape, own.dtype)
    return call(functools.partial(pair_kernel, bit), [out], where, [own, come], earlier, name="pair_up")


def order_kernel(where, arrays, outs):
    for k, ref in enumerate(arrays):
        outs[0][(where[1] >> 1) ^ k] = ref[...]


def full_small_kernel(rows, where, arrays, outs):
    units = outs[0].shape[1]
    for k, ref in enumerate(arrays):
        core = (where[1] & 1) ^ k
        for chip in range(4):
            for level in range(ref.shape[1]):
                at = pl.multiple_of(((level * 4 + chip) * 2 + core) * rows, rows)
                outs[0][pl.ds(at, rows), :] = ref[chip, level, :rows, :]
                for part in range(2):
                    outs[1][pl.ds(at + part * (rows // 2), rows // 2), :] = ref[
                        chip, level, rows:, part * (units // 2) : (part + 1) * (units // 2)
                    ]


def split_rows(own, inner, array, rows, sent, kept):
    step = inner * rows
    for at in range((kept.shape[0] - 16) // step):
        mine = pl.multiple_of((2 * at + own) * step, rows)
        other = pl.multiple_of((2 * at + 1 - own) * step, rows)
        kept[at * step : (at + 1) * step, :] = array[pl.ds(mine, step), :].astype(bf16)
        sent[at * step : (at + 1) * step, :] = array[pl.ds(other, step), :].astype(bf16)


def put_biases(biases, refs):
    high = biases.astype(bf16).astype(f32)
    both = jnp.concatenate([high, biases - high], axis=0).astype(bf16)
    for ref in refs:
        ref[ref.shape[0] - 16 :, : both.shape[1]] = both


def get_biases(ref, units):
    end = ref.shape[0]
    last = ref[end - 16 :, :units].astype(f32)
    return last[:8] + last[8:]


def small_product_kernel(rows, where_ref, first_ref, second_grad_ref, second_ref, slopes_ref, first_grad_ref, sent_ref, kept_ref, sign_ref, total_ref, bias_ref):
    turned = (((0,), (0,)), ((), ()))
    units = first_ref.shape[1]
    total_ref[:, :units] = lax.dot_general(
        first_ref[...], second_grad_ref[...], turned, preferred_element_type=f32
    )
    total_ref[:, units:] = lax.dot_general(
        second_ref[...], slopes_ref[...], turned, preferred_element_type=f32
    )
    split_rows(where_ref[1] & 1, 1, total_ref, rows, sent_ref, kept_ref)
    sum_rows([first_grad_ref, second_grad_ref, slopes_ref], bias_ref)
    put_biases(bias_ref[...], [sent_ref, kept_ref])
    sign_ref[...] = jnp.zeros_like(sign_ref)


def small_product(where, rows, first_act, second_grad, second_act, slopes, first_grad):
    units = first_act.shape[1]
    wide = units + slopes.shape[1]
    half = like((units // 2 + 16, wide), bf16)
    return pl.pallas_call(
        functools.partial(small_product_kernel, rows),
        in_specs=[SCALAR] + [WHOLE] * 5,
        out_specs=[WHOLE] * 3,
        out_shape=[half, half, SIGN],
        scratch_shapes=[pltpu.VMEM((units, wide), f32), pltpu.VMEM((8, units), f32)],
        compiler_params=pltpu.CompilerParams(vmem_limit_bytes=24 * 2**20),
        cost_estimate=LARGE_COST,
        name="small_product",
    )(where, first_act, second_grad, second_act, slopes, first_grad)


def quarter_kernel(rows, where_ref, kept_ref, come_ref, *refs):
    outs, sign_ref, total_ref = refs[-6:-2], refs[-2], refs[-1]
    sign_ref[...] = jnp.zeros_like(sign_ref)
    count, units = total_ref.shape[0], total_ref.shape[1] // 3 * 2
    total_ref[...] = kept_ref[:count, :].astype(f32) + come_ref[:count, :].astype(f32)
    for k, out in enumerate(outs):
        for at in range(count // rows // 4):
            first = pl.multiple_of((4 * at + ((where_ref[1] >> 1) ^ k)) * rows, rows)
            out[at * rows : (at + 1) * rows, :] = total_ref[pl.ds(first, rows), :].astype(bf16)
    put_biases(get_biases(kept_ref, units) + get_biases(come_ref, units), outs)


def quarter_rows(rows, where, kept, come, earlier):
    count = kept.shape[0] - 16
    quarter = like((count // 4 + 16, kept.shape[1]), bf16)
    return pl.pallas_call(
        functools.partial(quarter_kernel, rows),
        in_specs=[SCALAR, WHOLE, WHOLE] + [FAR for one in earlier],
        out_specs=[WHOLE] * 5,
        out_shape=[quarter] * 4 + [SIGN],
        scratch_shapes=[pltpu.VMEM((count, kept.shape[1]), f32)],
        compiler_params=pltpu.CompilerParams(vmem_limit_bytes=24 * 2**20),
        cost_estimate=LARGE_COST,
        name="quarter_rows",
    )(where, kept, come, *earlier)


def halve_kernel(bit, inner, rows, where, arrays, outs):
    sent_out, kept_out, total_ref = outs
    count, units = total_ref.shape[0], total_ref.shape[1] // 3 * 2
    total_ref[...] = sum(ref[:count, :].astype(f32) for ref in arrays)
    split_rows((where[bit[0]] >> bit[1]) & 1, inner, total_ref, rows, sent_out, kept_out)
    biases = [get_biases(ref, units) for ref in arrays]
    while len(biases) > 1:
        biases = [biases[k] + biases[k + 1] for k in range(0, len(biases), 2)]
    put_biases(biases[0], [sent_out, kept_out])


def halve_rows(bit, inner, rows, where, arrays, earlier):
    count, wide = arrays[0].shape[0] - 16, arrays[0].shape[1]
    return call(
        functools.partial(halve_kernel, bit, inner, rows),
        [like((count // 2 + 16, wide), bf16)] * 2,
        where,
        arrays,
        earlier,
        [pltpu.VMEM((count, wide), f32)],
        name="halve_rows",
        cost=SMALL_COST,
    )


def small_sum_kernel(where, arrays, outs):
    rows, units = outs[0].shape
    total = sum(ref[:rows, :].astype(f32) for ref in arrays)
    outs[0][...] = total[:, :units]
    outs[1][...] = total[:, units : units + CLS]
    outs[2][...] = total[:, units + LANES : units + LANES + BOX]
    outs[3][...] = sum(get_biases(ref, units) for ref in arrays)


def gelu_and_slope(values):
    normal = 0.5 * (1.0 + lax.erf(values * np.float32(np.sqrt(0.5))))
    density = jnp.exp(-0.5 * values * values) * np.float32(1.0 / np.sqrt(2.0 * np.pi))
    return values * normal, normal + values * density


def head_kernel(
    own_ref, one_ref, two_ref, labels_ref, ignore_ref, targets_ref, hidden_bias_ref, inner_ref, inner_bias_ref, heads_ref, heads_bias_ref,
    heads_out_ref, first_act_ref, second_act_ref, slopes_ref, second_grad_ref, first_grad_ref, first_slope_ref, second_slope_ref,
):
    first_pre = own_ref[...] + hidden_bias_ref[...]
    for come_ref in (one_ref, two_ref):
        first_pre = first_pre + come_ref[...].astype(f32)
    act, slope = gelu_and_slope(first_pre)
    first_slope_ref[...] = slope
    act = act.astype(bf16)
    first_act_ref[...] = act
    second_pre = jnp.dot(act, inner_ref[...], preferred_element_type=f32) + inner_bias_ref[...]
    act, slope = gelu_and_slope(second_pre)
    second_slope_ref[...] = slope
    act = act.astype(bf16)
    second_act_ref[...] = act
    heads = jnp.dot(act, heads_ref[...], preferred_element_type=f32) + heads_bias_ref[...]
    heads_out_ref[...] = heads
    logits, deltas = heads[:, :LANES], heads[:, LANES:]
    facts = []
    for n in range(labels_ref.shape[0]):
        fact = [labels_ref[n : n + 1, :].astype(f32), ignore_ref[n : n + 1, :].astype(f32)]
        fact += [targets_ref[n], jnp.zeros((2, LANES), f32)]
        facts.append(jnp.concatenate(fact, axis=0).T)
    facts = jnp.concatenate(facts, axis=0)
    label = facts[:, 0:1]
    kept = 1.0 - facts[:, 1:2]
    column = lax.broadcasted_iota(jnp.int32, logits.shape, 1)
    valid = column < CLS
    row_max = jnp.max(jnp.where(valid, logits, -jnp.inf), axis=1, keepdims=True)
    exponent = jnp.where(valid, jnp.exp(jnp.where(valid, logits - row_max, 0.0)), 0.0)
    softmax_rows = exponent / jnp.sum(exponent, axis=1, keepdims=True)
    hot = (column.astype(f32) == label).astype(f32)
    logit_slope = (softmax_rows - hot) * (kept * np.float32(1.0 / RPI))
    column = lax.broadcasted_iota(jnp.int32, deltas.shape, 1)
    target = facts[:, 2:3]
    for j in range(1, 4):
        target = jnp.where((column & 3) == j, facts[:, 2 + j : 3 + j], target)
    foreground = jnp.where(label < CLS - 1, kept, 0.0)
    hot = ((column >> 2).astype(f32) == label) & (column < BOX)
    delta_slope = jnp.where(
        hot,
        jnp.clip(deltas - target, -1.0, 1.0) * (foreground * np.float32(1.0 / RPI)),
        0.0,
    )
    slopes = jnp.concatenate([logit_slope, delta_slope], axis=1).astype(bf16)
    slopes_ref[...] = slopes
    turned = (((1,), (1,)), ((), ()))
    act_grad = lax.dot_general(slopes, heads_ref[...], turned, preferred_element_type=f32)
    second_grad = (act_grad * second_slope_ref[...]).astype(bf16)
    second_grad_ref[...] = second_grad
    act_grad = lax.dot_general(second_grad, inner_ref[...], turned, preferred_element_type=f32)
    first_grad = (act_grad * first_slope_ref[...]).astype(bf16)
    first_grad_ref[...] = first_grad


def sum_rows(refs, out_ref):
    out_ref[...] = jnp.zeros_like(out_ref)
    for k, ref in enumerate(refs):
        out_ref[k : k + 1, : ref.shape[1]] = jnp.sum(ref[...].astype(f32), axis=0, keepdims=True)


def row_outputs_kernel(where, arrays, outs):
    heads_ref, first_grad_ref, second_grad_ref, slopes_ref = arrays
    logits_ref, deltas_ref, bias_ref = outs
    for n in range(deltas_ref.shape[0]):
        rows = slice(n * LANES, (n + 1) * LANES)
        logits_ref[:, n, :] = heads_ref[rows, :LANES].T[:CLS]
        deltas_ref[n] = heads_ref[rows, LANES:].T[:BOX]
    sum_rows([first_grad_ref, second_grad_ref, slopes_ref], bias_ref)


def head_block(own, come, labels, ignore, targets, hidden_bias, inner, inner_bias, heads, heads_bias):
    count, units = own.shape
    wide = heads.shape[1]
    return pl.pallas_call(
        head_kernel,
        in_specs=[pl.BlockSpec(memory_space=pltpu.VMEM)] * 11,
        out_specs=[pl.BlockSpec(memory_space=pltpu.VMEM)] * 6,
        out_shape=[
            like((count, wide), f32),
            like((count, units), bf16),
            like((count, units), bf16),
            like((count, wide), bf16),
            like((count, units), bf16),
            like((count, units), bf16),
        ],
        scratch_shapes=[pltpu.VMEM((count, units), f32)] * 2,
        compiler_params=pltpu.CompilerParams(vmem_limit_bytes=24 * 2**20),
        cost_estimate=LARGE_COST,
        name="head_block",
    )(own, *come, labels, ignore, targets, hidden_bias, inner, inner_bias, heads, heads_bias)


def maps_kernel(where, arrays, outs):
    maps_ref, by_class_ref, across_first_ref = arrays
    pick_ref = outs[-1]
    size, part = by_class_ref.shape[:2]
    images = maps_ref.shape[0]
    for way in range(size):
        pick_ref[way * part : (way + 1) * part, :] = by_class_ref[where[0] ^ way]
    for n in range(images):
        flat = lax.dot_general(
            pick_ref[...], maps_ref[n], (((1,), (1,)), ((), ())), preferred_element_type=f32
        ).astype(bf16)
        flat = jnp.dot(flat, across_first_ref[...], preferred_element_type=f32).astype(bf16)
        for way in range(size):
            outs[way][n * part : (n + 1) * part, :] = flat[way * part : (way + 1) * part]


def maps_back_kernel(where, arrays, outs):
    came_refs, (by_class_ref, across_first_ref) = arrays[:-2], arrays[-2:]
    out_ref, pick_ref, flat_ref = outs
    size, part = by_class_ref.shape[:2]
    for way in range(size):
        pick_ref[way * part : (way + 1) * part, :] = by_class_ref[where[0] ^ way]
    for n in range(out_ref.shape[0]):
        for way in range(size):
            flat_ref[way * part : (way + 1) * part, :] = came_refs[way][n]
        cells = lax.dot_general(
            across_first_ref[...], flat_ref[...], (((1,), (1,)), ((), ())), preferred_element_type=f32
        ).astype(bf16)
        out_ref[n] = jnp.dot(cells, pick_ref[...], preferred_element_type=f32)


def arrange_kernel(sizes, where, arrays, outs):
    height, width, part, level_count = sizes
    for n in range(outs[0].shape[0]):
        for x in range(width):
            for k, ref in enumerate(arrays):
                outs[0][n, x * part : (x + 1) * part, k * height : (k + 1) * height] = ref[
                    n * part : (n + 1) * part, x * height : (x + 1) * height
                ]


def arrange_back_kernel(sizes, where, arrays, outs):
    height, width, part, level_count = sizes
    for n in range(arrays[0].shape[0]):
        for x in range(width):
            for k, out in enumerate(outs):
                out[n, :, x * height : (x + 1) * height] = sum(
                    ref[n, x * part : (x + 1) * part, k * height : (k + 1) * height].astype(f32)
                    for ref in arrays
                ).astype(bf16)


def split_span_kernel(length, where, arrays, outs):
    weight_ref, extra_ref = arrays
    total_ref = outs[-1]
    span, size = outs[0].shape[0], len(outs) - 1
    shape = (total_ref.shape[0], weight_ref.shape[0])
    row = lax.broadcasted_iota(jnp.int32, shape, 0)
    column = lax.broadcasted_iota(jnp.int32, shape, 1)
    kind = sum((row >= k * span).astype(jnp.int32) for k in range(1, size))
    matrix = jnp.where(column == (row - kind * span) * size + kind, 1.0, 0.0).astype(bf16)
    total_ref[...] = jnp.dot(matrix, weight_ref[...], preferred_element_type=f32)
    for k in range(size):
        at = k * span + length
        total_ref[at : at + extra_ref.shape[0], :] = extra_ref[...]
    for way, out in enumerate(outs[:-1]):
        at = pl.multiple_of((where[0] ^ way) * span, 8)
        out[...] = total_ref[pl.ds(at, span), :].astype(bf16)


def join_span_kernel(where, arrays, outs):
    total_ref = outs[-1]
    span = arrays[1].shape[0]
    for way, ref in enumerate(arrays[1:]):
        at = pl.multiple_of((where[0] ^ way) * span, 8)
        total_ref[pl.ds(at, span), :] = ref[...].astype(f32)
    product = jnp.dot(arrays[0][...], total_ref[...].astype(bf16), preferred_element_type=f32)
    for out in outs[:-1]:
        out[...] = product.astype(out.dtype)


def return_span_kernel(where, arrays, outs):
    total_ref = outs[-1]
    span = outs[0].shape[0]
    piece = sum(ref[...].astype(f32) for ref in arrays[1:]).astype(bf16)
    total_ref[...] = jnp.dot(arrays[0][...], piece, preferred_element_type=f32)
    for way, out in enumerate(outs[:-1]):
        at = pl.multiple_of((where[0] ^ way) * span, 8)
        out[...] = total_ref[pl.ds(at, span), :].astype(bf16)


def picking(rows, columns, pairs):
    matrix = np.zeros((rows, columns), np.float32)
    for a, b in pairs:
        matrix[a, b] = 1.0
    return jnp.asarray(matrix, bf16)


def swap(array, axis, bit):
    size = lax.axis_size(axis)
    return lax.ppermute(array, axis, [(at, at ^ bit) for at in range(size)])


def exchange(array, axis):
    return lax.all_to_all(array, axis, split_axis=0, concat_axis=0, tiled=True)


def exchange_ways(arrays, axis):
    return [arrays[0]] + [swap(one, axis, way) for way, one in enumerate(arrays) if way]


def product_kernel(bits, parts, with_sum, where_ref, *refs):
    number = len(bits)
    grad_refs, crop_refs, refs = refs[:parts], refs[parts : 2 * parts], refs[2 * parts :]
    sign_ref, refs = refs[-1], refs[:-1]
    sign_ref[...] = jnp.zeros_like(sign_ref)
    outs = refs[-number:] if with_sum else [refs[-1].at[n] for n in range(number)]
    rows = crop_refs[0].shape[0] // 8
    for n in range(number):
        total = refs[0][n].astype(f32) if with_sum else 0.0
        at = pl.multiple_of((where_ref[1] ^ bits[n]) * rows, 16)
        for grad_ref, crop_ref in zip(grad_refs, crop_refs):
            total = total + jnp.dot(
                crop_ref[pl.ds(at, rows), :], grad_ref[...], preferred_element_type=f32
            )
        outs[n][...] = total.astype(bf16)


def piece_product(crops, grads, where, bits, come, earlier):
    features = crops[0].shape[0]
    units = grads[0].shape[1]
    rows = features // 8
    number = len(bits)
    with_sum = come is not None
    come = [come] if with_sum else []
    outs = (
        [like((rows, units), bf16)] * number if with_sum else [like((number, rows, units), bf16)]
    )
    return pl.pallas_call(
        functools.partial(product_kernel, bits, len(grads), with_sum),
        in_specs=[SCALAR]
        + [WHOLE for one in (*grads, *crops, *come)]
        + [FAR for one in earlier],
        out_specs=[WHOLE for one in (*outs, SIGN)],
        out_shape=[*outs, SIGN],
        compiler_params=pltpu.CompilerParams(vmem_limit_bytes=24 * 2**20),
        cost_estimate=LARGE_COST,
        name="piece_product",
    )(where, *grads, *crops, *come, *earlier)


def butterfly(array):
    for axis in ("img", "level"):
        bit = 1
        while bit < lax.axis_size(axis):
            array = array + swap(array, axis, bit)
            bit *= 2
    return array


def contract_rows(left_side, right_side):
    return lax.dot_general(
        left_side, right_side, (((0,), (0,)), ((), ())), preferred_element_type=f32
    )


def pack_rows(array):
    rows, units = array.shape[-2], array.shape[-1] // 3 * 2
    beside = array[..., units:]
    below = jnp.concatenate([beside[..., : rows // 2, :], beside[..., rows // 2 :, :]], axis=-1)
    return jnp.concatenate([array[..., :units], below], axis=-2)


def per_device(
    pyramid,
    levels,
    region_boxes,
    labels,
    crowd_ignore,
    targets,
    hidden_weight,
    hidden_bias,
    inner_weight,
    inner_bias,
    class_weight,
    class_bias,
    delta_weight,
    delta_bias,
):
    size = lax.axis_size("level")
    planes = lax.axis_size("img")
    z = lax.axis_index("level")
    where = jnp.stack([z, lax.axis_index("img")]).astype(jnp.int32)
    images, height, width, channels = pyramid.shape[1:]
    regions = levels.shape[1]
    part = channels // size
    sizes = (height, width, part, size)
    rows, units = hidden_weight.shape
    block_rows = images * regions
    direct = planes == 8 and rows % size == 0

    packed = jnp.concatenate(
        [
            jnp.transpose(region_boxes, (0, 2, 1)),
            jnp.transpose(levels, (0, 2, 1)),
            jnp.zeros((images, 3, regions), jnp.int32),
        ],
        axis=1,
    )
    class_room, delta_room = LANES, units // 2 - LANES
    small = jnp.concatenate(
        [
            inner_weight,
            jnp.pad(class_weight, ((0, 0), (0, class_room - CLS))),
            jnp.pad(delta_weight, ((0, 0), (0, delta_room - BOX))),
        ],
        axis=1,
    )
    heads_bias = jnp.concatenate(
        [
            jnp.pad(class_bias, (0, class_room - CLS)),
            jnp.pad(delta_bias, (0, delta_room - BOX)),
        ]
    )[None]

    if direct:
        length = rows // size
        span = -(-(length + images) // 8) * 8
        to_span = picking(
            size * span,
            rows,
            [(k * span + j, j * size + k) for k in range(size) for j in range(length)],
        )
        room = -(-rows // 16) * 16
        features = planes * room
        from_span = picking(
            room,
            size * span,
            [(k * length + j, k * span + j) for k in range(size) for j in range(length)],
        )
        total = [pltpu.VMEM((size * span, units), f32)]
        *sent, sign = call(
            functools.partial(split_span_kernel, length),
            [like((span, units), bf16)] * size,
            where,
            [hidden_weight, packed.astype(f32).reshape(images, units)],
            scratch=total,
            name="split_span",
        )
        came = exchange_ways(sent, "level")
        piece, own_piece, sign = call(
            join_span_kernel,
            [like((room, units), bf16)] * 2,
            where,
            [from_span, *came],
            scratch=total,
            name="join_span",
        )
        boxes = jnp.stack([one[length : length + images].reshape(images, 8, regions) for one in came])
        pieces = [own_piece] + [swap(piece, "img", bit) for bit in (2, 4, 6)]
        order = [k * planes + at for at in range(planes) for k in range(size)]
        table = runs_of(order, length, part, size, room)
    else:
        boxes = exchange(jnp.broadcast_to(packed[None], (size,) + packed.shape), "level")
        boxes = jnp.stack([lax.dynamic_index_in_dim(boxes, z ^ way, 0, False) for way in range(size)])
        features = BINS * part
        whole = lax.all_gather(hidden_weight, AXES, axis=0, tiled=True)
        weight = lax.dynamic_index_in_dim(whole.reshape(features, size, units), z, 1, False)
        table = runs_of([0], features, part, 1, features)
    row = jnp.arange(8)[:, None]
    boxes = jnp.where(row == 4, boxes.astype(jnp.int32) ^ z, boxes.astype(jnp.int32)).astype(f32)

    spots = height * width
    by_class = picking(
        channels, channels, [(c % size * part + c // size, c) for c in range(channels)]
    ).reshape(size, part, channels)
    across_first = picking(
        spots, spots, [(y * width + x, x * height + y) for y in range(height) for x in range(width)]
    )
    picks = [
        pltpu.VMEM((channels, channels), bf16),
        pltpu.VMEM((channels, spots), bf16),
    ]
    small_rows = small.shape[0] // 2 * 3
    maps = call(
        maps_kernel,
        [like((images * part, spots), bf16)] * size,
        where,
        [pyramid[0].reshape(images, spots, channels), by_class, across_first],
        scratch=picks[:1],
        name="maps",
    )[:size]
    if direct:
        maps = [maps[0], *tie(maps[1:], sign)]
    maps_came = exchange_ways(maps[:3], "level")
    maps_came.append(swap(tie([maps[3]], maps_came[1])[0], "level", 3))
    if direct:
        smalls = tie([pack_rows(small)], maps_came[3])[0]
    maps, sign = call(
        functools.partial(arrange_kernel, sizes),
        [pltpu.VMEM((images, width * part, size * height), bf16)],
        where,
        maps_came,
        name="arrange",
    )

    ways = (3, 2, 1, 0)
    crops = []
    came_sums = {}
    for turn, way in enumerate(ways):
        if turn == 0:
            crop, turned, sign = crop_block(table, sizes, features, boxes[way], maps)
            if direct:
                smalls, unused = pair_up((0, 0), where, smalls, [sign])
                own_piece = tie([own_piece], sign)[0]
                pieces = [own_piece, *pieces[1:]]
                pieces = sum(([one, swap(one, "img", 1)] for one in pieces), [])
                weight = gather_pieces(where, pieces)
            own, sign = multiply(turned, weight)
            relayed = swap(own, "level", 1)
        else:
            crop, own, sign = crop_block(
                table,
                sizes,
                features,
                boxes[way],
                maps,
                weight,
                bf16 if way == 1 else f32,
                [sign],
                SMALL_COST if way == 1 else LARGE_COST,
                bf16 if way else f32,
            )
        crops.append(crop)
        if way == 2:
            middle = own
            if direct:
                smalls, sign = pair_up((0, 1), where, smalls, [sign])
                smalls = smalls.reshape(size, small_rows, units)
                smalls = [swap(smalls, "img", bit) if bit else smalls for bit in (0, 2, 4, 6)]
        if way == 1:
            came_sums[1] = swap(own, "level", 1)
            middle, sign = call(
                add_kernel, [like(middle.shape, bf16)], where, [middle, relayed], [sign], name="add"
            )
            came_sums[2] = swap(middle, "level", 2)
            before = sign
    came_sums = [came_sums[2], came_sums[1]]

    if direct:
        smalls, unused = call(
            order_kernel,
            [like((4, size, small_rows, units), bf16)],
            where,
            smalls,
            [before],
            name="in_order",
        )
        full_inner, full_heads, sign = call(
            functools.partial(full_small_kernel, small.shape[0]),
            [pltpu.VMEM((units, units), bf16), pltpu.VMEM((units, units // 2), bf16)],
            where,
            [smalls, swap(smalls, "img", 1)],
            name="full_small",
        )
    else:
        smalls = lax.all_gather(small, AXES, axis=0, tiled=True)
        full_inner, full_heads = smalls[:, :units], smalls[:, units:]

    head_rows, first_act, second_act, slopes, second_grad, first_grad = head_block(
        own,
        came_sums,
        labels,
        crowd_ignore,
        jnp.transpose(targets, (0, 2, 1)),
        hidden_bias[None],
        full_inner,
        inner_bias[None],
        full_heads,
        heads_bias,
    )

    near = swap(first_grad, "level", 1)
    far = swap(first_grad, "level", 2)
    grad_of = {0: first_grad, 1: near}

    shares = []

    def take_up(way, earlier=()):
        share, sign = spread_block(table, sizes, boxes[way], grad_of[way], weight, earlier)
        shares.append(share)
        return sign

    if direct:
        count = small.shape[0]
        sent, kept, sign = small_product(
            where, count, first_act, second_grad, second_act, slopes, first_grad
        )
        sign = take_up(0, [sign])
        *quarters, sign = quarter_rows(count, where, kept, swap(sent, "img", 1), [sign])
        quarters = [
            swap(one, "img", bit) if bit else one for one, bit in zip(quarters, (0, 2, 4, 6))
        ]
        grad_of[2] = tie([far], sign)[0]
        grad_of[3] = swap(grad_of[2], "level", 1)
        sign = take_up(1, [sign])
        sign = take_up(2, [sign])

        grads = [grad_of[way] for way in ways]
        parts, others = {}, {}

        def for_other(bits, sign):
            theirs = tuple(bit ^ 1 for bit in bits)
            products, sign = piece_product(crops, grads, where, theirs, None, [sign])
            others[bits] = swap(products, "img", 1)
            return sign

        def for_own(bits, sign):
            *own, sign = piece_product(crops, grads, where, bits, others[bits], [sign])
            for one, bit in zip(own, bits):
                parts[bit] = swap(one, "img", bit) if bit else one
            return sign

        sign = for_other((6,), sign)
        sign = for_other((2, 4, 0), sign)
        sign = for_own((6,), sign)
        sent, kept, sign = halve_rows((0, 1), 2, count, where, quarters, [sign])
        sign = for_own((2, 4, 0), sign)
        sign = take_up(3, [sign])
        sent, kept, sign = halve_rows(
            (0, 0), 1, count, where, [kept, swap(sent, "level", 2)], [sign]
        )
        *back, sign = call(
            functools.partial(arrange_back_kernel, sizes),
            [like((images, part, spots), bf16)] * size,
            where,
            shares,
            [sign],
            name="arrange_back",
        )
        inner_sum, class_sum, delta_sum, bias_total, sign = call(
            small_sum_kernel,
            [
                like((count, units), f32),
                like((count, CLS), f32),
                like((count, BOX), f32),
                like((8, units), f32),
            ],
            where,
            [kept, swap(sent, "level", 1)],
            [sign],
            name="small_sum",
            cost=TINY_COST,
        )
        back[3] = tie(back[3:], sign)[0]
        half, sign = call(
            add_kernel, [like(parts[0].shape, f32)], where, [parts[0], parts[6]], [sign], name="add", cost=TINY_COST
        )
        back[1] = tie(back[1:2], sign)[0]
        *out, sign = call(
            return_span_kernel,
            [like((span, units), bf16)] * size,
            where,
            [from_span.T, half, parts[2], parts[4]],
            [sign],
            scratch=total,
            name="return_span",
        )
    else:
        grad_of[2], grad_of[3] = far, swap(far, "level", 1)
        for way in range(size):
            take_up(way)
        *back, sign = call(
            functools.partial(arrange_back_kernel, sizes),
            [like((images, part, spots), bf16)] * size,
            where,
            shares,
            name="arrange_back",
        )
        small_sum = jnp.concatenate(
            [contract_rows(first_act, second_grad), contract_rows(second_act, slopes)], axis=1
        )
        small_sum = lax.psum_scatter(small_sum, AXES, scatter_dimension=0, tiled=True)
        inner_sum = small_sum[:, :units]
        class_sum = small_sum[:, units : units + CLS]
        delta_sum = small_sum[:, units + class_room : units + class_room + BOX]
        whole_grads = jnp.concatenate([grad_of[way] for way in ways])
        product = jnp.dot(
            jnp.concatenate(crops, axis=1), whole_grads, preferred_element_type=f32
        )
        own = (jnp.arange(size, dtype=jnp.int32) == z)[None, :, None]
        hidden_sum = lax.psum_scatter(
            jnp.where(own, product[:, None, :], 0.0).reshape(features * size, units),
            AXES,
            scatter_dimension=0,
            tiled=True,
        )

    map_grads, sign = call(
        maps_back_kernel,
        [like((images, spots, channels), f32)],
        where,
        [*exchange_ways(back, "level"), by_class, across_first],
        [sign],
        scratch=picks,
        name="maps_back",
    )
    map_grads = map_grads.reshape(1, images, height, width, channels)
    logits, deltas, bias_sums, unused = call(
        row_outputs_kernel,
        [
            like((CLS, images, LANES), f32),
            like((images, BOX, LANES), f32),
            like((8, units), f32),
        ],
        where,
        [head_rows, first_grad, second_grad, slopes],
        [sign],
        name="row_outputs",
    )
    if direct:
        hidden_sum = call(
            join_span_kernel,
            [like((rows, units), f32)],
            where,
            [to_span.T, *exchange_ways(out, "level")],
            [sign],
            scratch=total,
            name="join_span",
        )[0]

    if not direct:
        bias_total = butterfly(bias_sums)
    head_bias = bias_total[2, : class_room + delta_room]
    return (
        jnp.transpose(logits, (1, 2, 0)),
        jnp.transpose(deltas, (0, 2, 1)),
        map_grads,
        hidden_sum,
        bias_total[0],
        inner_sum,
        bias_total[1],
        class_sum,
        head_bias[:CLS],
        delta_sum,
        head_bias[class_room : class_room + BOX],
    )


def solution(mesh):
    return jax.shard_map(
        per_device,
        mesh=mesh,
        in_specs=(
            P("level", "img", None, None, None),
            P("img", "level", None),
            P("img", "level", None),
            P("img", "level"),
            P("img", "level"),
            P("img", "level", None),
            P(AXES, None),
            P(),
            P(AXES, None),
            P(),
            P(AXES, None),
            P(),
            P(AXES, None),
            P(),
        ),
        out_specs=(
            P("img", "level", None),
            P("img", "level", None),
            P("level", "img", None, None, None),
            P(AXES, None),
            P(),
            P(AXES, None),
            P(),
            P(AXES, None),
            P(),
            P(AXES, None),
            P(),
        ),
        check_vma=False,
    )
```

```python
import functools

import jax
import jax.numpy as jnp
import numpy as np
from jax import lax
from jax.experimental import pallas as pl
from jax.experimental.pallas import tpu as pltpu
from jax.sharding import PartitionSpec as P

POOL = 7
SAMPLES = 2
CLS = 81
BOX = 320
RPI = 512
BINS = POOL * POOL
LANES = 128
AXES = ("level", "img")
OFFSETS = (np.arange(SAMPLES * POOL, dtype=np.float32) + np.float32(0.5)) / np.float32(
    SAMPLES * POOL
)
SMALL_COST = pl.CostEstimate(flops=10**9, bytes_accessed=1, transcendentals=0)
TINY_COST = pl.CostEstimate(flops=1, bytes_accessed=1, transcendentals=0)
LARGE_COST = pl.CostEstimate(flops=3 * 10**10, bytes_accessed=1, transcendentals=0)
f32 = jnp.float32
bf16 = jnp.bfloat16
FAR = pl.BlockSpec(memory_space=pl.ANY)
WHOLE = pl.BlockSpec(memory_space=pltpu.VMEM)
SCALAR = pl.BlockSpec(memory_space=pltpu.SMEM)
like = jax.ShapeDtypeStruct
SIGN = jax.ShapeDtypeStruct((8, LANES), jnp.float32)


def bin_weights(low, span, centres, at):
    first = jnp.maximum(1.0 - jnp.abs((low + OFFSETS[2 * at] * span) - centres), 0.0)
    second = jnp.maximum(1.0 - jnp.abs((low + OFFSETS[2 * at + 1] * span) - centres), 0.0)
    return ((first + second) * 0.5).astype(bf16)


def fill_weights(box_ref, down_ref, across_ref, height, width, level_count):
    x0, y0, x1, y1, level = [box_ref[k : k + 1, :] for k in range(5)]
    centres = lax.broadcasted_iota(jnp.int32, (width, LANES), 0).astype(f32)
    for q in range(POOL):
        across_ref[q] = bin_weights(x0, x1 - x0, centres, q).astype(across_ref.dtype)
    centres = lax.broadcasted_iota(jnp.int32, (height, LANES), 0).astype(f32)
    for p in range(POOL):
        weights = bin_weights(y0, y1 - y0, centres, p).astype(f32)
        for k in range(level_count):
            down_ref[k * height : (k + 1) * height, p * LANES : (p + 1) * LANES] = jnp.where(
                level == float(k), weights, 0.0
            ).astype(bf16)


def runs_of(order, length, part, group, room):
    place = {chunk: at // group * room + at % group * length for at, chunk in enumerate(order)}
    table = []
    for at in range(BINS):
        row, end, runs = at * part, (at + 1) * part, []
        while row < end:
            chunk = row // length
            stop = min(end, (chunk + 1) * length)
            runs.append((row - at * part, place[chunk] + row - chunk * length, stop - row))
            row = stop
        table.append(runs)
    return table


def gaps_of(table, features):
    held = sorted((kept, kept + count) for runs in table for row, kept, count in runs)
    gaps, last = [], 0
    for first, end in held + [(features, features)]:
        if first > last:
            gaps.append((last, first))
        last = end
    return gaps


def gather_kernel(number, where_ref, *refs):
    kept_ref, sems = refs[-2:]
    rows = refs[0].shape[0]
    copies = []
    for k, ref in enumerate(refs[:number]):
        at = pl.multiple_of((where_ref[1] ^ k) * rows, 16)
        copies.append(pltpu.make_async_copy(ref, kept_ref.at[pl.ds(at, rows)], sems.at[k]))
    for copy in copies:
        copy.start()
    for copy in copies:
        copy.wait()


def gather_pieces(where, pieces):
    rows, units = pieces[0].shape
    number = len(pieces)
    return pl.pallas_call(
        functools.partial(gather_kernel, number),
        in_specs=[SCALAR] + [FAR for one in pieces],
        out_specs=WHOLE,
        out_shape=pltpu.VMEM((number * rows, units), bf16),
        scratch_shapes=[pltpu.SemaphoreType.DMA((number,))],
        compiler_params=pltpu.CompilerParams(vmem_limit_bytes=24 * 2**20),
        cost_estimate=LARGE_COST,
        name="gather_pieces",
    )(where, *pieces)


def crop_kernel(table, sizes, product, box_ref, maps_ref, *refs):
    if product:
        weight_ref = refs[0]
        crop_ref, out_ref, sign_ref, down_ref, across_ref, sums_ref, rows_ref, turned_ref = refs[-8:]
    else:
        crop_ref, out_ref, sign_ref, down_ref, across_ref, sums_ref, rows_ref = refs[-7:]
    sign_ref[...] = jnp.zeros_like(sign_ref)
    height, width, part, level_count = sizes
    for first, end in gaps_of(table, rows_ref.shape[0]):
        rows_ref[first:end, :] = jnp.zeros((end - first, LANES), f32)
    fill_weights(box_ref, down_ref, across_ref, height, width, level_count)
    sums_ref[...] = jnp.dot(maps_ref[...], down_ref[...], preferred_element_type=f32).astype(
        sums_ref.dtype
    )
    for p in range(POOL):
        lanes = slice(p * LANES, (p + 1) * LANES)
        for start in range(0, POOL, 2):
            bins = range(start, min(POOL, start + 2))
            totals = [None for q in bins]
            for x in range(width):
                piece = sums_ref[x * part : (x + 1) * part, lanes]
                for at, q in enumerate(bins):
                    term = across_ref[q, x : x + 1, :] * piece
                    totals[at] = term if x == 0 else totals[at] + term
            for at, q in enumerate(bins):
                for row, kept, count in table[p * POOL + q]:
                    rows_ref[kept : kept + count, :] = totals[at][row : row + count].astype(f32)
    crop = rows_ref[...].astype(bf16)
    crop_ref[...] = crop
    if not product:
        out_ref[...] = crop.T
        return
    turned_ref[pl.ds(pl.multiple_of(pl.program_id(0) * LANES, LANES), LANES), :] = crop.T

    @pl.when(pl.program_id(0) == pl.num_programs(0) - 1)
    def multiply():
        out_ref[...] = jnp.dot(
            turned_ref[...], weight_ref[...], preferred_element_type=f32
        ).astype(out_ref.dtype)


def spread_kernel(table, sizes, box_ref, grad_ref, weight_ref, *refs):
    total_ref, sign_ref, down_ref, across_ref, sums_ref, rows_ref, crop_ref = refs[-7:]
    sign_ref[...] = jnp.zeros_like(sign_ref)
    height, width, part, level_count = sizes
    images = box_ref.shape[0]
    for n in range(images):
        fill_weights(
            box_ref.at[n], down_ref.at[n], across_ref.at[n], height, width, level_count
        )
    crop_ref[...] = lax.dot_general(
        weight_ref[...], grad_ref[...], (((1,), (1,)), ((), ())), preferred_element_type=f32
    ).astype(bf16)
    for n in range(images):
        rows_ref[...] = crop_ref[:, n * LANES : (n + 1) * LANES].astype(f32)
        for p in range(POOL):
            lanes = slice(p * LANES, (p + 1) * LANES)
            pieces = []
            for q in range(POOL):
                runs = [rows_ref[kept : kept + count, :] for row, kept, count in table[p * POOL + q]]
                runs = runs[0] if len(runs) == 1 else jnp.concatenate(runs, axis=0)
                pieces.append(runs.astype(bf16))
            for x in range(width):
                total = across_ref[n, 0, x : x + 1, :] * pieces[0]
                for q in range(1, POOL):
                    total = total + across_ref[n, q, x : x + 1, :] * pieces[q]
                sums_ref[x * part : (x + 1) * part, lanes] = total
        total_ref[n] = lax.dot_general(
            sums_ref[...], down_ref[n], (((1,), (1,)), ((), ())), preferred_element_type=f32
        ).astype(bf16)


def crop_block(table, sizes, features, boxes, maps, weight=None, out_type=bf16, earlier=(), cost=LARGE_COST, sum_type=bf16):
    height, width, part, level_count = sizes
    images = boxes.shape[0]
    product = weight is not None
    first = [boxes, maps] + ([weight] if product else [])
    rows = images * LANES
    if product:
        units = weight.shape[1]
        out_spec = pl.BlockSpec((rows, units), lambda n: (0, 0))
        out_shape = like((rows, units), out_type)
        more = [pltpu.VMEM((rows, features), bf16)]
    else:
        out_spec = pl.BlockSpec((LANES, features), lambda n: (n, 0))
        out_shape = like((rows, features), bf16)
        more = []
    return pl.pallas_call(
        functools.partial(crop_kernel, table, sizes, product),
        grid=(images,),
        in_specs=[
            pl.BlockSpec((None, 8, LANES), lambda n: (n, 0, 0)),
            pl.BlockSpec((None, width * part, level_count * height), lambda n: (n, 0, 0)),
        ]
        + [WHOLE for one in first[2:]]
        + [FAR for one in earlier],
        out_specs=[
            pl.BlockSpec((features, LANES), lambda n: (0, n)),
            out_spec,
            pl.BlockSpec((8, LANES), lambda n: (0, 0)),
        ],
        out_shape=[like((features, rows), bf16), out_shape, SIGN],
        scratch_shapes=[
            pltpu.VMEM((level_count * height, POOL * LANES), bf16),
            pltpu.VMEM((POOL, width, LANES), sum_type),
            pltpu.VMEM((width * part, POOL * LANES), sum_type),
            pltpu.VMEM((features, LANES), f32),
        ]
        + more,
        compiler_params=pltpu.CompilerParams(vmem_limit_bytes=24 * 2**20),
        cost_estimate=cost,
        name="crop_block",
    )(*first, *earlier)


def multiply_kernel(rows_ref, weight_ref, out_ref, sign_ref):
    out_ref[...] = jnp.dot(rows_ref[...], weight_ref[...], preferred_element_type=f32).astype(bf16)
    sign_ref[...] = jnp.zeros_like(sign_ref)


def multiply(rows, weight):
    return pl.pallas_call(
        multiply_kernel,
        in_specs=[WHOLE, WHOLE],
        out_specs=[WHOLE, WHOLE],
        out_shape=[like((rows.shape[0], weight.shape[1]), bf16), SIGN],
        compiler_params=pltpu.CompilerParams(vmem_limit_bytes=24 * 2**20),
        cost_estimate=LARGE_COST,
        name="multiply",
    )(rows, weight)


def spread_block(table, sizes, boxes, grads, weight, earlier=()):
    height, width, part, level_count = sizes
    images = boxes.shape[0]
    features = weight.shape[0]
    return pl.pallas_call(
        functools.partial(spread_kernel, table, sizes),
        in_specs=[WHOLE, WHOLE, WHOLE] + [FAR for one in earlier],
        out_specs=[WHOLE, WHOLE],
        out_shape=[like((images, width * part, level_count * height), bf16), SIGN],
        scratch_shapes=[
            pltpu.VMEM((images, level_count * height, POOL * LANES), bf16),
            pltpu.VMEM((images, POOL, width, LANES), bf16),
            pltpu.VMEM((width * part, POOL * LANES), bf16),
            pltpu.VMEM((features, LANES), f32),
            pltpu.VMEM((features, images * LANES), bf16),
        ],
        compiler_params=pltpu.CompilerParams(vmem_limit_bytes=24 * 2**20),
        cost_estimate=LARGE_COST,
        name="spread_block",
    )(boxes, grads, weight, *earlier)


def call(kernel, outs, where, arrays, earlier=(), scratch=(), name=None, cost=LARGE_COST):
    arrays = list(arrays)

    def body(*refs):
        end = 1 + len(arrays)
        later = refs[end + len(earlier) :]
        later[len(outs)][...] = jnp.zeros(SIGN.shape, SIGN.dtype)
        kernel(refs[0], refs[1:end], (*later[: len(outs)], *later[len(outs) + 1 :]))

    return pl.pallas_call(
        body,
        in_specs=[SCALAR] + [WHOLE for one in arrays] + [FAR for one in earlier],
        out_specs=[WHOLE for one in (*outs, SIGN)],
        out_shape=[*outs, SIGN],
        scratch_shapes=scratch,
        compiler_params=pltpu.CompilerParams(vmem_limit_bytes=24 * 2**20),
        cost_estimate=cost,
        name=name,
    )(where, *arrays, *earlier)


def tie_kernel(*refs):
    pass


def tie(arrays, *earlier):
    return pl.pallas_call(
        tie_kernel,
        in_specs=[FAR for one in (*arrays, *earlier)],
        out_specs=[FAR for one in arrays],
        out_shape=[like(one.shape, one.dtype) for one in arrays],
        input_output_aliases={k: k for k in range(len(arrays))},
        compiler_params=pltpu.CompilerParams(vmem_limit_bytes=2**20),
        cost_estimate=TINY_COST,
        name="tie",
    )(*arrays, *earlier)


def add_kernel(where, arrays, outs):
    outs[0][...] = sum(ref[...].astype(f32) for ref in arrays).astype(outs[0].dtype)


def pair_kernel(bit, where, arrays, outs):
    own = (where[bit[0]] >> bit[1]) & 1
    outs[0][own] = arrays[0][...]
    outs[0][1 - own] = arrays[1][...]


def pair_up(bit, where, own, earlier):
    come = swap(own, AXES[bit[0]], 1 << bit[1])
    out = like((2,) + own.shape, own.dtype)
    return call(functools.partial(pair_kernel, bit), [out], where, [own, come], earlier, name="pair_up")


def order_kernel(where, arrays, outs):
    for k, ref in enumerate(arrays):
        outs[0][(where[1] >> 1) ^ k] = ref[...]


def full_small_kernel(rows, where, arrays, outs):
    units = outs[0].shape[1]
    for k, ref in enumerate(arrays):
        core = (where[1] & 1) ^ k
        for chip in range(4):
            for level in range(ref.shape[1]):
                at = pl.multiple_of(((level * 4 + chip) * 2 + core) * rows, rows)
                outs[0][pl.ds(at, rows), :] = ref[chip, level, :rows, :]
                for part in range(2):
                    outs[1][pl.ds(at + part * (rows // 2), rows // 2), :] = ref[
                        chip, level, rows:, part * (units // 2) : (part + 1) * (units // 2)
                    ]


def split_rows(own, inner, array, rows, sent, kept):
    step = inner * rows
    for at in range((kept.shape[0] - 16) // step):
        mine = pl.multiple_of((2 * at + own) * step, rows)
        other = pl.multiple_of((2 * at + 1 - own) * step, rows)
        kept[at * step : (at + 1) * step, :] = array[pl.ds(mine, step), :].astype(bf16)
        sent[at * step : (at + 1) * step, :] = array[pl.ds(other, step), :].astype(bf16)


def put_biases(biases, refs):
    high = biases.astype(bf16).astype(f32)
    both = jnp.concatenate([high, biases - high], axis=0).astype(bf16)
    for ref in refs:
        ref[ref.shape[0] - 16 :, : both.shape[1]] = both


def get_biases(ref, units):
    end = ref.shape[0]
    last = ref[end - 16 :, :units].astype(f32)
    return last[:8] + last[8:]


def small_product_kernel(rows, where_ref, first_ref, second_grad_ref, second_ref, slopes_ref, first_grad_ref, sent_ref, kept_ref, sign_ref, total_ref, bias_ref):
    turned = (((0,), (0,)), ((), ()))
    units = first_ref.shape[1]
    total_ref[:, :units] = lax.dot_general(
        first_ref[...], second_grad_ref[...], turned, preferred_element_type=f32
    )
    total_ref[:, units:] = lax.dot_general(
        second_ref[...], slopes_ref[...], turned, preferred_element_type=f32
    )
    split_rows(where_ref[1] & 1, 1, total_ref, rows, sent_ref, kept_ref)
    sum_rows([first_grad_ref, second_grad_ref, slopes_ref], bias_ref)
    put_biases(bias_ref[...], [sent_ref, kept_ref])
    sign_ref[...] = jnp.zeros_like(sign_ref)


def small_product(where, rows, first_act, second_grad, second_act, slopes, first_grad):
    units = first_act.shape[1]
    wide = units + slopes.shape[1]
    half = like((units // 2 + 16, wide), bf16)
    return pl.pallas_call(
        functools.partial(small_product_kernel, rows),
        in_specs=[SCALAR] + [WHOLE] * 5,
        out_specs=[WHOLE] * 3,
        out_shape=[half, half, SIGN],
        scratch_shapes=[pltpu.VMEM((units, wide), f32), pltpu.VMEM((8, units), f32)],
        compiler_params=pltpu.CompilerParams(vmem_limit_bytes=24 * 2**20),
        cost_estimate=LARGE_COST,
        name="small_product",
    )(where, first_act, second_grad, second_act, slopes, first_grad)


def quarter_kernel(rows, where_ref, kept_ref, come_ref, *refs):
    outs, sign_ref, total_ref = refs[-6:-2], refs[-2], refs[-1]
    sign_ref[...] = jnp.zeros_like(sign_ref)
    count, units = total_ref.shape[0], total_ref.shape[1] // 3 * 2
    total_ref[...] = kept_ref[:count, :].astype(f32) + come_ref[:count, :].astype(f32)
    for k, out in enumerate(outs):
        for at in range(count // rows // 4):
            first = pl.multiple_of((4 * at + ((where_ref[1] >> 1) ^ k)) * rows, rows)
            out[at * rows : (at + 1) * rows, :] = total_ref[pl.ds(first, rows), :].astype(bf16)
    put_biases(get_biases(kept_ref, units) + get_biases(come_ref, units), outs)


def quarter_rows(rows, where, kept, come, earlier):
    count = kept.shape[0] - 16
    quarter = like((count // 4 + 16, kept.shape[1]), bf16)
    return pl.pallas_call(
        functools.partial(quarter_kernel, rows),
        in_specs=[SCALAR, WHOLE, WHOLE] + [FAR for one in earlier],
        out_specs=[WHOLE] * 5,
        out_shape=[quarter] * 4 + [SIGN],
        scratch_shapes=[pltpu.VMEM((count, kept.shape[1]), f32)],
        compiler_params=pltpu.CompilerParams(vmem_limit_bytes=24 * 2**20),
        cost_estimate=LARGE_COST,
        name="quarter_rows",
    )(where, kept, come, *earlier)


def halve_kernel(bit, inner, rows, where, arrays, outs):
    sent_out, kept_out, total_ref = outs
    count, units = total_ref.shape[0], total_ref.shape[1] // 3 * 2
    total_ref[...] = sum(ref[:count, :].astype(f32) for ref in arrays)
    split_rows((where[bit[0]] >> bit[1]) & 1, inner, total_ref, rows, sent_out, kept_out)
    biases = [get_biases(ref, units) for ref in arrays]
    while len(biases) > 1:
        biases = [biases[k] + biases[k + 1] for k in range(0, len(biases), 2)]
    put_biases(biases[0], [sent_out, kept_out])


def halve_rows(bit, inner, rows, where, arrays, earlier):
    count, wide = arrays[0].shape[0] - 16, arrays[0].shape[1]
    return call(
        functools.partial(halve_kernel, bit, inner, rows),
        [like((count // 2 + 16, wide), bf16)] * 2,
        where,
        arrays,
        earlier,
        [pltpu.VMEM((count, wide), f32)],
        name="halve_rows",
        cost=SMALL_COST,
    )


def small_sum_kernel(where, arrays, outs):
    rows, units = outs[0].shape
    total = sum(ref[:rows, :].astype(f32) for ref in arrays)
    outs[0][...] = total[:, :units]
    outs[1][...] = total[:, units : units + CLS]
    outs[2][...] = total[:, units + LANES : units + LANES + BOX]
    outs[3][...] = sum(get_biases(ref, units) for ref in arrays)


def gelu_and_slope(values):
    normal = 0.5 * (1.0 + lax.erf(values * np.float32(np.sqrt(0.5))))
    density = jnp.exp(-0.5 * values * values) * np.float32(1.0 / np.sqrt(2.0 * np.pi))
    return values * normal, normal + values * density


def head_kernel(
    own_ref, one_ref, two_ref, labels_ref, ignore_ref, targets_ref, hidden_bias_ref, inner_ref, inner_bias_ref, heads_ref, heads_bias_ref,
    heads_out_ref, first_act_ref, second_act_ref, slopes_ref, second_grad_ref, first_grad_ref, first_slope_ref, second_slope_ref,
):
    first_pre = own_ref[...] + hidden_bias_ref[...]
    for come_ref in (one_ref, two_ref):
        first_pre = first_pre + come_ref[...].astype(f32)
    act, slope = gelu_and_slope(first_pre)
    first_slope_ref[...] = slope
    act = act.astype(bf16)
    first_act_ref[...] = act
    second_pre = jnp.dot(act, inner_ref[...], preferred_element_type=f32) + inner_bias_ref[...]
    act, slope = gelu_and_slope(second_pre)
    second_slope_ref[...] = slope
    act = act.astype(bf16)
    second_act_ref[...] = act
    heads = jnp.dot(act, heads_ref[...], preferred_element_type=f32) + heads_bias_ref[...]
    heads_out_ref[...] = heads
    logits, deltas = heads[:, :LANES], heads[:, LANES:]
    facts = []
    for n in range(labels_ref.shape[0]):
        fact = [labels_ref[n : n + 1, :].astype(f32), ignore_ref[n : n + 1, :].astype(f32)]
        fact += [targets_ref[n], jnp.zeros((2, LANES), f32)]
        facts.append(jnp.concatenate(fact, axis=0).T)
    facts = jnp.concatenate(facts, axis=0)
    label = facts[:, 0:1]
    kept = 1.0 - facts[:, 1:2]
    column = lax.broadcasted_iota(jnp.int32, logits.shape, 1)
    valid = column < CLS
    row_max = jnp.max(jnp.where(valid, logits, -jnp.inf), axis=1, keepdims=True)
    exponent = jnp.where(valid, jnp.exp(jnp.where(valid, logits - row_max, 0.0)), 0.0)
    softmax_rows = exponent / jnp.sum(exponent, axis=1, keepdims=True)
    hot = (column.astype(f32) == label).astype(f32)
    logit_slope = (softmax_rows - hot) * (kept * np.float32(1.0 / RPI))
    column = lax.broadcasted_iota(jnp.int32, deltas.shape, 1)
    target = facts[:, 2:3]
    for j in range(1, 4):
        target = jnp.where((column & 3) == j, facts[:, 2 + j : 3 + j], target)
    foreground = jnp.where(label < CLS - 1, kept, 0.0)
    hot = ((column >> 2).astype(f32) == label) & (column < BOX)
    delta_slope = jnp.where(
        hot,
        jnp.clip(deltas - target, -1.0, 1.0) * (foreground * np.float32(1.0 / RPI)),
        0.0,
    )
    slopes = jnp.concatenate([logit_slope, delta_slope], axis=1).astype(bf16)
    slopes_ref[...] = slopes
    turned = (((1,), (1,)), ((), ()))
    act_grad = lax.dot_general(slopes, heads_ref[...], turned, preferred_element_type=f32)
    second_grad = (act_grad * second_slope_ref[...]).astype(bf16)
    second_grad_ref[...] = second_grad
    act_grad = lax.dot_general(second_grad, inner_ref[...], turned, preferred_element_type=f32)
    first_grad = (act_grad * first_slope_ref[...]).astype(bf16)
    first_grad_ref[...] = first_grad


def sum_rows(refs, out_ref):
    out_ref[...] = jnp.zeros_like(out_ref)
    for k, ref in enumerate(refs):
        out_ref[k : k + 1, : ref.shape[1]] = jnp.sum(ref[...].astype(f32), axis=0, keepdims=True)


def row_outputs_kernel(where, arrays, outs):
    heads_ref, first_grad_ref, second_grad_ref, slopes_ref = arrays
    logits_ref, deltas_ref, bias_ref = outs
    for n in range(deltas_ref.shape[0]):
        rows = slice(n * LANES, (n + 1) * LANES)
        logits_ref[:, n, :] = heads_ref[rows, :LANES].T[:CLS]
        deltas_ref[n] = heads_ref[rows, LANES:].T[:BOX]
    sum_rows([first_grad_ref, second_grad_ref, slopes_ref], bias_ref)


def head_block(own, come, labels, ignore, targets, hidden_bias, inner, inner_bias, heads, heads_bias):
    count, units = own.shape
    wide = heads.shape[1]
    return pl.pallas_call(
        head_kernel,
        in_specs=[pl.BlockSpec(memory_space=pltpu.VMEM)] * 11,
        out_specs=[pl.BlockSpec(memory_space=pltpu.VMEM)] * 6,
        out_shape=[
            like((count, wide), f32),
            like((count, units), bf16),
            like((count, units), bf16),
            like((count, wide), bf16),
            like((count, units), bf16),
            like((count, units), bf16),
        ],
        scratch_shapes=[pltpu.VMEM((count, units), f32)] * 2,
        compiler_params=pltpu.CompilerParams(vmem_limit_bytes=24 * 2**20),
        cost_estimate=LARGE_COST,
        name="head_block",
    )(own, *come, labels, ignore, targets, hidden_bias, inner, inner_bias, heads, heads_bias)


def maps_kernel(where, arrays, outs):
    maps_ref, by_class_ref, across_first_ref = arrays
    pick_ref = outs[-1]
    size, part = by_class_ref.shape[:2]
    images = maps_ref.shape[0]
    for way in range(size):
        pick_ref[way * part : (way + 1) * part, :] = by_class_ref[where[0] ^ way]
    for n in range(images):
        flat = lax.dot_general(
            pick_ref[...], maps_ref[n], (((1,), (1,)), ((), ())), preferred_element_type=f32
        ).astype(bf16)
        flat = jnp.dot(flat, across_first_ref[...], preferred_element_type=f32).astype(bf16)
        for way in range(size):
            outs[way][n * part : (n + 1) * part, :] = flat[way * part : (way + 1) * part]


def maps_back_kernel(where, arrays, outs):
    came_refs, (by_class_ref, across_first_ref) = arrays[:-2], arrays[-2:]
    out_ref, pick_ref, flat_ref = outs
    size, part = by_class_ref.shape[:2]
    for way in range(size):
        pick_ref[way * part : (way + 1) * part, :] = by_class_ref[where[0] ^ way]
    for n in range(out_ref.shape[0]):
        for way in range(size):
            flat_ref[way * part : (way + 1) * part, :] = came_refs[way][n]
        cells = lax.dot_general(
            across_first_ref[...], flat_ref[...], (((1,), (1,)), ((), ())), preferred_element_type=f32
        ).astype(bf16)
        out_ref[n] = jnp.dot(cells, pick_ref[...], preferred_element_type=f32)


def arrange_kernel(sizes, where, arrays, outs):
    height, width, part, level_count = sizes
    for n in range(outs[0].shape[0]):
        for x in range(width):
            for k, ref in enumerate(arrays):
                outs[0][n, x * part : (x + 1) * part, k * height : (k + 1) * height] = ref[
                    n * part : (n + 1) * part, x * height : (x + 1) * height
                ]


def arrange_back_kernel(sizes, where, arrays, outs):
    height, width, part, level_count = sizes
    for n in range(arrays[0].shape[0]):
        for x in range(width):
            for k, out in enumerate(outs):
                out[n, :, x * height : (x + 1) * height] = sum(
                    ref[n, x * part : (x + 1) * part, k * height : (k + 1) * height].astype(f32)
                    for ref in arrays
                ).astype(bf16)


def split_span_kernel(length, where, arrays, outs):
    weight_ref, extra_ref = arrays
    total_ref = outs[-1]
    span, size = outs[0].shape[0], len(outs) - 1
    shape = (total_ref.shape[0], weight_ref.shape[0])
    row = lax.broadcasted_iota(jnp.int32, shape, 0)
    column = lax.broadcasted_iota(jnp.int32, shape, 1)
    kind = sum((row >= k * span).astype(jnp.int32) for k in range(1, size))
    matrix = jnp.where(column == (row - kind * span) * size + kind, 1.0, 0.0).astype(bf16)
    total_ref[...] = jnp.dot(matrix, weight_ref[...], preferred_element_type=f32)
    for k in range(size):
        at = k * span + length
        total_ref[at : at + extra_ref.shape[0], :] = extra_ref[...]
    for way, out in enumerate(outs[:-1]):
        at = pl.multiple_of((where[0] ^ way) * span, 8)
        out[...] = total_ref[pl.ds(at, span), :].astype(bf16)


def join_span_kernel(where, arrays, outs):
    total_ref = outs[-1]
    span = arrays[1].shape[0]
    for way, ref in enumerate(arrays[1:]):
        at = pl.multiple_of((where[0] ^ way) * span, 8)
        total_ref[pl.ds(at, span), :] = ref[...].astype(f32)
    product = jnp.dot(arrays[0][...], total_ref[...].astype(bf16), preferred_element_type=f32)
    for out in outs[:-1]:
        out[...] = product.astype(out.dtype)


def return_span_kernel(where, arrays, outs):
    total_ref = outs[-1]
    span = outs[0].shape[0]
    piece = sum(ref[...].astype(f32) for ref in arrays[1:]).astype(bf16)
    total_ref[...] = jnp.dot(arrays[0][...], piece, preferred_element_type=f32)
    for way, out in enumerate(outs[:-1]):
        at = pl.multiple_of((where[0] ^ way) * span, 8)
        out[...] = total_ref[pl.ds(at, span), :].astype(bf16)


def picking(rows, columns, pairs):
    matrix = np.zeros((rows, columns), np.float32)
    for a, b in pairs:
        matrix[a, b] = 1.0
    return jnp.asarray(matrix, bf16)


def swap(array, axis, bit):
    size = lax.axis_size(axis)
    return lax.ppermute(array, axis, [(at, at ^ bit) for at in range(size)])


def exchange(array, axis):
    return lax.all_to_all(array, axis, split_axis=0, concat_axis=0, tiled=True)


def exchange_ways(arrays, axis):
    return [arrays[0]] + [swap(one, axis, way) for way, one in enumerate(arrays) if way]


def product_kernel(bits, parts, with_sum, where_ref, *refs):
    number = len(bits)
    grad_refs, crop_refs, refs = refs[:parts], refs[parts : 2 * parts], refs[2 * parts :]
    sign_ref, refs = refs[-1], refs[:-1]
    sign_ref[...] = jnp.zeros_like(sign_ref)
    outs = refs[-number:] if with_sum else [refs[-1].at[n] for n in range(number)]
    rows = crop_refs[0].shape[0] // 8
    for n in range(number):
        total = refs[0][n].astype(f32) if with_sum else 0.0
        at = pl.multiple_of((where_ref[1] ^ bits[n]) * rows, 16)
        for grad_ref, crop_ref in zip(grad_refs, crop_refs):
            total = total + jnp.dot(
                crop_ref[pl.ds(at, rows), :], grad_ref[...], preferred_element_type=f32
            )
        outs[n][...] = total.astype(bf16)


def piece_product(crops, grads, where, bits, come, earlier):
    features = crops[0].shape[0]
    units = grads[0].shape[1]
    rows = features // 8
    number = len(bits)
    with_sum = come is not None
    come = [come] if with_sum else []
    outs = (
        [like((rows, units), bf16)] * number if with_sum else [like((number, rows, units), bf16)]
    )
    return pl.pallas_call(
        functools.partial(product_kernel, bits, len(grads), with_sum),
        in_specs=[SCALAR]
        + [WHOLE for one in (*grads, *crops, *come)]
        + [FAR for one in earlier],
        out_specs=[WHOLE for one in (*outs, SIGN)],
        out_shape=[*outs, SIGN],
        compiler_params=pltpu.CompilerParams(vmem_limit_bytes=24 * 2**20),
        cost_estimate=LARGE_COST,
        name="piece_product",
    )(where, *grads, *crops, *come, *earlier)


def butterfly(array):
    for axis in ("img", "level"):
        bit = 1
        while bit < lax.axis_size(axis):
            array = array + swap(array, axis, bit)
            bit *= 2
    return array


def contract_rows(left_side, right_side):
    return lax.dot_general(
        left_side, right_side, (((0,), (0,)), ((), ())), preferred_element_type=f32
    )


def pack_rows(array):
    rows, units = array.shape[-2], array.shape[-1] // 3 * 2
    beside = array[..., units:]
    below = jnp.concatenate([beside[..., : rows // 2, :], beside[..., rows // 2 :, :]], axis=-1)
    return jnp.concatenate([array[..., :units], below], axis=-2)


def per_device(
    pyramid,
    levels,
    region_boxes,
    labels,
    crowd_ignore,
    targets,
    hidden_weight,
    hidden_bias,
    inner_weight,
    inner_bias,
    class_weight,
    class_bias,
    delta_weight,
    delta_bias,
):
    size = lax.axis_size("level")
    planes = lax.axis_size("img")
    z = lax.axis_index("level")
    where = jnp.stack([z, lax.axis_index("img")]).astype(jnp.int32)
    images, height, width, channels = pyramid.shape[1:]
    regions = levels.shape[1]
    part = channels // size
    sizes = (height, width, part, size)
    rows, units = hidden_weight.shape
    block_rows = images * regions
    direct = planes == 8 and rows % size == 0

    packed = jnp.concatenate(
        [
            jnp.transpose(region_boxes, (0, 2, 1)),
            jnp.transpose(levels, (0, 2, 1)),
            jnp.zeros((images, 3, regions), jnp.int32),
        ],
        axis=1,
    )
    class_room, delta_room = LANES, units // 2 - LANES
    small = jnp.concatenate(
        [
            inner_weight,
            jnp.pad(class_weight, ((0, 0), (0, class_room - CLS))),
            jnp.pad(delta_weight, ((0, 0), (0, delta_room - BOX))),
        ],
        axis=1,
    )
    heads_bias = jnp.concatenate(
        [
            jnp.pad(class_bias, (0, class_room - CLS)),
            jnp.pad(delta_bias, (0, delta_room - BOX)),
        ]
    )[None]

    if direct:
        length = rows // size
        span = -(-(length + images) // 8) * 8
        to_span = picking(
            size * span,
            rows,
            [(k * span + j, j * size + k) for k in range(size) for j in range(length)],
        )
        room = -(-rows // 16) * 16
        features = planes * room
        from_span = picking(
            room,
            size * span,
            [(k * length + j, k * span + j) for k in range(size) for j in range(length)],
        )
        total = [pltpu.VMEM((size * span, units), f32)]
        *sent, sign = call(
            functools.partial(split_span_kernel, length),
            [like((span, units), bf16)] * size,
            where,
            [hidden_weight, packed.astype(f32).reshape(images, units)],
            scratch=total,
            name="split_span",
        )
        came = exchange_ways(sent, "level")
        piece, own_piece, sign = call(
            join_span_kernel,
            [like((room, units), bf16)] * 2,
            where,
            [from_span, *came],
            scratch=total,
            name="join_span",
        )
        boxes = jnp.stack([one[length : length + images].reshape(images, 8, regions) for one in came])
        pieces = [own_piece] + [swap(piece, "img", bit) for bit in (2, 4, 6)]
        order = [k * planes + at for at in range(planes) for k in range(size)]
        table = runs_of(order, length, part, size, room)
    else:
        boxes = exchange(jnp.broadcast_to(packed[None], (size,) + packed.shape), "level")
        boxes = jnp.stack([lax.dynamic_index_in_dim(boxes, z ^ way, 0, False) for way in range(size)])
        features = BINS * part
        whole = lax.all_gather(hidden_weight, AXES, axis=0, tiled=True)
        weight = lax.dynamic_index_in_dim(whole.reshape(features, size, units), z, 1, False)
        table = runs_of([0], features, part, 1, features)
    row = jnp.arange(8)[:, None]
    boxes = jnp.where(row == 4, boxes.astype(jnp.int32) ^ z, boxes.astype(jnp.int32)).astype(f32)

    spots = height * width
    by_class = picking(
        channels, channels, [(c % size * part + c // size, c) for c in range(channels)]
    ).reshape(size, part, channels)
    across_first = picking(
        spots, spots, [(y * width + x, x * height + y) for y in range(height) for x in range(width)]
    )
    picks = [
        pltpu.VMEM((channels, channels), bf16),
        pltpu.VMEM((channels, spots), bf16),
    ]
    small_rows = small.shape[0] // 2 * 3
    maps = call(
        maps_kernel,
        [like((images * part, spots), bf16)] * size,
        where,
        [pyramid[0].reshape(images, spots, channels), by_class, across_first],
        scratch=picks[:1],
        name="maps",
    )[:size]
    if direct:
        maps = [maps[0], *tie(maps[1:], sign)]
    maps_came = exchange_ways(maps[:3], "level")
    maps_came.append(swap(tie([maps[3]], maps_came[1])[0], "level", 3))
    if direct:
        smalls = tie([pack_rows(small)], maps_came[3])[0]
    maps, sign = call(
        functools.partial(arrange_kernel, sizes),
        [pltpu.VMEM((images, width * part, size * height), bf16)],
        where,
        maps_came,
        name="arrange",
    )

    ways = (3, 2, 1, 0)
    crops = []
    came_sums = {}
    for turn, way in enumerate(ways):
        if turn == 0:
            crop, turned, sign = crop_block(table, sizes, features, boxes[way], maps)
            if direct:
                smalls, unused = pair_up((0, 0), where, smalls, [sign])
                own_piece = tie([own_piece], sign)[0]
                pieces = [own_piece, *pieces[1:]]
                pieces = sum(([one, swap(one, "img", 1)] for one in pieces), [])
                weight = gather_pieces(where, pieces)
            own, sign = multiply(turned, weight)
            relayed = swap(own, "level", 1)
        else:
            crop, own, sign = crop_block(
                table,
                sizes,
                features,
                boxes[way],
                maps,
                weight,
                bf16 if way == 1 else f32,
                [sign],
                SMALL_COST if way == 1 else LARGE_COST,
                bf16 if way else f32,
            )
        crops.append(crop)
        if way == 2:
            middle = own
            if direct:
                smalls, sign = pair_up((0, 1), where, smalls, [sign])
                smalls = smalls.reshape(size, small_rows, units)
                smalls = [swap(smalls, "img", bit) if bit else smalls for bit in (0, 2, 4, 6)]
        if way == 1:
            came_sums[1] = swap(own, "level", 1)
            middle, sign = call(
                add_kernel, [like(middle.shape, bf16)], where, [middle, relayed], [sign], name="add"
            )
            came_sums[2] = swap(middle, "level", 2)
            before = sign
    came_sums = [came_sums[2], came_sums[1]]

    if direct:
        smalls, unused = call(
            order_kernel,
            [like((4, size, small_rows, units), bf16)],
            where,
            smalls,
            [before],
            name="in_order",
        )
        full_inner, full_heads, sign = call(
            functools.partial(full_small_kernel, small.shape[0]),
            [pltpu.VMEM((units, units), bf16), pltpu.VMEM((units, units // 2), bf16)],
            where,
            [smalls, swap(smalls, "img", 1)],
            name="full_small",
        )
    else:
        smalls = lax.all_gather(small, AXES, axis=0, tiled=True)
        full_inner, full_heads = smalls[:, :units], smalls[:, units:]

    head_rows, first_act, second_act, slopes, second_grad, first_grad = head_block(
        own,
        came_sums,
        labels,
        crowd_ignore,
        jnp.transpose(targets, (0, 2, 1)),
        hidden_bias[None],
        full_inner,
        inner_bias[None],
        full_heads,
        heads_bias,
    )

    near = swap(first_grad, "level", 1)
    far = swap(first_grad, "level", 2)
    grad_of = {0: first_grad, 1: near}

    shares = []

    def take_up(way, earlier=()):
        share, sign = spread_block(table, sizes, boxes[way], grad_of[way], weight, earlier)
        shares.append(share)
        return sign

    if direct:
        count = small.shape[0]
        sent, kept, sign = small_product(
            where, count, first_act, second_grad, second_act, slopes, first_grad
        )
        sign = take_up(0, [sign])
        *quarters, sign = quarter_rows(count, where, kept, swap(sent, "img", 1), [sign])
        quarters = [
            swap(one, "img", bit) if bit else one for one, bit in zip(quarters, (0, 2, 4, 6))
        ]
        grad_of[2] = tie([far], sign)[0]
        grad_of[3] = swap(grad_of[2], "level", 1)
        sign = take_up(1, [sign])
        sign = take_up(2, [sign])

        grads = [grad_of[way] for way in ways]
        parts, others = {}, {}

        def for_other(bits, sign):
            theirs = tuple(bit ^ 1 for bit in bits)
            products, sign = piece_product(crops, grads, where, theirs, None, [sign])
            others[bits] = swap(products, "img", 1)
            return sign

        def for_own(bits, sign):
            *own, sign = piece_product(crops, grads, where, bits, others[bits], [sign])
            for one, bit in zip(own, bits):
                parts[bit] = swap(one, "img", bit) if bit else one
            return sign

        sign = for_other((6,), sign)
        sign = for_other((2, 4, 0), sign)
        sign = for_own((6,), sign)
        sent, kept, sign = halve_rows((0, 0), 1, count, where, quarters, [sign])
        sign = for_own((2, 4, 0), sign)
        sign = take_up(3, [sign])
        sent, kept, sign = halve_rows(
            (0, 1), 1, count, where, [kept, swap(sent, "level", 1)], [sign]
        )
        *back, sign = call(
            functools.partial(arrange_back_kernel, sizes),
            [like((images, part, spots), bf16)] * size,
            where,
            shares,
            [sign],
            name="arrange_back",
        )
        inner_sum, class_sum, delta_sum, bias_total, sign = call(
            small_sum_kernel,
            [
                like((count, units), f32),
                like((count, CLS), f32),
                like((count, BOX), f32),
                like((8, units), f32),
            ],
            where,
            [kept, swap(sent, "level", 2)],
            [sign],
            name="small_sum",
            cost=TINY_COST,
        )
        back[3] = tie(back[3:], sign)[0]
        half, sign = call(
            add_kernel, [like(parts[0].shape, f32)], where, [parts[0], parts[6]], [sign], name="add", cost=TINY_COST
        )
        back[1] = tie(back[1:2], sign)[0]
        *out, sign = call(
            return_span_kernel,
            [like((span, units), bf16)] * size,
            where,
            [from_span.T, half, parts[2], parts[4]],
            [sign],
            scratch=total,
            name="return_span",
        )
    else:
        grad_of[2], grad_of[3] = far, swap(far, "level", 1)
        for way in range(size):
            take_up(way)
        *back, sign = call(
            functools.partial(arrange_back_kernel, sizes),
            [like((images, part, spots), bf16)] * size,
            where,
            shares,
            name="arrange_back",
        )
        small_sum = jnp.concatenate(
            [contract_rows(first_act, second_grad), contract_rows(second_act, slopes)], axis=1
        )
        small_sum = lax.psum_scatter(small_sum, AXES, scatter_dimension=0, tiled=True)
        inner_sum = small_sum[:, :units]
        class_sum = small_sum[:, units : units + CLS]
        delta_sum = small_sum[:, units + class_room : units + class_room + BOX]
        whole_grads = jnp.concatenate([grad_of[way] for way in ways])
        product = jnp.dot(
            jnp.concatenate(crops, axis=1), whole_grads, preferred_element_type=f32
        )
        own = (jnp.arange(size, dtype=jnp.int32) == z)[None, :, None]
        hidden_sum = lax.psum_scatter(
            jnp.where(own, product[:, None, :], 0.0).reshape(features * size, units),
            AXES,
            scatter_dimension=0,
            tiled=True,
        )

    map_grads, sign = call(
        maps_back_kernel,
        [like((images, spots, channels), f32)],
        where,
        [*exchange_ways(back, "level"), by_class, across_first],
        [sign],
        scratch=picks,
        name="maps_back",
    )
    map_grads = map_grads.reshape(1, images, height, width, channels)
    logits, deltas, bias_sums, unused = call(
        row_outputs_kernel,
        [
            like((CLS, images, LANES), f32),
            like((images, BOX, LANES), f32),
            like((8, units), f32),
        ],
        where,
        [head_rows, first_grad, second_grad, slopes],
        [sign],
        name="row_outputs",
    )
    if direct:
        hidden_sum = call(
            join_span_kernel,
            [like((rows, units), f32)],
            where,
            [to_span.T, *exchange_ways(out, "level")],
            [sign],
            scratch=total,
            name="join_span",
        )[0]

    if not direct:
        bias_total = butterfly(bias_sums)
    head_bias = bias_total[2, : class_room + delta_room]
    return (
        jnp.transpose(logits, (1, 2, 0)),
        jnp.transpose(deltas, (0, 2, 1)),
        map_grads,
        hidden_sum,
        bias_total[0],
        inner_sum,
        bias_total[1],
        class_sum,
        head_bias[:CLS],
        delta_sum,
        head_bias[class_room : class_room + BOX],
    )


def solution(mesh):
    return jax.shard_map(
        per_device,
        mesh=mesh,
        in_specs=(
            P("level", "img", None, None, None),
            P("img", "level", None),
            P("img", "level", None),
            P("img", "level"),
            P("img", "level"),
            P("img", "level", None),
            P(AXES, None),
            P(),
            P(AXES, None),
            P(),
            P(AXES, None),
            P(),
            P(AXES, None),
            P(),
        ),
        out_specs=(
            P("img", "level", None),
            P("img", "level", None),
            P("level", "img", None, None, None),
            P(AXES, None),
            P(),
            P(AXES, None),
            P(),
            P(AXES, None),
            P(),
            P(AXES, None),
            P(),
        ),
        check_vma=False,
    )
```
